32 devices in a mesh: dp: 16 (over z, y, core), tensor: 2 (over x).
Axes of the slice: x: 2, y: 2, z: 4, core: 2. Of those that a mesh axis runs over, the one named last changes fastest.
Arguments:
- frames: bfloat16 [65536, 512], P('dp'), may hold values from -6 to 6
- context_keys: bfloat16 [128, 10, 512], P('dp', None, 'tensor'), may hold values from -6 to 6
- context_values: bfloat16 [128, 10, 512], P('dp', None, 'tensor'), may hold values from -6 to 6
- time_start: int32 [128], P('dp'), may hold values from 0 to 511
- time_width: int32 [128], P('dp'), may hold values from 0 to 40
- freq_start: int32 [128], P('dp'), may hold values from 0 to 511
- freq_width: int32 [128], P('dp'), may hold values from 0 to 64
- context_count: int32 [128], P('dp'), may hold values from 0 to 10
- gain_one: float32 [512], replicated, may hold values from 0.5 to 1.5
- shift_one: float32 [512], replicated, may hold values from -1.75 to 1.75
- query_w: bfloat16 [512, 512], P('dp', 'tensor'), may hold values from -0.25 to 0.25
- key_w: bfloat16 [512, 512], P('dp', 'tensor'), may hold values from -0.25 to 0.25
- value_w: bfloat16 [512, 512], P('dp', 'tensor'), may hold values from -0.25 to 0.25
- out_w: bfloat16 [512, 512], P('tensor', 'dp'), may hold values from -0.75 to 0.75
- gain_two: float32 [512], replicated, may hold values from 0.5 to 1.5
- shift_two: float32 [512], replicated, may hold values from -1.75 to 1.75
- inner_w: bfloat16 [512, 2048], P('dp', 'tensor'), may hold values from -0.25 to 0.25
- inner_b: float32 [2048], P('tensor'), may hold values from -3 to 3
- outer_w: bfloat16 [2048, 512], P('tensor', 'dp'), may hold values from -0.1875 to 0.1875
- outer_b: float32 [512], replicated, may hold values from -3 to 3
- cotangent: bfloat16 [65536, 512], P('dp'), may hold values from -6 to 6
Outputs:
- output: bfloat16 [65536, 512], P('dp')
- grad_frames: bfloat16 [65536, 512], P('dp')
- grad_context_keys: float32 [128, 10, 512], P('dp', None, 'tensor')
- grad_context_values: float32 [128, 10, 512], P('dp', None, 'tensor')
- grad_gain_one: float32 [512], P('dp')
- grad_shift_one: float32 [512], P('dp')
- grad_query_w: float32 [512, 512], P('dp', 'tensor')
- grad_key_w: float32 [512, 512], P('dp', 'tensor')
- grad_value_w: float32 [512, 512], P('dp', 'tensor')
- grad_out_w: float32 [512, 512], P('tensor', 'dp')
- grad_gain_two: float32 [512], P('dp')
- grad_shift_two: float32 [512], P('dp')
- grad_inner_w: float32 [512, 2048], P('dp', 'tensor')
- grad_inner_b: float32 [2048], P(('tensor', 'dp'))
- grad_outer_w: float32 [2048, 512], P('tensor', 'dp')
- grad_outer_b: float32 [512], P('dp')
The draws below stay inside these ranges and needn't reach their ends.
All inputs are finite; a program needn't handle non-finite values.
Results may differ from the reference program's by a relative error of at most 0.024.
Values may be sent and summed in bfloat16 or wider, within the bound.
No kernel may reach another device: no remote copies, remote signals or barrier semaphores. Data moves between devices by JAX's collectives and lax.ppermute only.
A program may use at most 192 MiB of HBM per device.

```python
import jax
import jax.numpy as jnp
from jax import lax

D = 512
HEADS = 8
HEAD_DIM = 64
FF = 2048
SPAN = 512
LEFT = 10
RIGHT = 2
TIME_MAX = 40
FREQ_MAX = 64
SPANS = 128
FRAMES = 65536
N_TENSOR = 2


def set_ends(entries, stream_key, smallest, largest):
    place = [jax.random.randint(jax.random.fold_in(stream_key, axis), (), 0, length) for axis, length in enumerate(entries.shape)]
    longest = entries.shape.index(max(entries.shape))
    next_to = place[:longest] + [(place[longest] + 1) % entries.shape[longest]] + place[longest + 1:]
    return entries.at[tuple(place)].set(smallest).at[tuple(next_to)].set(largest)


def steps_of(own_key, dims, shards, least, top_value):
    def one(dim, shards_of):
        heights = jax.random.uniform(jax.random.fold_in(jax.random.fold_in(own_key, 6), dim), (shards_of,), jnp.float32, least / len(shards), top_value / len(shards))
        return jnp.repeat(jnp.exp(heights), dims[dim] // shards_of).reshape((-1,) + (1,) * (len(dims) - dim - 1))

    level = one(*shards[0])
    for cut in shards[1:]:
        level = level * one(*cut)
    return level


def normal_values(rng, dims, spread, limit, shards=(), held_as=jnp.bfloat16):
    values = spread * jax.random.normal(rng, dims, jnp.float32)
    if shards:
        values = values * steps_of(rng, dims, shards, -0.22, 0.18)
    return jnp.clip(values, -limit, limit).astype(held_as)


def setup_inputs(seed: int = 0) -> dict:
    splits = jax.random.split(jax.random.key(seed), 22)
    return {
        "frames": normal_values(splits[0], (FRAMES, D), 1.0, 6.0, ((0, 16),)),
        "context_keys": normal_values(splits[1], (SPANS, LEFT, D), 1.0, 6.0, ((0, 16), (2, 2))),
        "context_values": normal_values(splits[2], (SPANS, LEFT, D), 1.0, 6.0, ((0, 16), (2, 2))),
        "time_start": set_ends(jax.random.randint(splits[3], (SPANS,), 0, SPAN), jax.random.fold_in(splits[3], 1), 0, SPAN - 1).astype(jnp.int32),
        "time_width": set_ends(jax.random.randint(splits[4], (SPANS,), 0, TIME_MAX + 1), jax.random.fold_in(splits[4], 1), 0, TIME_MAX).astype(jnp.int32),
        "freq_start": set_ends(jax.random.randint(splits[5], (SPANS,), 0, D), jax.random.fold_in(splits[5], 1), 0, D - 1).astype(jnp.int32),
        "freq_width": set_ends(jax.random.randint(splits[6], (SPANS,), 0, FREQ_MAX + 1), jax.random.fold_in(splits[6], 1), 0, FREQ_MAX).astype(jnp.int32),
        "context_count": set_ends(jax.random.randint(splits[7], (SPANS,), 0, LEFT + 1), jax.random.fold_in(splits[7], 1), 0, LEFT).astype(jnp.int32),
        "gain_one": jnp.clip(1.0 + 0.1 * jax.random.normal(splits[8], (D,), jnp.float32), 0.5, 1.5),
        "shift_one": normal_values(splits[9], (D,), 0.3, 1.75, (), jnp.float32),
        "query_w": normal_values(splits[10], (D, D), D ** -0.5, 0.25, ((0, 16), (1, 2))),
        "key_w": normal_values(splits[11], (D, D), D ** -0.5, 0.25, ((0, 16), (1, 2))),
        "value_w": normal_values(splits[12], (D, D), D ** -0.5, 0.25, ((0, 16), (1, 2))),
        "out_w": normal_values(splits[13], (D, D), (D // 8) ** -0.5, 0.75, ((0, 2), (1, 16))),
        "gain_two": jnp.clip(1.0 + 0.1 * jax.random.normal(splits[14], (D,), jnp.float32), 0.5, 1.5),
        "shift_two": normal_values(splits[15], (D,), 0.3, 1.75, (), jnp.float32),
        "inner_w": normal_values(splits[16], (D, FF), D ** -0.5, 0.25, ((0, 16), (1, 2))),
        "inner_b": normal_values(splits[17], (FF,), 0.5, 3.0, ((0, 2),), jnp.float32),
        "outer_w": normal_values(splits[18], (FF, D), (FF // 2) ** -0.5, 0.1875, ((0, 2), (1, 16))),
        "outer_b": normal_values(splits[19], (D,), 0.5, 3.0, (), jnp.float32),
        "cotangent": normal_values(splits[20], (FRAMES, D), 1.0, 6.0, ((0, 16),)),
    }


@jax.custom_vjp
def low(v):
    return lax.optimization_barrier(v.astype(jnp.bfloat16)).astype(jnp.float32)

@jax.custom_vjp
def low_back(v):
    return v

def low_keep(v):
    return (low(v), None)

def low_pass(kept, grad):
    return (grad,)

def back_keep(v):
    return (v, None)

def back_low(kept, grad):
    return (low(grad),)
low.defvjp(low_keep, low_pass)
low_back.defvjp(back_keep, back_low)
epsilon = 1e-05
highest = lax.Precision.HIGHEST

def layer_norm(values, gain_row, shift_row):
    center = values - lax.optimization_barrier(jnp.mean(values, axis=-1, keepdims=True))
    variance = lax.optimization_barrier(jnp.mean(center * center, axis=-1, keepdims=True))
    return center * lax.rsqrt(variance + epsilon) * gain_row + shift_row

def gelu_tanh(values):
    return 0.5 * values * (1.0 + jnp.tanh(0.7978845608 * (values + 0.044715 * values * values * values)))

def band_mask(context_count):
    row_index = jnp.arange(SPAN)[:, None]
    places = jnp.arange(LEFT + SPAN)[None, :] - LEFT
    inside = (places >= row_index - LEFT) & (places <= row_index + RIGHT)
    return inside & (places >= -context_count)

def keep_masks(time_start, time_width, freq_start, freq_width):
    positions = jnp.arange(SPAN)[None, :]
    hidden_time = (positions >= time_start[:, None]) & (positions < time_start[:, None] + time_width[:, None])
    columns = jnp.arange(D)[None, :]
    hidden_freq = (columns >= freq_start[:, None]) & (columns < freq_start[:, None] + freq_width[:, None])
    keep_time = jnp.where(hidden_time, 0.0, 1.0).astype(jnp.float32)
    keep_freq = jnp.where(hidden_freq, 0.0, 1.0).astype(jnp.float32)
    return (keep_time, keep_freq)

def span_attention(queries, keys_all, values_all, context_count):
    scores = jnp.einsum('qhe,khe->hqk', queries, keys_all, precision=highest) * HEAD_DIM ** (-0.5)
    scores = low_back(scores)
    scores = jnp.where(band_mask(context_count)[None], scores, -1e+30)
    row_top = lax.optimization_barrier(jnp.max(scores, axis=-1, keepdims=True))
    expo = jnp.exp(scores - row_top)
    probs = expo / lax.optimization_barrier(jnp.sum(expo, axis=-1, keepdims=True))
    probs = low(probs)
    return jnp.einsum('hqk,khe->qhe', probs, values_all, precision=highest)

def span_forward(params, span_frames, span_keys, span_values, keep_time, keep_freq, context_count):
    gain_one, shift_one, query_w, key_w, value_w, out_w, gain_two, shift_two, inner_w, inner_b, outer_w, outer_b = params
    masked = span_frames * keep_time[:, None] * keep_freq[None, :]
    normed_one = low(layer_norm(masked, gain_one, shift_one))
    queries = low(low_back(jnp.dot(normed_one, query_w, precision=highest)))
    keys_new = low(low_back(jnp.dot(normed_one, key_w, precision=highest)))
    values_new = low(low_back(jnp.dot(normed_one, value_w, precision=highest)))
    keys_all = jnp.concatenate([span_keys, keys_new], axis=0).reshape(LEFT + SPAN, HEADS, HEAD_DIM)
    values_all = jnp.concatenate([span_values, values_new], axis=0).reshape(LEFT + SPAN, HEADS, HEAD_DIM)
    attended = span_attention(queries.reshape(SPAN, HEADS, HEAD_DIM), keys_all, values_all, context_count)
    attended = low(low_back(attended.reshape(SPAN, D)))
    grouped = attended.reshape(SPAN, N_TENSOR, D // N_TENSOR)
    out_groups = out_w.reshape(N_TENSOR, D // N_TENSOR, D)
    partials = jnp.einsum('rgc,gcd->grd', grouped, out_groups, precision=highest)
    mixed_sum = low_back(lax.optimization_barrier(jnp.sum(low(partials), axis=0)))
    middle = masked + mixed_sum
    normed_two = low(layer_norm(middle, gain_two, shift_two))
    inner_act = low_back(jnp.dot(normed_two, inner_w, precision=highest) + inner_b)
    hidden = low(gelu_tanh(inner_act))
    hidden_groups = hidden.reshape(SPAN, N_TENSOR, FF // N_TENSOR)
    outer_groups = outer_w.reshape(N_TENSOR, FF // N_TENSOR, D)
    partials_two = jnp.einsum('rgc,gcd->grd', hidden_groups, outer_groups, precision=highest)
    return middle + lax.optimization_barrier(jnp.sum(low(partials_two), axis=0)) + outer_b

def reference(frames, context_keys, context_values, time_start, time_width, freq_start, freq_width, context_count, gain_one, shift_one, query_w, key_w, value_w, out_w, gain_two, shift_two, inner_w, inner_b, outer_w, outer_b, cotangent):
    params = tuple((item.astype(jnp.float32) for item in (gain_one, shift_one, query_w, key_w, value_w, out_w, gain_two, shift_two, inner_w, inner_b, outer_w, outer_b)))
    zero_grads = tuple((jnp.zeros(item.shape, jnp.float32) for item in params))
    keep_time, keep_freq = keep_masks(time_start, time_width, freq_start, freq_width)
    pieces = (frames.reshape(SPANS, SPAN, D), context_keys, context_values, keep_time, keep_freq, context_count, cotangent.reshape(SPANS, SPAN, D))

    def one_span(totals, piece):
        span_frames, span_keys, span_values, span_time, span_freq, span_count, span_cot = piece

        def local(weights, inputs_x, keys_c, values_c):
            return span_forward(weights, inputs_x, keys_c, values_c, span_time, span_freq, span_count)
        output, pullback = jax.vjp(local, params, span_frames.astype(jnp.float32), span_keys.astype(jnp.float32), span_values.astype(jnp.float32))
        grad_params, grad_input, grad_keys, grad_values = pullback(span_cot.astype(jnp.float32))
        totals = tuple((left_item + right_item for left_item, right_item in zip(totals, grad_params)))
        return (totals, (output.astype(jnp.bfloat16), grad_input.astype(jnp.bfloat16), grad_keys, grad_values))
    totals, (outputs, grad_inputs, grad_keys, grad_values) = lax.scan(one_span, zero_grads, pieces)
    g_gain_one, g_shift_one, g_query, g_key, g_value, g_out, g_gain_two, g_shift_two, g_inner, g_inner_b, g_outer, g_outer_b = totals
    return (outputs.reshape(FRAMES, D), grad_inputs.reshape(FRAMES, D), grad_keys, grad_values, g_gain_one, g_shift_one, g_query, g_key, g_value, g_out, g_gain_two, g_shift_two, g_inner, g_inner_b, g_outer, g_outer_b)
```

```python
import functools

import jax
import jax.numpy as jnp
from jax import lax
from jax.experimental import pallas as pl
from jax.experimental.pallas import tpu as pltpu
from jax.sharding import PartitionSpec as P

D = 512
HEAD_DIM = 64
SPAN = 512
LEFT = 10
RIGHT = 2
FF = 2048
PAIR = 2 * HEAD_DIM
PAIRS = D // PAIR
GROUPS = 2
EG = D // GROUPS
FG = FF // GROUPS
TOP = 16
KEYS = TOP + SPAN + 16
EXTRA = 128
NEGATIVE = -1e30
epsilon = 1e-05
F32 = jnp.float32
BF16 = jnp.bfloat16
VMEM_LIMIT = 56 * 1024 * 1024
FORWARD_BLOCKS = tuple((96, 96 * b, 96 * b) for b in range(5)) + ((32, 480, 416),)


def dot(a, b):
    return lax.dot_general(a, b, (((1,), (0,)), ((), ())), preferred_element_type=F32)


def dot_nt(a, b):
    return lax.dot_general(a, b, (((1,), (1,)), ((), ())), preferred_element_type=F32)


def dot_tn(a, b):
    return lax.dot_general(a, b, (((0,), (0,)), ((), ())), preferred_element_type=F32)


def iota(shape, dim):
    return lax.broadcasted_iota(jnp.int32, shape, dim)


def row_mean(v):
    return jnp.sum(v, axis=-1, keepdims=True) * (1.0 / D)


def normalize(v):
    center = v - row_mean(v)
    scale = lax.rsqrt(row_mean(center * center) + epsilon)
    return center * scale, scale


def fold_rows(v):
    total = v[0:8]
    for r in range(8, v.shape[0], 8):
        total = total + v[r : r + 8]
    return total


def masked_rows(meta, span, frames_ref, row0, rows):
    places = iota((rows, 1), 0) + row0
    hide_t = (places >= meta[1, span]) & (places < meta[1, span] + meta[2, span])
    columns = iota((1, D), 1)
    hide_f = (columns >= meta[3, span]) & (columns < meta[3, span] + meta[4, span])
    keep = jnp.where(hide_t, 0.0, 1.0) * jnp.where(hide_f, 0.0, 1.0)
    return frames_ref[pl.ds(row0, rows), :].astype(F32) * keep, keep


def load_slots(places, slots_ref, w_ref, sems, start):
    count, rows = slots_ref.shape[0], slots_ref.shape[1]
    for j in range(count):
        copy = pltpu.make_async_copy(
            slots_ref.at[j],
            w_ref.at[places[0, j], pl.ds(pl.multiple_of(places[1, j], 16), rows), :],
            sems.at[j],
        )
        if start:
            copy.start()
        else:
            copy.wait()


def low_half():
    return iota((1, PAIR), 1) < HEAD_DIM


def attention_forward_kernel(
    meta, places, frames_ref, ctx_k_ref, ctx_v_ref, norm_ref, slots_ref,
    n1_ref, q_ref, k_ref, v_ref, att_ref, mid_ref,
    w_ref, sems, ke_ref, ko_ref, ve_ref, vo_ref, bias_ref, ones_ref,
):
    step = pl.program_id(0)
    span = meta[0, 0] + step

    @pl.when(step == 0)
    def _():
        load_slots(places, slots_ref, w_ref, sems, True)
        r, c = iota((96, 256), 0), iota((96, 256), 1) % 128
        bias_ref[...] = jnp.where((c >= r + 6) & (c <= r + 18), 0.0, NEGATIVE)
        r, c = iota((256, 128), 0), iota((256, 128), 1)
        ones_ref[...] = jnp.where((r < 128) == (c < 64), 1.0, 0.0).astype(BF16)

    for r0 in range(0, SPAN, 128):
        masked, _ = masked_rows(meta, span, frames_ref, r0, 128)
        xhat, _ = normalize(masked)
        n1_ref[r0 : r0 + 128, :] = (xhat * norm_ref[0:1, :] + norm_ref[1:2, :]).astype(BF16)

    @pl.when(step == 0)
    def _():
        load_slots(places, slots_ref, w_ref, sems, False)

    k_ref[0, 0:TOP, :] = ctx_k_ref[0]
    v_ref[0, 0:TOP, :] = ctx_v_ref[0]
    k_ref[0, TOP + SPAN :, :] = jnp.zeros((16, D), BF16)
    v_ref[0, TOP + SPAN :, :] = jnp.zeros((16, D), BF16)
    n1 = n1_ref[...]
    for g in range(GROUPS):
        cols = slice(g * EG, (g + 1) * EG)
        q_ref[:, cols] = (dot(n1, w_ref[g, :, 0:EG]) * HEAD_DIM**-0.5).astype(BF16)
        k_ref[0, TOP : TOP + SPAN, cols] = dot(n1, w_ref[g, :, EG : 2 * EG]).astype(BF16)
        v_ref[0, TOP : TOP + SPAN, cols] = dot(n1, w_ref[g, :, 2 * EG : 3 * EG]).astype(BF16)

    even = iota((1, D), 1) % PAIR < HEAD_DIM
    zero = jnp.zeros((), BF16)
    for r0, rows in ((0, 144), (144, 144), (288, 128), (416, 128)):
        kb, vb = k_ref[0, r0 : r0 + rows, :], v_ref[0, r0 : r0 + rows, :]
        ke_ref[r0 : r0 + rows, :] = jnp.where(even, kb, zero)
        ko_ref[r0 : r0 + rows, :] = jnp.where(even, zero, kb)
        ve_ref[r0 : r0 + rows, :] = jnp.where(even, vb, zero)
        vo_ref[r0 : r0 + rows, :] = jnp.where(even, zero, vb)

    first = TOP - meta[5, span]
    for j in range(PAIRS):
        lanes = slice(j * PAIR, (j + 1) * PAIR)
        for rows, q0, w0 in FORWARD_BLOCKS:
            window = slice(w0, w0 + 128)
            keys = jnp.concatenate([ke_ref[window, lanes], ko_ref[window, lanes]], axis=0)
            scores = dot_nt(q_ref[q0 : q0 + rows, lanes], keys)
            if q0 == 480:
                r, c = iota((rows, 256), 0), iota((rows, 256), 1) % 128 - 64
                bias = jnp.where((c >= r + 6) & (c <= r + 18) & (c < 48), 0.0, NEGATIVE)
            else:
                bias = bias_ref[...]
            scores = scores + bias
            if q0 == 0:
                scores = jnp.where(iota((rows, 256), 1) % 128 >= first, scores, NEGATIVE)
            expo = []
            for half in (scores[:, :128], scores[:, 128:]):
                top = jnp.max(half, axis=-1, keepdims=True)
                expo.append(jnp.exp(half - top).astype(BF16))
            values = jnp.concatenate([ve_ref[window, lanes], vo_ref[window, lanes]], axis=0)
            values = jnp.concatenate([values, ones_ref[...]], axis=1)
            mixed = dot(jnp.concatenate(expo, axis=1), values)
            att_ref[q0 : q0 + rows, lanes] = (mixed[:, :PAIR] / mixed[:, PAIR:]).astype(BF16)

    att = att_ref[...]
    mid_ref[...] = dot_nt(att[:, :EG], w_ref[0, :, 3 * EG :]) + dot_nt(
        att[:, EG:], w_ref[1, :, 3 * EG :]
    )
    for r0 in range(0, SPAN, 128):
        masked, _ = masked_rows(meta, span, frames_ref, r0, 128)
        mid_ref[r0 : r0 + 128, :] = mid_ref[r0 : r0 + 128, :] + masked


def spec(block, index, **kw):
    return pl.BlockSpec(block, index, **kw)


def params():
    return pltpu.CompilerParams(
        dimension_semantics=("arbitrary",), vmem_limit_bytes=VMEM_LIMIT
    )


def attention_forward(meta, places, frames, ctx_k, ctx_v, norm, slots, spans):
    rows = spans * SPAN
    whole = pl.BlockSpec(memory_space=pl.ANY)
    row_block = spec((SPAN, D), lambda s, m, p: (s, 0))
    keys_block = spec((1, KEYS, D), lambda s, m, p: (s, 0, 0))
    flops = 2 * rows * D * D * 4 + 2 * rows * D * 640
    return pl.pallas_call(
        attention_forward_kernel,
        grid_spec=pltpu.PrefetchScalarGridSpec(
            num_scalar_prefetch=2,
            grid=(spans,),
            in_specs=[
                spec((SPAN, D), lambda s, m, p: (m[0, 0] + s, 0)),
                spec((1, TOP, D), lambda s, m, p: (m[0, 1] + s, 0, 0)),
                spec((1, TOP, D), lambda s, m, p: (m[0, 1] + s, 0, 0)),
                spec((8, D), lambda s, m, p: (0, 0)),
                whole,
            ],
            out_specs=[row_block, row_block, keys_block, keys_block, row_block, row_block],
            scratch_shapes=[
                pltpu.VMEM((GROUPS, D, 4 * EG), BF16),
                pltpu.SemaphoreType.DMA((slots.shape[0],)),
                pltpu.VMEM((KEYS, D), BF16),
                pltpu.VMEM((KEYS, D), BF16),
                pltpu.VMEM((KEYS, D), BF16),
                pltpu.VMEM((KEYS, D), BF16),
                pltpu.VMEM((96, 256), F32),
                pltpu.VMEM((256, 128), BF16),
            ],
        ),
        out_shape=[
            jax.ShapeDtypeStruct((rows, D), BF16),
            jax.ShapeDtypeStruct((rows, D), BF16),
            jax.ShapeDtypeStruct((spans, KEYS, D), BF16),
            jax.ShapeDtypeStruct((spans, KEYS, D), BF16),
            jax.ShapeDtypeStruct((rows, D), BF16),
            jax.ShapeDtypeStruct((rows, D), F32),
        ],
        compiler_params=params(),
        cost_estimate=pl.CostEstimate(
            flops=flops, bytes_accessed=rows * D * 14, transcendentals=rows * 1024
        ),
        name="attention_forward",
    )(meta, places, frames, ctx_k, ctx_v, norm, slots)


def feed_forward_kernel(
    meta, places, mid_ref, cot_ref, norm_ref, inner_b_ref, slots_ref,
    out_ref, gm_ref, grad_ref, sums_ref, sums_b_ref,
    w_ref, sems, n2_ref, n2t_ref, cott_ref, hid_ref, gin_ref, dn_ref, acc_ref,
):
    step = pl.program_id(0)

    @pl.when(step == 0)
    def _():
        load_slots(places, slots_ref, w_ref, sems, True)
        acc_ref[...] = jnp.zeros_like(acc_ref)
        sums_ref[...] = jnp.zeros_like(sums_ref)
        sums_b_ref[...] = jnp.zeros_like(sums_b_ref)

    for r0 in range(0, SPAN, 128):
        xhat, _ = normalize(mid_ref[r0 : r0 + 128, :])
        n2_ref[r0 : r0 + 128, :] = (xhat * norm_ref[2:3, :] + norm_ref[3:4, :]).astype(BF16)
    n2t_ref[...] = n2_ref[...].T
    cott_ref[...] = cot_ref[...].T

    @pl.when(step == 0)
    def _():
        load_slots(places, slots_ref, w_ref, sems, False)

    chunk = 256
    for g in range(GROUPS):
        for c0 in range(0, FG, chunk):
            cols = slice(g * FG + c0, g * FG + c0 + chunk)
            act = dot(n2_ref[...], w_ref[g, :, c0 : c0 + chunk]) + inner_b_ref[0:1, cols]
            square = act * act
            tanh = jnp.tanh(act * (0.7978845608 + (0.7978845608 * 0.044715) * square))
            weight = 0.5 + 0.5 * tanh
            hidden = act * weight
            hid_ref[:, cols] = hidden.astype(BF16)
            slope = weight + (hidden - hidden * weight) * (
                2.0 * 0.7978845608 + (6.0 * 0.7978845608 * 0.044715) * square
            )
            grad = dot(cot_ref[...], w_ref[g, :, FG + c0 : FG + c0 + chunk]) * slope
            grad_low = grad.astype(BF16)
            gin_ref[:, cols] = grad_low
            sums_b_ref[:, cols] += fold_rows(grad_low.astype(F32))

    hid, gin = hid_ref, gin_ref
    out_ref[...] = (
        mid_ref[...]
        + dot_nt(hid[:, :FG], w_ref[0, :, FG:])
        + dot_nt(hid[:, FG:], w_ref[1, :, FG:])
        + norm_ref[4:5, :]
    ).astype(BF16)
    dn_ref[...] = dot_nt(gin[:, :FG], w_ref[0, :, :FG]) + dot_nt(gin[:, FG:], w_ref[1, :, :FG])
    for g in range(GROUPS):
        cols = slice(g * FG, (g + 1) * FG)
        acc_ref[g, :, :FG] += dot(n2t_ref[...], gin[:, cols])
        acc_ref[g, :, FG:] += dot(cott_ref[...], hid[:, cols])

    for r0 in range(0, SPAN, 128):
        rows = slice(r0, r0 + 128)
        xhat, scale = normalize(mid_ref[rows, :])
        grad = dn_ref[rows, :]
        cot = cot_ref[rows, :].astype(F32)
        sums_ref[0:8, :] += fold_rows(grad * xhat)
        sums_ref[8:16, :] += fold_rows(grad)
        sums_ref[16:24, :] += fold_rows(cot)
        t = grad * norm_ref[2:3, :]
        gm_ref[rows, :] = (cot + scale * (t - row_mean(t) - xhat * row_mean(t * xhat))).astype(BF16)

    @pl.when(step == pl.num_programs(0) - 1)
    def _():
        for g in range(GROUPS):
            grad_ref[g, :, : 2 * FG] = acc_ref[g].astype(BF16)
        grad_ref[:, :, 2 * FG :] = jnp.zeros((GROUPS, D, EXTRA), BF16)


def feed_forward(meta, places, mid, cot, norm, inner_b, slots, spans):
    rows = spans * SPAN
    whole = pl.BlockSpec(memory_space=pl.ANY)
    row_block = spec((SPAN, D), lambda s, m, p: (s, 0))
    return pl.pallas_call(
        feed_forward_kernel,
        grid_spec=pltpu.PrefetchScalarGridSpec(
            num_scalar_prefetch=2,
            grid=(spans,),
            in_specs=[
                row_block,
                spec((SPAN, D), lambda s, m, p: (m[0, 0] + s, 0)),
                spec((8, D), lambda s, m, p: (0, 0)),
                spec((1, FF), lambda s, m, p: (0, 0)),
                whole,
            ],
            out_specs=[
                row_block,
                row_block,
                spec((GROUPS, D, 2 * FG + EXTRA), lambda s, m, p: (0, 0, 0)),
                spec((24, D), lambda s, m, p: (0, 0)),
                spec((8, FF), lambda s, m, p: (0, 0)),
            ],
            scratch_shapes=[
                pltpu.VMEM((GROUPS, D, 2 * FG), BF16),
                pltpu.SemaphoreType.DMA((slots.shape[0],)),
                pltpu.VMEM((SPAN, D), BF16),
                pltpu.VMEM((D, SPAN), BF16),
                pltpu.VMEM((D, SPAN), BF16),
                pltpu.VMEM((SPAN, FF), BF16),
                pltpu.VMEM((SPAN, FF), BF16),
                pltpu.VMEM((SPAN, D), F32),
                pltpu.VMEM((GROUPS, D, 2 * FG), F32),
            ],
        ),
        out_shape=[
            jax.ShapeDtypeStruct((rows, D), BF16),
            jax.ShapeDtypeStruct((rows, D), BF16),
            jax.ShapeDtypeStruct((GROUPS, D, 2 * FG + EXTRA), BF16),
            jax.ShapeDtypeStruct((24, D), F32),
            jax.ShapeDtypeStruct((8, FF), F32),
        ],
        compiler_params=params(),
        cost_estimate=pl.CostEstimate(
            flops=12 * rows * D * FF, bytes_accessed=rows * D * 10, transcendentals=rows * FF
        ),
        name="feed_forward",
    )(meta, places, mid, cot, norm, inner_b, slots)


def attention_backward_kernel(
    meta, places, frames_ref, n1_ref, q_ref, k_ref, v_ref, att_ref, gm_ref, norm_ref, slots_ref,
    gf_ref, gck_ref, gcv_ref, grad_ref, sums_ref,
    w_ref, sems, gatt_ref, dq_ref, dk_ref, dv_ref, dkb_ref, dvb_ref, n1t_ref, gmt_ref, dn_ref,
    bias_ref, acc_ref,
):
    step = pl.program_id(0)
    span = meta[0, 0] + step

    @pl.when(step == 0)
    def _():
        load_slots(places, slots_ref, w_ref, sems, True)
        acc_ref[...] = jnp.zeros_like(acc_ref)
        sums_ref[...] = jnp.zeros_like(sums_ref)
        r, c = iota((160, 256), 0), iota((160, 256), 1) % 128
        bias_ref[...] = jnp.where((r >= c + 6) & (r <= c + 18), 0.0, NEGATIVE)

    n1t_ref[...] = n1_ref[...].T
    gmt_ref[...] = gm_ref[...].T

    @pl.when(step == 0)
    def _():
        load_slots(places, slots_ref, w_ref, sems, False)

    for g in range(GROUPS):
        gatt_ref[:, g * EG : (g + 1) * EG] = dot(gm_ref[...], w_ref[g, :, 3 * EG :]).astype(BF16)

    first = TOP - meta[5, span]
    even = low_half()
    zero = jnp.zeros((), BF16)
    for j in range(PAIRS):
        lanes = slice(j * PAIR, (j + 1) * PAIR)
        for b in range(SPAN // 128):
            rows, window = slice(128 * b, 128 * b + 128), slice(128 * b, 128 * b + 160)
            kw, vw = k_ref[0, window, lanes], v_ref[0, window, lanes]
            qb, ob = q_ref[rows, lanes], gatt_ref[rows, lanes]
            qs = jnp.concatenate([jnp.where(even, qb, zero), jnp.where(even, zero, qb)], axis=0)
            os = jnp.concatenate([jnp.where(even, ob, zero), jnp.where(even, zero, ob)], axis=0)
            scores = dot_nt(kw, qs) + bias_ref[...]
            if b == 0:
                scores = jnp.where(iota((160, 256), 0) >= first, scores, NEGATIVE)
            if b == SPAN // 128 - 1:
                scores = jnp.where(iota((160, 256), 0) < 144, scores, NEGATIVE)
            expo = jnp.exp(scores - jnp.max(scores, axis=0, keepdims=True))
            probs = expo * (1.0 / jnp.sum(expo, axis=0, keepdims=True))
            grad_probs = dot_nt(vw, os)
            delta = jnp.sum(probs * grad_probs, axis=0, keepdims=True)
            ds = (probs * (grad_probs - delta)).astype(BF16)
            dv = dot(probs.astype(BF16), os)
            dk = dot(ds, qs)
            if b == 0:
                dkb_ref[window, lanes] = dk
                dvb_ref[window, lanes] = dv
            else:
                lap, rest = slice(128 * b, 128 * b + 32), slice(128 * b + 32, 128 * b + 160)
                dkb_ref[lap, lanes] += dk[:32]
                dvb_ref[lap, lanes] += dv[:32]
                dkb_ref[rest, lanes] = dk[32:]
                dvb_ref[rest, lanes] = dv[32:]
            dq = dot_tn(ds, kw)
            dq = jnp.where(even, dq[:128], dq[128:]) * HEAD_DIM**-0.5
            dq_ref[rows, lanes] = dq.astype(BF16)
    gck_ref[0] = dkb_ref[0:TOP, :]
    gcv_ref[0] = dvb_ref[0:TOP, :]
    dk_ref[...] = dkb_ref[TOP : TOP + SPAN, :].astype(BF16)
    dv_ref[...] = dvb_ref[TOP : TOP + SPAN, :].astype(BF16)

    for g in range(GROUPS):
        cols = slice(g * EG, (g + 1) * EG)
        acc_ref[g, :, 0:EG] += dot(n1t_ref[...], dq_ref[:, cols])
        acc_ref[g, :, EG : 2 * EG] += dot(n1t_ref[...], dk_ref[:, cols])
        acc_ref[g, :, 2 * EG : 3 * EG] += dot(n1t_ref[...], dv_ref[:, cols])
        acc_ref[g, :, 3 * EG :] += dot(gmt_ref[...], att_ref[:, cols])
    total = None
    for g in range(GROUPS):
        cols = slice(g * EG, (g + 1) * EG)
        for m, ref in enumerate((dq_ref, dk_ref, dv_ref)):
            term = dot_nt(ref[:, cols], w_ref[g, :, m * EG : (m + 1) * EG])
            total = term if total is None else total + term
    dn_ref[...] = total
    for r0 in range(0, SPAN, 128):
        rows = slice(r0, r0 + 128)
        masked, keep = masked_rows(meta, span, frames_ref, r0, 128)
        xhat, scale = normalize(masked)
        grad = dn_ref[rows, :]
        sums_ref[0:8, :] += fold_rows(grad * xhat)
        sums_ref[8:16, :] += fold_rows(grad)
        t = grad * norm_ref[0:1, :]
        back = scale * (t - row_mean(t) - xhat * row_mean(t * xhat))
        gf_ref[rows, :] = ((gm_ref[rows, :].astype(F32) + back) * keep).astype(BF16)

    @pl.when(step == pl.num_programs(0) - 1)
    def _():
        for g in range(GROUPS):
            grad_ref[g, :, : 4 * EG] = acc_ref[g].astype(BF16)
        grad_ref[:, :, 4 * EG :] = jnp.zeros((GROUPS, D, EXTRA), BF16)


def attention_backward(meta, places, frames, n1, q, k, v, att, gm, norm, slots, spans):
    rows = spans * SPAN
    whole = pl.BlockSpec(memory_space=pl.ANY)
    row_block = spec((SPAN, D), lambda s, m, p: (s, 0))
    keys_block = spec((1, KEYS, D), lambda s, m, p: (s, 0, 0))
    top_block = spec((1, TOP, D), lambda s, m, p: (s, 0, 0))
    low = pltpu.VMEM((SPAN, D), BF16)
    return pl.pallas_call(
        attention_backward_kernel,
        grid_spec=pltpu.PrefetchScalarGridSpec(
            num_scalar_prefetch=2,
            grid=(spans,),
            in_specs=[
                spec((SPAN, D), lambda s, m, p: (m[0, 0] + s, 0)),
                row_block,
                row_block,
                keys_block,
                keys_block,
                row_block,
                row_block,
                spec((8, D), lambda s, m, p: (0, 0)),
                whole,
            ],
            out_specs=[
                row_block,
                top_block,
                top_block,
                spec((GROUPS, D, 4 * EG + EXTRA), lambda s, m, p: (0, 0, 0)),
                spec((16, D), lambda s, m, p: (0, 0)),
            ],
            scratch_shapes=[
                pltpu.VMEM((GROUPS, D, 4 * EG), BF16),
                pltpu.SemaphoreType.DMA((slots.shape[0],)),
                low,
                low,
                low,
                low,
                pltpu.VMEM((KEYS, D), F32),
                pltpu.VMEM((KEYS, D), F32),
                low,
                low,
                pltpu.VMEM((SPAN, D), F32),
                pltpu.VMEM((160, 256), F32),
                pltpu.VMEM((GROUPS, D, 4 * EG), F32),
            ],
        ),
        out_shape=[
            jax.ShapeDtypeStruct((rows, D), BF16),
            jax.ShapeDtypeStruct((spans, TOP, D), F32),
            jax.ShapeDtypeStruct((spans, TOP, D), F32),
            jax.ShapeDtypeStruct((GROUPS, D, 4 * EG + EXTRA), BF16),
            jax.ShapeDtypeStruct((16, D), F32),
        ],
        compiler_params=params(),
        cost_estimate=pl.CostEstimate(
            flops=2 * rows * D * D * 8 + 2 * rows * D * 1600,
            bytes_accessed=rows * D * 14,
            transcendentals=rows * 1280,
        ),
        name="attention_backward",
    )(meta, places, frames, n1, q, k, v, att, gm, norm, slots)


BITS = {"core": ("dp", 1), "y": ("dp", 2), "z1": ("dp", 4), "z2": ("dp", 8), "x": ("tensor", 1)}
BIT_DIM = {"z2": 1, "z1": 2, "y": 3, "core": 4, "x": 0}


def swap(value, bit):
    axis, distance = BITS[bit]
    count = lax.axis_size(axis)
    return lax.ppermute(value, axis, [(i, i ^ distance) for i in range(count)])


def my_bit(bit):
    axis, distance = BITS[bit]
    return (lax.axis_index(axis) // distance) % 2


def gather_slots(piece, order):
    held = piece[None]
    for bit in order:
        held = jnp.concatenate([held, swap(held, bit)], axis=0)
    return held


def slot_places(order, rows):
    groups, firsts = [], []
    dp, tensor = lax.axis_index("dp"), lax.axis_index("tensor")
    for j in range(2 ** len(order)):
        dp_flip = sum(BITS[b][1] for i, b in enumerate(order) if j >> i & 1 and b != "x")
        x_flip = sum(1 for i, b in enumerate(order) if j >> i & 1 and b == "x")
        groups.append(tensor ^ x_flip)
        firsts.append((dp ^ dp_flip) * rows)
    return jnp.stack([jnp.stack(groups), jnp.stack(firsts)]).astype(jnp.int32)


def scatter_sum(grad, order):
    columns = grad.shape[-1]
    held = grad.reshape(2, 2, 2, 2, 2, -1, columns)
    for bit in order:
        dim, mine = BIT_DIM[bit], my_bit(bit)
        keep = lax.dynamic_index_in_dim(held, mine, dim, keepdims=True)
        send = lax.dynamic_index_in_dim(held, 1 - mine, dim, keepdims=True)
        held = (keep.astype(F32) + swap(send, bit).astype(F32)).astype(BF16)
    return held.reshape(-1, columns)


ATTENTION_ORDER = ("z2", "z1", "y", "x", "core")
FEED_ORDER = ("z2", "z1", "x", "y", "core")
ATTENTION_SUM = ("core", "x", "y", "z1", "z2")
FEED_SUM = ("core", "y", "z1", "z2", "x")


def body(
    frames,
    context_keys,
    context_values,
    time_start,
    time_width,
    freq_start,
    freq_width,
    context_count,
    gain_one,
    shift_one,
    query_w,
    key_w,
    value_w,
    out_w,
    gain_two,
    shift_two,
    inner_w,
    inner_b,
    outer_w,
    outer_b,
    cotangent,
):
    tensor, dp = lax.axis_size("tensor"), lax.axis_size("dp")
    tuned = tensor == 2 and dp == 16
    spans = time_start.shape[0] // tensor
    t_index = lax.axis_index("tensor")
    base = t_index * spans

    attention_piece = jnp.concatenate([query_w, key_w, value_w, out_w.T], axis=1)
    feed_piece = jnp.concatenate([inner_w, outer_w.T], axis=1)
    inner_b_full = lax.all_gather(inner_b, "tensor", axis=0, tiled=True).reshape(1, FF)
    if tuned:
        attention_slots = gather_slots(attention_piece, ATTENTION_ORDER)
        feed_slots = gather_slots(feed_piece, FEED_ORDER)
        attention_places = slot_places(ATTENTION_ORDER, attention_piece.shape[0])
        feed_places = slot_places(FEED_ORDER, feed_piece.shape[0])
    else:
        def canonical(parts, width):
            grouped = []
            for part in parts:
                whole = lax.all_gather(part, "dp", axis=0, tiled=True)
                whole = lax.all_gather(whole, "tensor", axis=1, tiled=True)
                grouped.append(whole.reshape(D, GROUPS, width).swapaxes(0, 1))
            return jnp.concatenate(grouped, axis=2)

        attention_slots = canonical((query_w, key_w, value_w, out_w.T), EG)
        feed_slots = canonical((inner_w, outer_w.T), FG)
        attention_places = feed_places = jnp.array([[0, 1], [0, 0]], jnp.int32)

    context = jnp.stack([context_keys, context_values])
    context = lax.all_to_all(context, "tensor", split_axis=1, concat_axis=3, tiled=True)
    context = jnp.pad(context, ((0, 0), (0, 0), (TOP - LEFT, 0), (0, 0)))

    first_row = jnp.zeros_like(time_start).at[0].set(base)
    meta = jnp.stack(
        [first_row, time_start, time_width, freq_start, freq_width, context_count]
    ).astype(jnp.int32)
    norm = jnp.stack(
        [gain_one, shift_one, gain_two, shift_two, outer_b]
        + [jnp.zeros_like(gain_one)] * 3
    )

    n1, q, k, v, att, mid = attention_forward(
        meta, attention_places, frames, context[0], context[1], norm, attention_slots, spans
    )
    out_half, gm, feed_grad, sums_two, sums_b = feed_forward(
        meta, feed_places, mid, cotangent, norm, inner_b_full, feed_slots, spans
    )
    frames_half, gck, gcv, attention_grad, sums_one = attention_backward(
        meta, attention_places, frames, n1, q, k, v, att, gm, norm, attention_slots, spans
    )

    def both(half):
        if not tuned:
            return lax.all_gather(half, "tensor", axis=0, tiled=True)
        other = swap(half, "x")
        rows = half.shape[0]
        whole = jnp.zeros((2 * rows, D), half.dtype)
        whole = lax.dynamic_update_slice_in_dim(whole, half, t_index * rows, 0)
        return lax.dynamic_update_slice_in_dim(whole, other, (1 - t_index) * rows, 0)

    output = both(out_half)
    grad_frames = both(frames_half)
    grad_context = jnp.stack([gck, gcv])[:, :, TOP - LEFT :]
    grad_context = lax.all_to_all(grad_context, "tensor", split_axis=3, concat_axis=1, tiled=True)

    gain_two_sum, shift_two_sum, outer_b_sum = (
        jnp.sum(sums_two[8 * i : 8 * i + 8], axis=0) for i in range(3)
    )
    gain_one_sum, shift_one_sum = (jnp.sum(sums_one[8 * i : 8 * i + 8], axis=0) for i in range(2))
    inner_b_sum = jnp.sum(sums_b, axis=0)

    if tuned:
        def shared(item):
            return jnp.broadcast_to(item.reshape(1, dp, -1), (GROUPS, dp, D // dp))

        def with_extra(grad, vectors):
            row = jnp.concatenate(vectors, axis=2).astype(BF16)
            row = jnp.pad(row, ((0, 0), (0, 0), (0, 2 * EXTRA - row.shape[2])))
            block = row.reshape(GROUPS, dp, 2, EXTRA)
            block = jnp.pad(block, ((0, 0), (0, 0), (0, D // dp - 2), (0, 0)))
            block = block.reshape(GROUPS, D, EXTRA)
            return lax.dynamic_update_slice(grad, block, (0, 0, grad.shape[2] - EXTRA))

        feed_sum = scatter_sum(
            with_extra(
                feed_grad,
                [inner_b_sum.reshape(GROUPS, dp, -1)]
                + [shared(item) for item in (gain_two_sum, shift_two_sum, outer_b_sum)],
            ),
            FEED_SUM,
        ).astype(F32)
        attention_sum = scatter_sum(
            with_extra(attention_grad, [shared(gain_one_sum), shared(shift_one_sum)]), ATTENTION_SUM
        ).astype(F32)
        extra = feed_sum[:2, 2 * FG :].reshape(-1)
        sum_inner_b, sum_gain_two, sum_shift_two, sum_outer_b = (
            extra[:64], extra[64:96], extra[96:128], extra[128:160]
        )
        extra = attention_sum[0, 4 * EG :]
        sum_gain_one, sum_shift_one = extra[:32], extra[32:64]
        sum_query, sum_key, sum_value, sum_out = (
            attention_sum[:, i * EG : (i + 1) * EG] for i in range(4)
        )
        sum_inner, sum_outer = feed_sum[:, :FG], feed_sum[:, FG : 2 * FG]
    else:
        def whole_grad(grad, index, width):
            return grad[:, :, index * width : (index + 1) * width].swapaxes(0, 1).reshape(D, -1)

        def scattered(grad):
            part = lax.psum_scatter(grad, "dp", scatter_dimension=0, tiled=True)
            return lax.psum_scatter(part, "tensor", scatter_dimension=1, tiled=True).astype(F32)

        def vector(item):
            item = lax.psum(item, "tensor")
            return lax.psum_scatter(item, "dp", scatter_dimension=0, tiled=True)

        sum_query, sum_key, sum_value, sum_out = (
            scattered(whole_grad(attention_grad, i, EG)) for i in range(4)
        )
        sum_inner, sum_outer = (scattered(whole_grad(feed_grad, i, FG)) for i in range(2))
        sum_gain_one, sum_shift_one = vector(gain_one_sum), vector(shift_one_sum)
        sum_gain_two, sum_shift_two = vector(gain_two_sum), vector(shift_two_sum)
        sum_outer_b = vector(outer_b_sum)
        sum_inner_b = lax.psum_scatter(inner_b_sum, "tensor", scatter_dimension=0, tiled=True)
        sum_inner_b = lax.psum_scatter(sum_inner_b, "dp", scatter_dimension=0, tiled=True)

    return (
        output,
        grad_frames,
        grad_context[0],
        grad_context[1],
        sum_gain_one,
        sum_shift_one,
        sum_query,
        sum_key,
        sum_value,
        sum_out.T,
        sum_gain_two,
        sum_shift_two,
        sum_inner,
        sum_inner_b,
        sum_outer.T,
        sum_outer_b,
    )


def solution(mesh):
    in_specs = (
        P("dp", None),
        P("dp", None, "tensor"),
        P("dp", None, "tensor"),
        P("dp"),
        P("dp"),
        P("dp"),
        P("dp"),
        P("dp"),
        P(),
        P(),
        P("dp", "tensor"),
        P("dp", "tensor"),
        P("dp", "tensor"),
        P("tensor", "dp"),
        P(),
        P(),
        P("dp", "tensor"),
        P("tensor"),
        P("tensor", "dp"),
        P(),
        P("dp", None),
    )
    out_specs = (
        P("dp", None),
        P("dp", None),
        P("dp", None, "tensor"),
        P("dp", None, "tensor"),
        P("dp"),
        P("dp"),
        P("dp", "tensor"),
        P("dp", "tensor"),
        P("dp", "tensor"),
        P("tensor", "dp"),
        P("dp"),
        P("dp"),
        P("dp", "tensor"),
        P(("tensor", "dp")),
        P("tensor", "dp"),
        P("dp"),
    )
    return jax.shard_map(body, mesh=mesh, in_specs=in_specs, out_specs=out_specs, check_vma=False)
```

```python
import functools

import jax
import jax.numpy as jnp
from jax import lax
from jax.experimental import pallas as pl
from jax.experimental.pallas import tpu as pltpu
from jax.sharding import PartitionSpec as P

D = 512
HEAD_DIM = 64
SPAN = 512
LEFT = 10
RIGHT = 2
FF = 2048
PAIR = 2 * HEAD_DIM
PAIRS = D // PAIR
GROUPS = 2
EG = D // GROUPS
FG = FF // GROUPS
TOP = 16
KEYS = TOP + SPAN + 16
EXTRA = 128
CHUNK = 2
NEGATIVE = -1e30
epsilon = 1e-05
F32 = jnp.float32
BF16 = jnp.bfloat16
VMEM_LIMIT = 56 * 1024 * 1024
FORWARD_BLOCKS = tuple((96, 96 * b, 96 * b) for b in range(5)) + ((32, 480, 416),)


def dot(a, b):
    return lax.dot_general(a, b, (((1,), (0,)), ((), ())), preferred_element_type=F32)


def dot_nt(a, b):
    return lax.dot_general(a, b, (((1,), (1,)), ((), ())), preferred_element_type=F32)


def dot_tn(a, b):
    return lax.dot_general(a, b, (((0,), (0,)), ((), ())), preferred_element_type=F32)


def iota(shape, dim):
    return lax.broadcasted_iota(jnp.int32, shape, dim)


def row_mean(v):
    return jnp.sum(v, axis=-1, keepdims=True) * (1.0 / D)


def normalize(v):
    center = v - row_mean(v)
    scale = lax.rsqrt(row_mean(center * center) + epsilon)
    return center * scale, scale


def fold_rows(v):
    total = v[0:8]
    for r in range(8, v.shape[0], 8):
        total = total + v[r : r + 8]
    return total


def masked_rows(meta, span, frames_ref, row0, rows):
    places = iota((rows, 1), 0) + row0
    hide_t = (places >= meta[1, span]) & (places < meta[1, span] + meta[2, span])
    columns = iota((1, D), 1)
    hide_f = (columns >= meta[3, span]) & (columns < meta[3, span] + meta[4, span])
    keep = jnp.where(hide_t, 0.0, 1.0) * jnp.where(hide_f, 0.0, 1.0)
    return frames_ref[pl.ds(row0, rows), :].astype(F32) * keep, keep


def load_slots(places, pieces, w_ref, sems, start):
    j = 0
    for piece in pieces:
        for i in range(piece.shape[0]):
            copy = pltpu.make_async_copy(
                piece.at[i],
                w_ref.at[
                    places[0, j], pl.ds(pl.multiple_of(places[1, j], 16), piece.shape[1]), :
                ],
                sems.at[j],
            )
            if start:
                copy.start()
            else:
                copy.wait()
            j += 1


def load_weights(places, pieces, w_ref, sems, start):
    if len(pieces) > 1 or pieces[0].shape != w_ref.shape:
        load_slots(places, pieces, w_ref, sems, start)
        return
    copy = pltpu.make_async_copy(pieces[0], w_ref, sems.at[0])
    if start:
        copy.start()
    else:
        copy.wait()


def vector_block(rows_of, wide, own_rows):
    blocks = D // own_rows
    r, c = iota((D, D), 0), iota((D, D), 1)
    value = jnp.zeros((D, D), F32)
    for i, vector in enumerate(rows_of):
        value = jnp.where(r % own_rows == i, vector, value)
    value = jnp.where(r // own_rows == c // own_rows, value, 0.0).astype(BF16)
    pick = jnp.where(iota((D, EXTRA), 0) % own_rows == iota((D, EXTRA), 1), 1.0, 0.0)
    block = dot(value, pick.astype(BF16))
    if wide is not None:
        width = wide.shape[1]
        share = width // blocks
        r, c = iota((D, width), 0), iota((D, width), 1)
        here = (r // own_rows == c // share) & (r % own_rows == len(rows_of))
        value = jnp.where(here, wide, 0.0).astype(BF16)
        pick = jnp.where(iota((width, EXTRA), 0) % share == iota((width, EXTRA), 1), 1.0, 0.0)
        block = block + dot(value, pick.astype(BF16))
    return block.astype(BF16)


def column_sum(v):
    return jnp.sum(v, axis=0, keepdims=True)


def split_core(core_bit, grad_ref, keeps, sends, width):
    blocks, part = keeps[0].shape[1], keeps[0].shape[2]
    rows = D // (2 * blocks)
    for outs, bit in ((keeps, core_bit), (sends, 1 - core_bit)):
        for i in range(blocks):
            first = pl.multiple_of((2 * i + bit) * rows, 16)
            for h, out in enumerate(outs):
                for g in range(GROUPS):
                    out[g, i, :, :width] = grad_ref[g, pl.ds(first + h * part, part), :width].astype(BF16)


def split_extra(core_bit, block_ref, keeps, sends, width):
    blocks, part = keeps[0].shape[1], keeps[0].shape[2]
    rows = D // (2 * blocks)
    for outs, bit in ((keeps, core_bit), (sends, 1 - core_bit)):
        for i in range(blocks):
            first = pl.multiple_of((2 * i + bit) * rows, 16)
            for h, out in enumerate(outs):
                for g in range(GROUPS):
                    value = block_ref[g, pl.ds(first + h * part, part), :]
                    out[g, i, :, width:] = value.astype(BF16)


def low_half():
    return iota((1, PAIR), 1) < HEAD_DIM


def attention_forward_kernel(first_span, count, tokens, meta, places, *refs):
    frames_ref, ctx_k_ref, ctx_v_ref, norm_ref = refs[:4]
    slots_ref, refs = refs[4 : 4 + count], refs[4 + count + tokens :]
    n1_ref, q_ref, k_ref, v_ref, att_ref, mid_ref = refs[:6]
    if first_span == 0:
        weights_out, refs = refs[6], refs[7:]
    else:
        refs = refs[6:]
    w_ref, sems, ke_ref, ko_ref, ve_ref, vo_ref, bias_ref, ones_ref = refs
    step = pl.program_id(0)
    span = meta[0, 0] + first_span + step

    @pl.when(step == 0)
    def _():
        load_weights(places, slots_ref, w_ref, sems, True)
        r, c = iota((96, 256), 0), iota((96, 256), 1) % 128
        bias_ref[...] = jnp.where((c >= r + 6) & (c <= r + 18), 0.0, NEGATIVE)
        r, c = iota((256, 128), 0), iota((256, 128), 1)
        ones_ref[...] = jnp.where((r < 128) == (c < 64), 1.0, 0.0).astype(BF16)

    for r0 in range(0, SPAN, 128):
        masked, _ = masked_rows(meta, span, frames_ref, r0, 128)
        xhat, _ = normalize(masked)
        n1_ref[r0 : r0 + 128, :] = (xhat * norm_ref[0:1, :] + norm_ref[1:2, :]).astype(BF16)

    @pl.when(step == 0)
    def _():
        load_weights(places, slots_ref, w_ref, sems, False)
        if first_span == 0:
            pltpu.make_async_copy(w_ref, weights_out, sems.at[0]).start()

    k_ref[0, 0:TOP, :] = ctx_k_ref[0]
    v_ref[0, 0:TOP, :] = ctx_v_ref[0]
    k_ref[0, TOP + SPAN :, :] = jnp.zeros((16, D), BF16)
    v_ref[0, TOP + SPAN :, :] = jnp.zeros((16, D), BF16)
    n1 = n1_ref[...]
    for g in range(GROUPS):
        cols = slice(g * EG, (g + 1) * EG)
        q_ref[:, cols] = (dot(n1, w_ref[g, :, 0:EG]) * HEAD_DIM**-0.5).astype(BF16)
        k_ref[0, TOP : TOP + SPAN, cols] = dot(n1, w_ref[g, :, EG : 2 * EG]).astype(BF16)
        v_ref[0, TOP : TOP + SPAN, cols] = dot(n1, w_ref[g, :, 2 * EG : 3 * EG]).astype(BF16)

    even = iota((1, D), 1) % PAIR < HEAD_DIM
    zero = jnp.zeros((), BF16)
    for r0, rows in ((0, 144), (144, 144), (288, 128), (416, 128)):
        kb, vb = k_ref[0, r0 : r0 + rows, :], v_ref[0, r0 : r0 + rows, :]
        ke_ref[r0 : r0 + rows, :] = jnp.where(even, kb, zero)
        ko_ref[r0 : r0 + rows, :] = jnp.where(even, zero, kb)
        ve_ref[r0 : r0 + rows, :] = jnp.where(even, vb, zero)
        vo_ref[r0 : r0 + rows, :] = jnp.where(even, zero, vb)

    first_key = TOP - meta[5, span]
    for j in range(PAIRS):
        lanes = slice(j * PAIR, (j + 1) * PAIR)
        for rows, q0, w0 in FORWARD_BLOCKS:
            window = slice(w0, w0 + 128)
            keys = jnp.concatenate([ke_ref[window, lanes], ko_ref[window, lanes]], axis=0)
            scores = dot_nt(q_ref[q0 : q0 + rows, lanes], keys)
            if q0 == 480:
                r, c = iota((rows, 256), 0), iota((rows, 256), 1) % 128 - 64
                bias = jnp.where((c >= r + 6) & (c <= r + 18) & (c < 48), 0.0, NEGATIVE)
            else:
                bias = bias_ref[...]
            scores = scores + bias
            if q0 == 0:
                scores = jnp.where(iota((rows, 256), 1) % 128 >= first_key, scores, NEGATIVE)
            expo = []
            for half in (scores[:, :128], scores[:, 128:]):
                top = jnp.max(half, axis=-1, keepdims=True)
                expo.append(jnp.exp(half - top).astype(BF16))
            values = jnp.concatenate([ve_ref[window, lanes], vo_ref[window, lanes]], axis=0)
            values = jnp.concatenate([values, ones_ref[...]], axis=1)
            mixed = dot(jnp.concatenate(expo, axis=1), values)
            att_ref[q0 : q0 + rows, lanes] = (mixed[:, :PAIR] / mixed[:, PAIR:]).astype(BF16)

    att = att_ref[...]
    mid_ref[...] = dot_nt(att[:, :EG], w_ref[0, :, 3 * EG :]) + dot_nt(
        att[:, EG:], w_ref[1, :, 3 * EG :]
    )
    for r0 in range(0, SPAN, 128):
        masked, _ = masked_rows(meta, span, frames_ref, r0, 128)
        mid_ref[r0 : r0 + 128, :] = mid_ref[r0 : r0 + 128, :] + masked

    if first_span == 0:
        @pl.when(step == 0)
        def _():
            pltpu.make_async_copy(w_ref, weights_out, sems.at[0]).wait()


def spec(block, index, **kw):
    return pl.BlockSpec(block, index, **kw)


def params():
    return pltpu.CompilerParams(
        dimension_semantics=("arbitrary",), vmem_limit_bytes=VMEM_LIMIT
    )


def cost(micros, size):
    return pl.CostEstimate(flops=int(micros * 1.1e9), bytes_accessed=size, transcendentals=0)


def slot_count(pieces):
    return sum(piece.shape[0] for piece in pieces)


def row_block():
    return spec((SPAN, D), lambda s, m, p: (s, 0))


def fixed(shape):
    return spec(shape, lambda s, m, p: (0,) * len(shape))


def struct(shape, dtype):
    return jax.ShapeDtypeStruct(shape, dtype)


def attention_forward(
    meta, places, frames, ctx_k, ctx_v, norm, pieces, tokens, first_span, spans
):
    rows = spans * SPAN
    keys_block = spec((1, KEYS, D), lambda s, m, p: (s, 0, 0))
    top_block = spec((1, TOP, D), lambda s, m, p: (first_span + s, 0, 0))
    return pl.pallas_call(
        functools.partial(attention_forward_kernel, first_span, len(pieces), len(tokens)),
        grid_spec=pltpu.PrefetchScalarGridSpec(
            num_scalar_prefetch=2,
            grid=(spans,),
            in_specs=[
                spec((SPAN, D), lambda s, m, p: (m[0, 0] + first_span + s, 0)),
                top_block,
                top_block,
                fixed((8, D)),
            ]
            + [pl.BlockSpec(memory_space=pl.ANY)] * (len(pieces) + len(tokens)),
            out_specs=[
                row_block(), row_block(), keys_block, keys_block, row_block(), row_block()
            ]
            + [pl.BlockSpec(memory_space=pl.ANY)] * (first_span == 0),
            scratch_shapes=[
                pltpu.VMEM((GROUPS, D, 4 * EG), BF16),
                pltpu.SemaphoreType.DMA((slot_count(pieces),)),
                pltpu.VMEM((KEYS, D), BF16),
                pltpu.VMEM((KEYS, D), BF16),
                pltpu.VMEM((KEYS, D), BF16),
                pltpu.VMEM((KEYS, D), BF16),
                pltpu.VMEM((96, 256), F32),
                pltpu.VMEM((256, 128), BF16),
            ],
        ),
        out_shape=[
            struct((rows, D), BF16),
            struct((rows, D), BF16),
            struct((spans, KEYS, D), BF16),
            struct((spans, KEYS, D), BF16),
            struct((rows, D), BF16),
            struct((rows, D), F32),
        ]
        + [struct((GROUPS, D, 4 * EG), BF16)] * (first_span == 0),
        compiler_params=params(),
        cost_estimate=cost(4.5 * spans, rows * D * 14),
        name="attention_forward",
    )(meta, places, frames, ctx_k, ctx_v, norm, *pieces, *tokens)


def feed_forward_kernel(first, last, parts, count, meta, places, *refs):
    mid_ref, cot_ref, att_ref, norm_ref, inner_b_ref = refs[:5]
    slots_ref, refs = refs[5 : 5 + count], refs[5 + count :]
    if not first:
        (_, before_ref, before_sums_ref, before_sums_b_ref), refs = refs[:4], refs[4:]
    (out_ref, chunk_ref, gm_ref), refs = refs[:3], refs[3:]
    if last:
        keeps, sends, refs = refs[:parts], refs[parts : 2 * parts], refs[2 * parts :]
    else:
        (grad_ref, left_sums_ref, left_sums_b_ref), refs = refs[:3], refs[3:]
        weights_out, refs = (refs[0], refs[1:]) if first else (None, refs)
    w_ref, sems, n2_ref, n2t_ref, cott_ref, hid_ref, gin_ref, dn_ref, acc_ref = refs[:9]
    sums_ref, sums_b_ref, refs = refs[9], refs[10], refs[11:]
    step = pl.program_id(0)

    @pl.when(step == 0)
    def _():
        load_weights(places, slots_ref, w_ref, sems, True)
        acc_ref[...] = jnp.zeros_like(acc_ref)
        if first:
            sums_ref[...] = jnp.zeros_like(sums_ref)
            sums_b_ref[...] = jnp.zeros_like(sums_b_ref)
        else:
            pltpu.make_async_copy(before_ref, refs[0], refs[1]).start()
            sums_ref[...] = before_sums_ref[...]
            sums_b_ref[...] = before_sums_b_ref[...]

    for r0 in range(0, SPAN, 128):
        xhat, _ = normalize(mid_ref[r0 : r0 + 128, :])
        n2_ref[r0 : r0 + 128, :] = (xhat * norm_ref[2:3, :] + norm_ref[3:4, :]).astype(BF16)
    n2t_ref[...] = n2_ref[...].T
    cott_ref[...] = cot_ref[...].T

    @pl.when(step == 0)
    def _():
        load_weights(places, slots_ref, w_ref, sems, False)
        if first and not last:
            pltpu.make_async_copy(w_ref, weights_out, sems.at[0]).start()

    chunk = 256
    for g in range(GROUPS):
        for c0 in range(0, FG, chunk):
            cols = slice(g * FG + c0, g * FG + c0 + chunk)
            act = dot(n2_ref[...], w_ref[g, :, c0 : c0 + chunk]) + inner_b_ref[0:1, cols]
            square = act * act
            tanh = jnp.tanh(act * (0.7978845608 + (0.7978845608 * 0.044715) * square))
            weight = 0.5 + 0.5 * tanh
            hidden = act * weight
            hid_ref[:, cols] = hidden.astype(BF16)
            slope = weight + (hidden - hidden * weight) * (
                2.0 * 0.7978845608 + (6.0 * 0.7978845608 * 0.044715) * square
            )
            grad = dot(cot_ref[...], w_ref[g, :, FG + c0 : FG + c0 + chunk]) * slope
            grad_low = grad.astype(BF16)
            gin_ref[:, cols] = grad_low
            sums_b_ref[:, cols] += fold_rows(grad_low.astype(F32))

    hid, gin = hid_ref, gin_ref
    out = (
        mid_ref[...]
        + dot_nt(hid[:, :FG], w_ref[0, :, FG:])
        + dot_nt(hid[:, FG:], w_ref[1, :, FG:])
        + norm_ref[4:5, :]
    ).astype(BF16)
    out_ref[...] = out
    chunk_ref[...] = out
    dn_ref[...] = dot_nt(gin[:, :FG], w_ref[0, :, :FG]) + dot_nt(gin[:, FG:], w_ref[1, :, :FG])
    for g in range(GROUPS):
        cols = slice(g * FG, (g + 1) * FG)
        acc_ref[g, :, :FG] += dot(n2t_ref[...], gin[:, cols])
        acc_ref[g, :, FG : 2 * FG] += dot(cott_ref[...], hid[:, cols])

    for r0 in range(0, SPAN, 128):
        rows = slice(r0, r0 + 128)
        xhat, scale = normalize(mid_ref[rows, :])
        grad = dn_ref[rows, :]
        cot = cot_ref[rows, :].astype(F32)
        sums_ref[0:8, :] += fold_rows(grad * xhat)
        sums_ref[8:16, :] += fold_rows(grad)
        sums_ref[16:24, :] += fold_rows(cot)
        t = grad * norm_ref[2:3, :]
        gm_ref[rows, :] = (cot + scale * (t - row_mean(t) - xhat * row_mean(t * xhat))).astype(BF16)

    for g in range(GROUPS):
        acc_ref[g, :, 2 * FG :] += dot_tn(gm_ref[...], att_ref[:, g * EG : (g + 1) * EG])

    @pl.when(step == pl.num_programs(0) - 1)
    def _():
        if first and not last:
            pltpu.make_async_copy(w_ref, weights_out, sems.at[0]).wait()
        if not first:
            pltpu.make_async_copy(before_ref, refs[0], refs[1]).wait()
            for g in range(GROUPS):
                acc_ref[g] += refs[0][g].astype(F32)
        if not last:
            for g in range(GROUPS):
                grad_ref[g] = acc_ref[g].astype(BF16)
            left_sums_ref[...] = sums_ref[...]
            left_sums_b_ref[...] = sums_b_ref[...]
        else:
            split_core(meta[0, 1], acc_ref, keeps, sends, FEED_WIDTH - EXTRA)
            vectors = [column_sum(sums_ref[8 * i : 8 * i + 8, :]) for i in range(3)]
            for g in range(GROUPS):
                wide = column_sum(sums_b_ref[:, g * FG : (g + 1) * FG])
                refs[-1][g] = vector_block(vectors, wide, 2 * 16).astype(F32)
            split_extra(meta[0, 1], refs[-1], keeps, sends, FEED_WIDTH - EXTRA)


FEED_WIDTH = 2 * FG + EG + EXTRA
ATTENTION_WIDTH = 3 * EG + EXTRA


def gradient_outs(parts, width):
    shape = (GROUPS, 8, D // 16 // parts, width)
    return [fixed(shape)] * (2 * parts), [struct(shape, BF16)] * (2 * parts)


def feed_forward(
    meta, places, mid, cot, att, norm, inner_b, pieces, before, first_span, spans, last, parts
):
    rows = spans * SPAN
    first = not before
    whole = pl.BlockSpec(memory_space=pl.ANY)
    whole_rows = spec((SPAN, D), lambda s, m, p: (m[0, 0] + first_span + s, 0))
    in_specs = [row_block(), whole_rows, row_block(), fixed((8, D)), fixed((1, FF))]
    in_specs += [whole] * len(pieces)
    args = [mid, cot, att, norm, inner_b, *pieces]
    aliases = {}
    scratch = [
        pltpu.VMEM((GROUPS, D, 2 * FG), BF16),
        pltpu.SemaphoreType.DMA((slot_count(pieces),)),
        pltpu.VMEM((SPAN, D), BF16),
        pltpu.VMEM((D, SPAN), BF16),
        pltpu.VMEM((D, SPAN), BF16),
        pltpu.VMEM((SPAN, FF), BF16),
        pltpu.VMEM((SPAN, FF), BF16),
        pltpu.VMEM((SPAN, D), F32),
        pltpu.VMEM((GROUPS, D, FEED_WIDTH - EXTRA), F32),
        pltpu.VMEM((24, D), F32),
        pltpu.VMEM((8, FF), F32),
    ]
    if not first:
        aliases = {2 + len(args): 0}
        in_specs += [whole, whole, fixed((24, D)), fixed((8, FF))]
        args += before
        scratch += [
            pltpu.VMEM((GROUPS, D, FEED_WIDTH - EXTRA), BF16), pltpu.SemaphoreType.DMA(())
        ]
    out_specs = [whole_rows, row_block(), row_block()]
    out_shape = [struct(cot.shape, BF16), struct((rows, D), BF16), struct((rows, D), BF16)]
    if last:
        more_specs, more_shapes = gradient_outs(parts, FEED_WIDTH)
        scratch += [pltpu.VMEM((GROUPS, D, EXTRA), F32)]
    else:
        shape = (GROUPS, D, FEED_WIDTH - EXTRA)
        more_specs = [fixed(shape), fixed((24, D)), fixed((8, FF))]
        more_shapes = [struct(shape, BF16), struct((24, D), F32), struct((8, FF), F32)]
        if first:
            more_specs += [whole]
            more_shapes += [struct((GROUPS, D, 2 * FG), BF16)]
    outs = pl.pallas_call(
        functools.partial(feed_forward_kernel, first, last, parts, len(pieces)),
        grid_spec=pltpu.PrefetchScalarGridSpec(
            num_scalar_prefetch=2,
            grid=(spans,),
            in_specs=in_specs,
            out_specs=out_specs + more_specs,
            scratch_shapes=scratch,
        ),
        out_shape=out_shape + more_shapes,
        input_output_aliases=aliases,
        compiler_params=params(),
        cost_estimate=cost(11 * spans, rows * D * 10),
        name="feed_forward",
    )(meta, places, *args)
    return outs[0], outs[1], outs[2], outs[3:]


def attention_backward_kernel(
    first, last, parts, first_span, meta, places, *refs
):
    frames_ref, n1_ref, q_ref, k_ref, v_ref, gm_ref, norm_ref, weights_ref = refs[:8]
    refs = refs[8:]
    if not first:
        (_, before_ref, before_sums_ref), refs = refs[:3], refs[3:]
    (gf_ref, chunk_ref, gctx_ref), refs = refs[:3], refs[3:]
    if last:
        keeps, sends, refs = refs[:parts], refs[parts : 2 * parts], refs[2 * parts :]
    else:
        (grad_ref, left_sums_ref), refs = refs[:2], refs[2:]
    w_ref, sems, gatt_ref, dq_ref, dk_ref, dv_ref, dkb_ref, dvb_ref = refs[:8]
    n1t_ref, dn_ref, bias_ref, acc_ref, sums_ref = refs[8:13]
    refs = refs[13:]
    step = pl.program_id(0)
    span = meta[0, 0] + first_span + step

    @pl.when(step == 0)
    def _():
        load_weights(places, [weights_ref], w_ref, sems, True)
        acc_ref[...] = jnp.zeros_like(acc_ref)
        if first:
            sums_ref[...] = jnp.zeros_like(sums_ref)
        else:
            pltpu.make_async_copy(before_ref, refs[0], refs[1]).start()
            sums_ref[...] = before_sums_ref[...]
        r, c = iota((160, 256), 0), iota((160, 256), 1) % 128
        bias_ref[...] = jnp.where((r >= c + 6) & (r <= c + 18), 0.0, NEGATIVE)

    n1t_ref[...] = n1_ref[...].T

    @pl.when(step == 0)
    def _():
        load_weights(places, [weights_ref], w_ref, sems, False)

    for g in range(GROUPS):
        gatt_ref[:, g * EG : (g + 1) * EG] = dot(gm_ref[...], w_ref[g, :, 3 * EG :]).astype(BF16)

    first_key = TOP - meta[5, span]
    even = low_half()
    zero = jnp.zeros((), BF16)
    for j in range(PAIRS):
        lanes = slice(j * PAIR, (j + 1) * PAIR)
        for b in range(SPAN // 128):
            rows, window = slice(128 * b, 128 * b + 128), slice(128 * b, 128 * b + 160)
            kw, vw = k_ref[0, window, lanes], v_ref[0, window, lanes]
            qb, ob = q_ref[rows, lanes], gatt_ref[rows, lanes]
            qs = jnp.concatenate([jnp.where(even, qb, zero), jnp.where(even, zero, qb)], axis=0)
            os = jnp.concatenate([jnp.where(even, ob, zero), jnp.where(even, zero, ob)], axis=0)
            scores = dot_nt(kw, qs) + bias_ref[...]
            if b == 0:
                scores = jnp.where(iota((160, 256), 0) >= first_key, scores, NEGATIVE)
            if b == SPAN // 128 - 1:
                scores = jnp.where(iota((160, 256), 0) < 144, scores, NEGATIVE)
            expo = jnp.exp(scores - jnp.max(scores, axis=0, keepdims=True))
            probs = expo * (1.0 / jnp.sum(expo, axis=0, keepdims=True))
            grad_probs = dot_nt(vw, os)
            delta = jnp.sum(probs * grad_probs, axis=0, keepdims=True)
            ds = (probs * (grad_probs - delta)).astype(BF16)
            dv = dot(probs.astype(BF16), os)
            dk = dot(ds, qs)
            if b == 0:
                dkb_ref[window, lanes] = dk
                dvb_ref[window, lanes] = dv
            else:
                lap, rest = slice(128 * b, 128 * b + 32), slice(128 * b + 32, 128 * b + 160)
                dkb_ref[lap, lanes] += dk[:32]
                dvb_ref[lap, lanes] += dv[:32]
                dkb_ref[rest, lanes] = dk[32:]
                dvb_ref[rest, lanes] = dv[32:]
            dq = dot_tn(ds, kw)
            dq = jnp.where(even, dq[:128], dq[128:]) * HEAD_DIM**-0.5
            dq_ref[rows, lanes] = dq.astype(BF16)
    for g in range(GROUPS):
        gctx_ref[g, 0, 0] = dkb_ref[0:TOP, g * EG : (g + 1) * EG]
        gctx_ref[g, 1, 0] = dvb_ref[0:TOP, g * EG : (g + 1) * EG]
    dk_ref[...] = dkb_ref[TOP : TOP + SPAN, :].astype(BF16)
    dv_ref[...] = dvb_ref[TOP : TOP + SPAN, :].astype(BF16)

    for g in range(GROUPS):
        cols = slice(g * EG, (g + 1) * EG)
        acc_ref[g, :, 0:EG] += dot(n1t_ref[...], dq_ref[:, cols])
        acc_ref[g, :, EG : 2 * EG] += dot(n1t_ref[...], dk_ref[:, cols])
        acc_ref[g, :, 2 * EG : 3 * EG] += dot(n1t_ref[...], dv_ref[:, cols])
    total = None
    for g in range(GROUPS):
        cols = slice(g * EG, (g + 1) * EG)
        for m, ref in enumerate((dq_ref, dk_ref, dv_ref)):
            term = dot_nt(ref[:, cols], w_ref[g, :, m * EG : (m + 1) * EG])
            total = term if total is None else total + term
    dn_ref[...] = total
    for r0 in range(0, SPAN, 128):
        rows = slice(r0, r0 + 128)
        masked, keep = masked_rows(meta, span, frames_ref, r0, 128)
        xhat, scale = normalize(masked)
        grad = dn_ref[rows, :]
        sums_ref[0:8, :] += fold_rows(grad * xhat)
        sums_ref[8:16, :] += fold_rows(grad)
        t = grad * norm_ref[0:1, :]
        back = scale * (t - row_mean(t) - xhat * row_mean(t * xhat))
        result = ((gm_ref[rows, :].astype(F32) + back) * keep).astype(BF16)
        gf_ref[rows, :] = result
        chunk_ref[rows, :] = result

    @pl.when(step == pl.num_programs(0) - 1)
    def _():
        if not first:
            pltpu.make_async_copy(before_ref, refs[0], refs[1]).wait()
            for g in range(GROUPS):
                acc_ref[g] += refs[0][g].astype(F32)
        if not last:
            for g in range(GROUPS):
                grad_ref[g] = acc_ref[g].astype(BF16)
            left_sums_ref[...] = sums_ref[...]
        else:
            split_core(meta[0, 1], acc_ref, keeps, sends, 3 * EG)
            vectors = [column_sum(sums_ref[8 * i : 8 * i + 8, :]) for i in range(2)]
            block = vector_block(vectors, None, 2 * 16).astype(F32)
            for g in range(GROUPS):
                refs[-1][g] = block
            split_extra(meta[0, 1], refs[-1], keeps, sends, 3 * EG)


def attention_backward(
    meta, places, frames, kept, gm, norm, weights, before, first_span, spans, last, parts
):
    rows = spans * SPAN
    first = not before
    whole = pl.BlockSpec(memory_space=pl.ANY)
    whole_rows = spec((SPAN, D), lambda s, m, p: (m[0, 0] + first_span + s, 0))
    keys_block = spec((1, KEYS, D), lambda s, m, p: (s, 0, 0))
    low = pltpu.VMEM((SPAN, D), BF16)
    in_specs = [
        whole_rows, row_block(), row_block(), keys_block, keys_block, row_block(), fixed((8, D)),
        whole,
    ]
    args = [frames, *kept, gm, norm, weights]
    aliases = {}
    scratch = [
        pltpu.VMEM((GROUPS, D, 4 * EG), BF16),
        pltpu.SemaphoreType.DMA((1,)),
        low,
        low,
        low,
        low,
        pltpu.VMEM((KEYS, D), F32),
        pltpu.VMEM((KEYS, D), F32),
        low,
        pltpu.VMEM((SPAN, D), F32),
        pltpu.VMEM((160, 256), F32),
        pltpu.VMEM((GROUPS, D, 3 * EG), F32),
        pltpu.VMEM((16, D), F32),
    ]
    if not first:
        aliases = {2 + len(args): 0}
        in_specs += [whole, whole, fixed((16, D))]
        args += before
        scratch += [pltpu.VMEM((GROUPS, D, 3 * EG), BF16), pltpu.SemaphoreType.DMA(())]
    out_specs = [
        whole_rows,
        row_block(),
        spec((GROUPS, 2, 1, TOP, EG), lambda s, m, p: (0, 0, s, 0, 0)),
    ]
    out_shape = [
        struct(frames.shape, BF16),
        struct((rows, D), BF16),
        struct((GROUPS, 2, spans, TOP, EG), F32),
    ]
    if last:
        more_specs, more_shapes = gradient_outs(parts, ATTENTION_WIDTH)
        scratch += [pltpu.VMEM((GROUPS, D, EXTRA), F32)]
    else:
        more_specs = [fixed((GROUPS, D, 3 * EG)), fixed((16, D))]
        more_shapes = [struct((GROUPS, D, 3 * EG), BF16), struct((16, D), F32)]
    outs = pl.pallas_call(
        functools.partial(attention_backward_kernel, first, last, parts, first_span),
        grid_spec=pltpu.PrefetchScalarGridSpec(
            num_scalar_prefetch=2,
            grid=(spans,),
            in_specs=in_specs,
            out_specs=out_specs + more_specs,
            scratch_shapes=scratch,
        ),
        out_shape=out_shape + more_shapes,
        input_output_aliases=aliases,
        compiler_params=params(),
        cost_estimate=cost(10 * spans, rows * D * 14),
        name="attention_backward",
    )(meta, places, *args)
    return outs[0], outs[1], outs[2], outs[3:]


BITS = {"core": ("dp", 1), "y": ("dp", 2), "z1": ("dp", 4), "z2": ("dp", 8), "x": ("tensor", 1)}
BIT_DIM = {"x": 0, "z2": 1, "z1": 2, "y": 3}


def swap(value, bit):
    axis, distance = BITS[bit]
    count = lax.axis_size(axis)
    return lax.ppermute(value, axis, [(i, i ^ distance) for i in range(count)])


def my_bit(bit):
    axis, distance = BITS[bit]
    return (lax.axis_index(axis) // distance) % 2


def tie(value, *tokens):
    return lax.optimization_barrier((value, tokens))[0]


def piece_places(order, rows, first):
    groups, firsts = [], []
    dp, tensor = lax.axis_index("dp"), lax.axis_index("tensor")
    for j in range(2 ** len(order)):
        dp_flip = sum(BITS[b][1] for i, b in enumerate(order) if j >> i & 1 and b != "x")
        x_flip = sum(1 for i, b in enumerate(order) if j >> i & 1 and b == "x")
        groups.append(tensor ^ x_flip)
        firsts.append((dp ^ dp_flip) * rows + first)
    return jnp.stack([jnp.stack(groups), jnp.stack(firsts)]).astype(jnp.int32)


class Gather:
    def __init__(self, piece, shared, orders):
        self.shared, self.orders = shared, orders
        self.rows = piece.shape[0]
        self.part = self.rows // len(orders)
        self.held = [piece[None]]
        self.got = None
        self.step = 0
        self.steps = len(shared) + len(orders[0])

    def after(self, *tokens):
        if self.got is None:
            self.held = list(tie(tuple(self.held), *tokens))
        else:
            self.got = list(tie(tuple(self.got), *tokens))

    def exchange(self):
        if self.got is not None:
            self.held = [jnp.concatenate(pair, axis=0) for pair in zip(self.held, self.got)]
        if self.step < len(self.shared):
            bits = [self.shared[self.step]]
        else:
            if self.step == len(self.shared):
                whole = self.held[0]
                self.held = [
                    whole[:, h * self.part : (h + 1) * self.part] for h in range(len(self.orders))
                ]
            bits = [order[self.step - len(self.shared)] for order in self.orders]
        self.got = [swap(held, bit) for held, bit in zip(self.held, bits)]
        self.step += 1

    def result(self):
        return [array for pair in zip(self.held, self.got) for array in pair]

    def places(self):
        return jnp.concatenate(
            [
                piece_places(self.shared + order, self.rows, h * self.part)
                for h, order in enumerate(self.orders)
            ],
            axis=1,
        )


class Scatter:
    def __init__(self, keeps_sends, orders):
        parts = len(orders)
        self.orders = orders
        self.rows, self.columns = keeps_sends[0].shape[2:]
        shape = (2, 2, 2, 2, self.rows, self.columns)
        self.keeps = [keep.reshape(shape) for keep in keeps_sends[:parts]]
        self.gots = [swap(send, "core").reshape(shape) for send in keeps_sends[parts:]]
        self.step = 0

    def after(self, *tokens):
        self.gots = list(tie(tuple(self.gots), *tokens))

    def exchange(self):
        for h, order in enumerate(self.orders):
            bit = order[self.step]
            dim, mine = BIT_DIM[bit], my_bit(bit)
            halves = []
            for place in (1 - mine, mine):
                total = sum(
                    lax.dynamic_index_in_dim(v, place, dim, keepdims=True).astype(F32)
                    for v in (self.keeps[h], self.gots[h])
                )
                halves.append(total.astype(BF16))
            self.keeps[h], self.gots[h] = halves[1], swap(halves[0], bit)
        self.step += 1

    def result(self):
        while self.step < len(self.orders[0]):
            self.exchange()
        return jnp.concatenate(
            [
                (keep.astype(F32) + got.astype(F32)).reshape(self.rows, self.columns)
                for keep, got in zip(self.keeps, self.gots)
            ],
            axis=0,
        )


SHARED_ORDER = ("z2", "z1")
ATTENTION_ORDERS = (("y", "x", "core"), ("x", "y", "core"))
FEED_ORDERS = (("y", "x", "core"), ("x", "y", "core"))
ATTENTION_SUMS = (("y", "z1", "z2", "x"), ("z1", "z2", "y", "x"))
FEED_SUMS = (("y", "z1", "z2", "x"), ("z1", "z2", "y", "x"))


def body(
    frames,
    context_keys,
    context_values,
    time_start,
    time_width,
    freq_start,
    freq_width,
    context_count,
    gain_one,
    shift_one,
    query_w,
    key_w,
    value_w,
    out_w,
    gain_two,
    shift_two,
    inner_w,
    inner_b,
    outer_w,
    outer_b,
    cotangent,
):
    tensor, dp = lax.axis_size("tensor"), lax.axis_size("dp")
    tuned = tensor == 2 and dp == 16
    spans = time_start.shape[0] // tensor
    t_index = lax.axis_index("tensor")
    base = t_index * spans

    def pick(first, second):
        return jnp.where(t_index == 0, first, second)

    attention_piece = jnp.concatenate([query_w, key_w, value_w, out_w.T], axis=1)
    feed_piece = jnp.concatenate([inner_w, outer_w.T], axis=1)
    context = jnp.stack([context_keys, context_values])
    if tuned:
        gather = Gather(attention_piece, SHARED_ORDER, ATTENTION_ORDERS)
        feed_gather = Gather(feed_piece, SHARED_ORDER, FEED_ORDERS)
        gather.exchange()
        context, inner_b = tie((context, inner_b), *gather.got)
        mine = lax.dynamic_slice_in_dim(context, base, spans, 1)
        theirs = swap(lax.dynamic_slice_in_dim(context, (1 - t_index) * spans, spans, 1), "x")
        context = pick(
            jnp.concatenate([mine, theirs], axis=3), jnp.concatenate([theirs, mine], axis=3)
        )
        other_b = swap(inner_b, "x")
        inner_b_full = pick(
            jnp.concatenate([inner_b, other_b]), jnp.concatenate([other_b, inner_b])
        ).reshape(1, FF)
        gather.exchange()
        feed_gather.after(*gather.got)
        feed_gather.exchange()
        gather.exchange()
        gather.exchange()
        gather.exchange()
        feed_gather.exchange()
        feed_gather.exchange()
        attention_pieces, attention_places = gather.result(), gather.places()
        feed_places = feed_gather.places()
    else:
        def canonical(parts, width):
            grouped = []
            for part in parts:
                whole = lax.all_gather(part, "dp", axis=0, tiled=True)
                whole = lax.all_gather(whole, "tensor", axis=1, tiled=True)
                grouped.append(whole.reshape(D, GROUPS, width).swapaxes(0, 1))
            return [jnp.concatenate(grouped, axis=2)]

        attention_pieces = canonical((query_w, key_w, value_w, out_w.T), EG)
        feed_pieces = canonical((inner_w, outer_w.T), FG)
        attention_places = feed_places = jnp.array([[0, 1], [0, 0]], jnp.int32)
        context = lax.all_to_all(context, "tensor", split_axis=1, concat_axis=3, tiled=True)
        inner_b_full = lax.all_gather(inner_b, "tensor", axis=0, tiled=True).reshape(1, FF)
    context = jnp.pad(context, ((0, 0), (0, 0), (TOP - LEFT, 0), (0, 0)))

    core_bit = my_bit("core") if tuned else 0
    first_row = jnp.zeros_like(time_start).at[0].set(base).at[1].set(core_bit)
    meta = jnp.stack(
        [first_row, time_start, time_width, freq_start, freq_width, context_count]
    ).astype(jnp.int32)
    norm = jnp.stack(
        [gain_one, shift_one, gain_two, shift_two, outer_b] + [jnp.zeros_like(gain_one)] * 3
    )

    chunk = min(CHUNK, spans)
    firsts = range(0, spans, chunk)
    final = spans - chunk

    def exchange(value):
        return swap(value, "x") if tuned else value

    weights = None
    kept = []
    if tuned:
        meta = tie(meta, inner_b_full, attention_places, feed_places)
    for first in firsts:
        pieces = attention_pieces if weights is None else [weights]
        saved = attention_forward(
            meta, attention_places, frames, context[0], context[1], norm, pieces, [], first, chunk
        )
        weights = saved[6] if first == 0 else weights
        kept.append(saved[:6])
        if tuned and feed_gather.step < feed_gather.steps:
            feed_gather.after(saved[0])
            feed_gather.exchange()
    if tuned:
        while feed_gather.step < feed_gather.steps:
            feed_gather.exchange()
        feed_pieces = feed_gather.result()

    outs, gms, before, feed_weights = [], [], [], None
    parts = len(FEED_SUMS) if tuned else 1
    for first, saved in zip(firsts, kept):
        pieces = feed_pieces if feed_weights is None else [feed_weights]
        output, part, gm, rest = feed_forward(
            meta, feed_places, saved[5], cotangent, saved[4], norm, inner_b_full, pieces, before,
            first, chunk, first == final, parts,
        )
        if first == 0 and first != final:
            *rest, feed_weights = rest
        outs.append(exchange(part))
        gms.append(gm)
        before = [output, *rest]
    feed_grad = rest
    frame_parts, contexts, before = [], [], []
    parts = len(ATTENTION_SUMS) if tuned else 1
    if tuned:
        feed_grad = list(tie(tuple(feed_grad), outs[0]))
        feed_scatter = Scatter(feed_grad, FEED_SUMS)
        feed_scatter.exchange()
    for index, (first, saved, gm) in enumerate(zip(firsts, kept, gms)):
        own_meta = meta
        if tuned:
            own_meta = tie(meta, *feed_scatter.keeps, *(outs[-1:] if index > 0 else []))
        grad_frames, part, gctx, rest = attention_backward(
            own_meta, attention_places, frames, saved[:4], gm, norm, weights, before, first, chunk,
            first == final, parts,
        )
        frame_parts.append(exchange(part))
        contexts.append(gctx)
        before = [grad_frames, *rest]
        if tuned and index == 0:
            feed_scatter.after(grad_frames)
            feed_scatter.exchange()
    attention_grad = rest
    if tuned:
        attention_grad = list(tie(tuple(attention_grad), frame_parts[0], *feed_scatter.gots))
        attention_scatter = Scatter(attention_grad, ATTENTION_SUMS)
        output, grad_frames = tie((output, grad_frames), *attention_scatter.gots)
        feed_scatter.exchange()
        attention_scatter.after(*feed_scatter.keeps)
        attention_scatter.exchange()
        attention_scatter.exchange()
        attention_scatter.exchange()
        attention_scatter.gots, feed_scatter.gots, frame_parts[-1], contexts = tie(
            (attention_scatter.gots, feed_scatter.gots, frame_parts[-1], contexts)
        )


    if tuned:
        def both(whole, parts):
            for first, part in zip(firsts, parts):
                place = ((1 - t_index) * spans + first) * SPAN
                whole = lax.dynamic_update_slice_in_dim(whole, part, place, 0)
            return whole

        output = both(output, outs)
        grad_frames = both(grad_frames, frame_parts)
        gctx = jnp.concatenate(contexts, axis=2)[:, :, :, TOP - LEFT :]
        mine, theirs = (
            lax.dynamic_index_in_dim(gctx, place, 0, keepdims=False)
            for place in (t_index, 1 - t_index)
        )
        theirs = swap(theirs, "x")
        grad_context = pick(
            jnp.concatenate([mine, theirs], axis=1), jnp.concatenate([theirs, mine], axis=1)
        )
        feed_sum = feed_scatter.result()
        attention_sum = attention_scatter.result()
        extra = feed_sum[:4, FEED_WIDTH - EXTRA :]
        sum_gain_two, sum_shift_two, sum_outer_b = (extra[i, :32] for i in range(3))
        sum_inner_b = extra[3, :64]
        sum_gain_one, sum_shift_one = (
            attention_sum[i, 3 * EG : 3 * EG + 32] for i in range(2)
        )
        sum_query, sum_key, sum_value = (
            attention_sum[:, i * EG : (i + 1) * EG] for i in range(3)
        )
        sum_inner, sum_outer = feed_sum[:, :FG], feed_sum[:, FG : 2 * FG]
        sum_out = feed_sum[:, 2 * FG : 2 * FG + EG]
    else:
        def both(parts):
            return lax.all_gather(jnp.concatenate(parts, axis=0), "tensor", axis=0, tiled=True)

        output = both(outs)
        grad_frames = both(frame_parts)
        gctx = jnp.concatenate(contexts, axis=2)[:, :, :, TOP - LEFT :]
        grad_context = jnp.moveaxis(gctx, 0, 3).reshape(2, spans, LEFT, D)
        grad_context = lax.all_to_all(
            grad_context, "tensor", split_axis=3, concat_axis=1, tiled=True
        )
        attention_grad, feed_grad = (
            jnp.stack(pair, axis=2).reshape(GROUPS, D, -1) for pair in (attention_grad, feed_grad)
        )

        def whole_grad(grad, index, width):
            return grad[:, :, index * width : (index + 1) * width].swapaxes(0, 1).reshape(D, -1)

        def scattered(grad):
            part = lax.psum_scatter(grad, "dp", scatter_dimension=0, tiled=True)
            return lax.psum_scatter(part, "tensor", scatter_dimension=1, tiled=True).astype(F32)

        def summed(item):
            item = lax.psum(item, "tensor")
            return lax.psum_scatter(item, "dp", scatter_dimension=0, tiled=True)

        def vector(grad, index):
            item = grad[0, :, -EXTRA:].reshape(16, 32, EXTRA)[:, index, :32].reshape(D)
            return summed(item.astype(F32))

        sum_query, sum_key, sum_value = (
            scattered(whole_grad(attention_grad, i, EG)) for i in range(3)
        )
        sum_inner, sum_outer = (scattered(whole_grad(feed_grad, i, FG)) for i in range(2))
        sum_out = scattered(feed_grad[:, :, 2 * FG : 2 * FG + EG].swapaxes(0, 1).reshape(D, -1))
        sum_gain_one, sum_shift_one = (vector(attention_grad, i) for i in range(2))
        sum_gain_two, sum_shift_two, sum_outer_b = (vector(feed_grad, i) for i in range(3))
        sum_inner_b = feed_grad[:, :, -EXTRA:].reshape(GROUPS, 16, 32, EXTRA)[:, :, 3, :64]
        sum_inner_b = sum_inner_b.reshape(FF).astype(F32)
        sum_inner_b = lax.psum_scatter(sum_inner_b, "tensor", scatter_dimension=0, tiled=True)
        sum_inner_b = lax.psum_scatter(sum_inner_b, "dp", scatter_dimension=0, tiled=True)

    return (
        output,
        grad_frames,
        grad_context[0],
        grad_context[1],
        sum_gain_one,
        sum_shift_one,
        sum_query,
        sum_key,
        sum_value,
        sum_out.T,
        sum_gain_two,
        sum_shift_two,
        sum_inner,
        sum_inner_b,
        sum_outer.T,
        sum_outer_b,
    )


def solution(mesh):
    in_specs = (
        P("dp", None),
        P("dp", None, "tensor"),
        P("dp", None, "tensor"),
        P("dp"),
        P("dp"),
        P("dp"),
        P("dp"),
        P("dp"),
        P(),
        P(),
        P("dp", "tensor"),
        P("dp", "tensor"),
        P("dp", "tensor"),
        P("tensor", "dp"),
        P(),
        P(),
        P("dp", "tensor"),
        P("tensor"),
        P("tensor", "dp"),
        P(),
        P("dp", None),
    )
    out_specs = (
        P("dp", None),
        P("dp", None),
        P("dp", None, "tensor"),
        P("dp", None, "tensor"),
        P("dp"),
        P("dp"),
        P("dp", "tensor"),
        P("dp", "tensor"),
        P("dp", "tensor"),
        P("tensor", "dp"),
        P("dp"),
        P("dp"),
        P("dp", "tensor"),
        P(("tensor", "dp")),
        P("tensor", "dp"),
        P("dp"),
    )
    return jax.shard_map(body, mesh=mesh, in_specs=in_specs, out_specs=out_specs, check_vma=False)
```

```python
import functools

import jax
import jax.numpy as jnp
from jax import lax
from jax.experimental import pallas as pl
from jax.experimental.pallas import tpu as pltpu
from jax.sharding import PartitionSpec as P

D = 512
HEAD_DIM = 64
SPAN = 512
LEFT = 10
RIGHT = 2
FF = 2048
PAIR = 2 * HEAD_DIM
PAIRS = D // PAIR
GROUPS = 2
EG = D // GROUPS
FG = FF // GROUPS
TOP = 16
KEYS = TOP + SPAN + 16
EXTRA = 128
CHUNK = 2
NEGATIVE = -1e30
epsilon = 1e-05
F32 = jnp.float32
BF16 = jnp.bfloat16
VMEM_LIMIT = 56 * 1024 * 1024
FORWARD_BLOCKS = tuple((96, 96 * b, 96 * b) for b in range(5)) + ((32, 480, 416),)


def dot(a, b):
    return lax.dot_general(a, b, (((1,), (0,)), ((), ())), preferred_element_type=F32)


def dot_nt(a, b):
    return lax.dot_general(a, b, (((1,), (1,)), ((), ())), preferred_element_type=F32)


def dot_tn(a, b):
    return lax.dot_general(a, b, (((0,), (0,)), ((), ())), preferred_element_type=F32)


def iota(shape, dim):
    return lax.broadcasted_iota(jnp.int32, shape, dim)


def row_mean(v):
    return jnp.sum(v, axis=-1, keepdims=True) * (1.0 / D)


def normalize(v):
    center = v - row_mean(v)
    scale = lax.rsqrt(row_mean(center * center) + epsilon)
    return center * scale, scale


def fold_rows(v):
    total = v[0:8]
    for r in range(8, v.shape[0], 8):
        total = total + v[r : r + 8]
    return total


def masked_rows(meta, span, frames_ref, row0, rows):
    places = iota((rows, 1), 0) + row0
    hide_t = (places >= meta[1, span]) & (places < meta[1, span] + meta[2, span])
    columns = iota((1, D), 1)
    hide_f = (columns >= meta[3, span]) & (columns < meta[3, span] + meta[4, span])
    keep = jnp.where(hide_t, 0.0, 1.0) * jnp.where(hide_f, 0.0, 1.0)
    return frames_ref[pl.ds(row0, rows), :].astype(F32) * keep, keep


def load_slots(places, pieces, w_ref, sems, start):
    j = 0
    for piece in pieces:
        for i in range(piece.shape[0]):
            copy = pltpu.make_async_copy(
                piece.at[i],
                w_ref.at[
                    places[0, j], pl.ds(pl.multiple_of(places[1, j], 16), piece.shape[1]), :
                ],
                sems.at[j],
            )
            if start:
                copy.start()
            else:
                copy.wait()
            j += 1


def load_weights(places, pieces, w_ref, sems, start):
    if len(pieces) > 1 or pieces[0].shape != w_ref.shape:
        load_slots(places, pieces, w_ref, sems, start)
        return
    copy = pltpu.make_async_copy(pieces[0], w_ref, sems.at[0])
    if start:
        copy.start()
    else:
        copy.wait()


def vector_block(rows_of, wide, own_rows):
    blocks = D // own_rows
    r, c = iota((D, D), 0), iota((D, D), 1)
    value = jnp.zeros((D, D), F32)
    for i, vector in enumerate(rows_of):
        value = jnp.where(r % own_rows == i, vector, value)
    value = jnp.where(r // own_rows == c // own_rows, value, 0.0).astype(BF16)
    pick = jnp.where(iota((D, EXTRA), 0) % own_rows == iota((D, EXTRA), 1), 1.0, 0.0)
    block = dot(value, pick.astype(BF16))
    if wide is not None:
        width = wide.shape[1]
        share = width // blocks
        r, c = iota((D, width), 0), iota((D, width), 1)
        here = (r // own_rows == c // share) & (r % own_rows == len(rows_of))
        value = jnp.where(here, wide, 0.0).astype(BF16)
        pick = jnp.where(iota((width, EXTRA), 0) % share == iota((width, EXTRA), 1), 1.0, 0.0)
        block = block + dot(value, pick.astype(BF16))
    return block.astype(BF16)


def column_sum(v):
    return jnp.sum(v, axis=0, keepdims=True)


def split_core(core_bit, grad_ref, keeps, sends, width):
    blocks, part = keeps[0].shape[1], keeps[0].shape[2]
    rows = D // (2 * blocks)
    for outs, bit in ((keeps, core_bit), (sends, 1 - core_bit)):
        for i in range(blocks):
            first = pl.multiple_of((2 * i + bit) * rows, 16)
            for h, out in enumerate(outs):
                for g in range(GROUPS):
                    out[g, i, :, :width] = grad_ref[g, pl.ds(first + h * part, part), :width].astype(BF16)


def split_extra(core_bit, block_ref, keeps, sends, width):
    blocks, part = keeps[0].shape[1], keeps[0].shape[2]
    rows = D // (2 * blocks)
    for outs, bit in ((keeps, core_bit), (sends, 1 - core_bit)):
        for i in range(blocks):
            first = pl.multiple_of((2 * i + bit) * rows, 16)
            for h, out in enumerate(outs):
                for g in range(GROUPS):
                    value = block_ref[g, pl.ds(first + h * part, part), :]
                    out[g, i, :, width:] = value.astype(BF16)


class GradientStore:
    def __init__(self, last, core_bit, held, outs, sems):
        self.last, self.core_bit, self.held, self.outs, self.sems = last, core_bit, held, outs, sems
        self.jobs = []

    def copies(self, number, columns):
        for g, _, target, width in columns:
            cols = pl.ds(target, width)
            if not self.last:
                yield pltpu.make_async_copy(
                    self.held[0].at[g, :, cols], self.outs[0].at[g, :, cols],
                    self.sems.at[number, 0, 0, g],
                )
                continue
            parts = len(self.held)
            for h, held in enumerate(self.held):
                for side in range(2):
                    yield pltpu.make_async_copy(
                        held.at[side, g, :, :, cols],
                        self.outs[h + side * parts].at[g, :, :, cols],
                        self.sems.at[number, h, side, g],
                    )

    def put(self, result_ref, columns):
        for g, source, target, width in columns:
            if not self.last:
                self.held[0][g, :, target : target + width] = result_ref[
                    :, source : source + width
                ].astype(BF16)
                continue
            for h, held in enumerate(self.held):
                blocks, part = held.shape[2], held.shape[3]
                rows = D // (2 * blocks)
                for side, bit in ((0, self.core_bit), (1, 1 - self.core_bit)):
                    for i in range(blocks):
                        first = pl.multiple_of((2 * i + bit) * rows + h * part, 16)
                        held[side, g, i, :, target : target + width] = result_ref[
                            pl.ds(first, part), source : source + width
                        ].astype(BF16)
        number = len(self.jobs)
        self.jobs.append(columns)
        for copy in self.copies(number, columns):
            copy.start()

    def finish(self):
        for number, columns in enumerate(self.jobs):
            for copy in self.copies(number, columns):
                copy.wait()


def gradient_buffers(last, parts, width, jobs):
    if not last:
        shapes = [struct((GROUPS, D, width), BF16)]
        held = [pltpu.VMEM((GROUPS, D, width), BF16)]
    else:
        part = D // 16 // parts
        shapes = [struct((GROUPS, 8, part, width), BF16)] * (2 * parts)
        held = [pltpu.VMEM((2, GROUPS, 8, part, width), BF16)] * parts
    sems = pltpu.SemaphoreType.DMA((jobs, parts if last else 1, 2, GROUPS))
    return held, sems, shapes


def low_half():
    return iota((1, PAIR), 1) < HEAD_DIM


def attention_forward_kernel(first_span, count, tokens, meta, places, *refs):
    frames_ref, ctx_k_ref, ctx_v_ref, norm_ref = refs[:4]
    slots_ref, refs = refs[4 : 4 + count], refs[4 + count + tokens :]
    n1_ref, q_ref, k_ref, v_ref, att_ref, mid_ref = refs[:6]
    if first_span == 0:
        weights_out, refs = refs[6], refs[7:]
    else:
        refs = refs[6:]
    w_ref, sems, ke_ref, ko_ref, ve_ref, vo_ref, bias_ref, ones_ref = refs
    step = pl.program_id(0)
    span = meta[0, 0] + first_span + step

    @pl.when(step == 0)
    def _():
        load_weights(places, slots_ref, w_ref, sems, True)
        r, c = iota((96, 256), 0), iota((96, 256), 1) % 128
        bias_ref[...] = jnp.where((c >= r + 6) & (c <= r + 18), 0.0, NEGATIVE)
        r, c = iota((256, 128), 0), iota((256, 128), 1)
        ones_ref[...] = jnp.where((r < 128) == (c < 64), 1.0, 0.0).astype(BF16)

    for r0 in range(0, SPAN, 128):
        masked, _ = masked_rows(meta, span, frames_ref, r0, 128)
        xhat, _ = normalize(masked)
        n1_ref[r0 : r0 + 128, :] = (xhat * norm_ref[0:1, :] + norm_ref[1:2, :]).astype(BF16)

    @pl.when(step == 0)
    def _():
        load_weights(places, slots_ref, w_ref, sems, False)
        if first_span == 0:
            pltpu.make_async_copy(w_ref, weights_out, sems.at[0]).start()

    k_ref[0, 0:TOP, :] = ctx_k_ref[0]
    v_ref[0, 0:TOP, :] = ctx_v_ref[0]
    k_ref[0, TOP + SPAN :, :] = jnp.zeros((16, D), BF16)
    v_ref[0, TOP + SPAN :, :] = jnp.zeros((16, D), BF16)
    n1 = n1_ref[...]
    for g in range(GROUPS):
        cols = slice(g * EG, (g + 1) * EG)
        q_ref[:, cols] = (dot(n1, w_ref[g, :, 0:EG]) * HEAD_DIM**-0.5).astype(BF16)
        k_ref[0, TOP : TOP + SPAN, cols] = dot(n1, w_ref[g, :, EG : 2 * EG]).astype(BF16)
        v_ref[0, TOP : TOP + SPAN, cols] = dot(n1, w_ref[g, :, 2 * EG : 3 * EG]).astype(BF16)

    even = iota((1, D), 1) % PAIR < HEAD_DIM
    zero = jnp.zeros((), BF16)
    for r0, rows in ((0, 144), (144, 144), (288, 128), (416, 128)):
        kb, vb = k_ref[0, r0 : r0 + rows, :], v_ref[0, r0 : r0 + rows, :]
        ke_ref[r0 : r0 + rows, :] = jnp.where(even, kb, zero)
        ko_ref[r0 : r0 + rows, :] = jnp.where(even, zero, kb)
        ve_ref[r0 : r0 + rows, :] = jnp.where(even, vb, zero)
        vo_ref[r0 : r0 + rows, :] = jnp.where(even, zero, vb)

    first_key = TOP - meta[5, span]
    for j in range(PAIRS):
        lanes = slice(j * PAIR, (j + 1) * PAIR)
        for rows, q0, w0 in FORWARD_BLOCKS:
            window = slice(w0, w0 + 128)
            keys = jnp.concatenate([ke_ref[window, lanes], ko_ref[window, lanes]], axis=0)
            scores = dot_nt(q_ref[q0 : q0 + rows, lanes], keys)
            if q0 == 480:
                r, c = iota((rows, 256), 0), iota((rows, 256), 1) % 128 - 64
                bias = jnp.where((c >= r + 6) & (c <= r + 18) & (c < 48), 0.0, NEGATIVE)
            else:
                bias = bias_ref[...]
            scores = scores + bias
            if q0 == 0:
                scores = jnp.where(iota((rows, 256), 1) % 128 >= first_key, scores, NEGATIVE)
            expo = []
            for half in (scores[:, :128], scores[:, 128:]):
                top = jnp.max(half, axis=-1, keepdims=True)
                expo.append(jnp.exp(half - top).astype(BF16))
            values = jnp.concatenate([ve_ref[window, lanes], vo_ref[window, lanes]], axis=0)
            values = jnp.concatenate([values, ones_ref[...]], axis=1)
            mixed = dot(jnp.concatenate(expo, axis=1), values)
            att_ref[q0 : q0 + rows, lanes] = (mixed[:, :PAIR] / mixed[:, PAIR:]).astype(BF16)

    att = att_ref[...]
    mid_ref[...] = dot_nt(att[:, :EG], w_ref[0, :, 3 * EG :]) + dot_nt(
        att[:, EG:], w_ref[1, :, 3 * EG :]
    )
    for r0 in range(0, SPAN, 128):
        masked, _ = masked_rows(meta, span, frames_ref, r0, 128)
        mid_ref[r0 : r0 + 128, :] = mid_ref[r0 : r0 + 128, :] + masked

    if first_span == 0:
        @pl.when(step == 0)
        def _():
            pltpu.make_async_copy(w_ref, weights_out, sems.at[0]).wait()


def spec(block, index, **kw):
    return pl.BlockSpec(block, index, **kw)


def params():
    return pltpu.CompilerParams(
        dimension_semantics=("arbitrary",), vmem_limit_bytes=VMEM_LIMIT
    )


def cost(micros, size):
    return pl.CostEstimate(flops=int(micros * 1.1e9), bytes_accessed=size, transcendentals=0)


def slot_count(pieces):
    return sum(piece.shape[0] for piece in pieces)


def row_block(first=0):
    return spec((SPAN, D), lambda s, m, p: (first + s, 0))


def fixed(shape):
    return spec(shape, lambda s, m, p: (0,) * len(shape))


def struct(shape, dtype):
    return jax.ShapeDtypeStruct(shape, dtype)


def attention_forward(
    meta, places, frames, ctx_k, ctx_v, norm, pieces, tokens, first_span, spans
):
    rows = spans * SPAN
    keys_block = spec((1, KEYS, D), lambda s, m, p: (s, 0, 0))
    top_block = spec((1, TOP, D), lambda s, m, p: (first_span + s, 0, 0))
    return pl.pallas_call(
        functools.partial(attention_forward_kernel, first_span, len(pieces), len(tokens)),
        grid_spec=pltpu.PrefetchScalarGridSpec(
            num_scalar_prefetch=2,
            grid=(spans,),
            in_specs=[
                spec((SPAN, D), lambda s, m, p: (m[0, 0] + first_span + s, 0)),
                top_block,
                top_block,
                fixed((8, D)),
            ]
            + [pl.BlockSpec(memory_space=pl.ANY)] * (len(pieces) + len(tokens)),
            out_specs=[
                row_block(), row_block(), keys_block, keys_block, row_block(), row_block()
            ]
            + [pl.BlockSpec(memory_space=pl.ANY)] * (first_span == 0),
            scratch_shapes=[
                pltpu.VMEM((GROUPS, D, 4 * EG), BF16),
                pltpu.SemaphoreType.DMA((slot_count(pieces),)),
                pltpu.VMEM((KEYS, D), BF16),
                pltpu.VMEM((KEYS, D), BF16),
                pltpu.VMEM((KEYS, D), BF16),
                pltpu.VMEM((KEYS, D), BF16),
                pltpu.VMEM((96, 256), F32),
                pltpu.VMEM((256, 128), BF16),
            ],
        ),
        out_shape=[
            struct((rows, D), BF16),
            struct((rows, D), BF16),
            struct((spans, KEYS, D), BF16),
            struct((spans, KEYS, D), BF16),
            struct((rows, D), BF16),
            struct((rows, D), F32),
        ]
        + [struct((GROUPS, D, 4 * EG), BF16)] * (first_span == 0),
        compiler_params=params(),
        cost_estimate=cost(4.5 * spans, rows * D * 14),
        name="attention_forward",
    )(meta, places, frames, ctx_k, ctx_v, norm, *pieces, *tokens)


FEED_WIDTH = 2 * FG + EG + EXTRA
ATTENTION_WIDTH = 3 * EG + EXTRA


def feed_forward_kernel(first, last, parts, count, meta, places, *refs):
    mid_ref, cot_ref, att_ref, norm_ref, inner_b_ref = refs[:5]
    slots_ref, refs = refs[5 : 5 + count], refs[5 + count :]
    if not first:
        (_, before_src, before_sums_ref, before_sums_b_ref), refs = refs[:4], refs[4:]
    (out_ref, chunk_ref, gm_ref), refs = refs[:3], refs[3:]
    if last:
        outs, refs = refs[: 2 * parts], refs[2 * parts :]
    else:
        outs, (left_sums_ref, left_sums_b_ref), refs = refs[:1], refs[1:3], refs[3:]
    if first and not last:
        weights_out, refs = refs[0], refs[1:]
    held, refs = refs[: len(outs) // 2 or 1], refs[len(outs) // 2 or 1 :]
    w_ref, sems, out_sems, n2_ref, cots_ref, gms_ref, atts_ref, hid_ref, gin_ref, dn_ref = refs[:10]
    result_ref, sums_ref, sums_b_ref = refs[10:13]
    refs = refs[13:]
    step = pl.program_id(0)
    here = pl.ds(pl.multiple_of(step * SPAN, SPAN), SPAN)

    @pl.when(step == 0)
    def _():
        load_weights(places, slots_ref, w_ref, sems, True)
        if first:
            sums_ref[...] = jnp.zeros_like(sums_ref)
            sums_b_ref[...] = jnp.zeros_like(sums_b_ref)
        else:
            pltpu.make_async_copy(before_src, refs[0], refs[1]).start()
            sums_ref[...] = before_sums_ref[...]
            sums_b_ref[...] = before_sums_b_ref[...]

    for r0 in range(0, SPAN, 128):
        xhat, _ = normalize(mid_ref[r0 : r0 + 128, :])
        place = pl.ds(pl.multiple_of(step * SPAN + r0, 128), 128)
        n2_ref[place, :] = (xhat * norm_ref[2:3, :] + norm_ref[3:4, :]).astype(BF16)
    cots_ref[here, :] = cot_ref[...]
    atts_ref[here, :] = att_ref[...]

    @pl.when(step == 0)
    def _():
        load_weights(places, slots_ref, w_ref, sems, False)
        if first and not last:
            pltpu.make_async_copy(w_ref, weights_out, sems.at[0]).start()

    chunk = 512
    for g in range(GROUPS):
        for c0 in range(0, FG, chunk):
            cols = slice(g * FG + c0, g * FG + c0 + chunk)
            act = dot(n2_ref[here, :], w_ref[g, :, c0 : c0 + chunk]) + inner_b_ref[0:1, cols]
            square = act * act
            tanh = jnp.tanh(act * (0.7978845608 + (0.7978845608 * 0.044715) * square))
            weight = 0.5 + 0.5 * tanh
            hidden = act * weight
            hid_ref[here, cols] = hidden.astype(BF16)
            slope = weight + (hidden - hidden * weight) * (
                2.0 * 0.7978845608 + (6.0 * 0.7978845608 * 0.044715) * square
            )
            grad = dot(cot_ref[...], w_ref[g, :, FG + c0 : FG + c0 + chunk]) * slope
            grad_low = grad.astype(BF16)
            gin_ref[here, cols] = grad_low
            sums_b_ref[:, cols] += fold_rows(grad_low.astype(F32))

    out = (
        mid_ref[...]
        + dot_nt(hid_ref[here, :FG], w_ref[0, :, FG:])
        + dot_nt(hid_ref[here, FG:], w_ref[1, :, FG:])
        + norm_ref[4:5, :]
    ).astype(BF16)
    out_ref[...] = out
    chunk_ref[...] = out
    dn_ref[...] = dot_nt(gin_ref[here, :FG], w_ref[0, :, :FG]) + dot_nt(
        gin_ref[here, FG:], w_ref[1, :, :FG]
    )

    for r0 in range(0, SPAN, 128):
        rows = slice(r0, r0 + 128)
        xhat, scale = normalize(mid_ref[rows, :])
        grad = dn_ref[rows, :]
        cot = cot_ref[rows, :].astype(F32)
        sums_ref[0:8, :] += fold_rows(grad * xhat)
        sums_ref[8:16, :] += fold_rows(grad)
        sums_ref[16:24, :] += fold_rows(cot)
        t = grad * norm_ref[2:3, :]
        gm = (cot + scale * (t - row_mean(t) - xhat * row_mean(t * xhat))).astype(BF16)
        gm_ref[rows, :] = gm
        gms_ref[pl.ds(pl.multiple_of(step * SPAN + r0, 128), 128), :] = gm

    @pl.when(step == pl.num_programs(0) - 1)
    def _():
        store = GradientStore(last, meta[0, 1], held, outs, out_sems)
        if first and not last:
            pltpu.make_async_copy(w_ref, weights_out, sems.at[0]).wait()
        if not first:
            pltpu.make_async_copy(before_src, refs[0], refs[1]).wait()
        if last:
            vectors = [column_sum(sums_ref[8 * i : 8 * i + 8, :]) for i in range(3)]
            for g in range(GROUPS):
                wide = column_sum(sums_b_ref[:, g * FG : (g + 1) * FG])
                result_ref[1, :, g * EXTRA : (g + 1) * EXTRA] = vector_block(
                    vectors, wide, 32
                ).astype(F32)
            store.put(
                result_ref.at[1],
                [(g, g * EXTRA, FEED_WIDTH - EXTRA, EXTRA) for g in range(GROUPS)],
            )
        else:
            left_sums_ref[...] = sums_ref[...]
            left_sums_b_ref[...] = sums_b_ref[...]
        jobs = [(n2_ref, gin_ref, 512 * c, [(c // 2, 0, 512 * (c % 2), 512)]) for c in range(4)]
        jobs += [
            (cots_ref, hid_ref, 512 * c, [(c // 2, 0, FG + 512 * (c % 2), 512)]) for c in range(4)
        ]
        jobs += [(gms_ref, atts_ref, 0, [(g, g * EG, 2 * FG, EG) for g in range(GROUPS)])]
        for number, (left, right, first_column, columns) in enumerate(jobs):
            result = dot_tn(left[...], right[:, first_column : first_column + 512])
            buffer = result_ref.at[number % 2]
            if first:
                buffer[...] = result
            else:
                for g, source, target, width in columns:
                    buffer[:, source : source + width] = result[
                        :, source : source + width
                    ] + refs[0][g, :, target : target + width].astype(F32)
            store.put(buffer, columns)
        store.finish()


def feed_forward(
    meta, places, mid, cot, att, norm, inner_b, pieces, before, first_span, spans, last, parts
):
    rows = spans * SPAN
    first = not before
    whole = pl.BlockSpec(memory_space=pl.ANY)
    whole_rows = spec((SPAN, D), lambda s, m, p: (m[0, 0] + first_span + s, 0))
    in_specs = [row_block(first_span), whole_rows, row_block(first_span), fixed((8, D)), fixed((1, FF))]
    in_specs += [whole] * len(pieces)
    args = [mid, cot, att, norm, inner_b, *pieces]
    aliases = {}
    held, out_sems, shapes = gradient_buffers(last, parts, FEED_WIDTH if last else FEED_WIDTH - EXTRA, 10)
    low = pltpu.VMEM((rows, D), BF16)
    scratch = held + [
        pltpu.VMEM((GROUPS, D, 2 * FG), BF16),
        pltpu.SemaphoreType.DMA((slot_count(pieces),)),
        out_sems,
        low,
        low,
        low,
        low,
        pltpu.VMEM((rows, FF), BF16),
        pltpu.VMEM((rows, FF), BF16),
        pltpu.VMEM((SPAN, D), F32),
        pltpu.VMEM((2, D, 512), F32),
        pltpu.VMEM((24, D), F32),
        pltpu.VMEM((8, FF), F32),
    ]
    if not first:
        aliases = {2 + len(args): 0}
        in_specs += [whole, whole, fixed((24, D)), fixed((8, FF))]
        args += before
        scratch += [
            pltpu.VMEM((GROUPS, D, FEED_WIDTH - EXTRA), BF16), pltpu.SemaphoreType.DMA(())
        ]
    out_specs = [whole_rows, row_block(), row_block()] + [whole] * len(shapes)
    out_shape = [struct(cot.shape, BF16), struct((rows, D), BF16), struct((rows, D), BF16)]
    out_shape += shapes
    if not last:
        out_specs += [fixed((24, D)), fixed((8, FF))]
        out_shape += [struct((24, D), F32), struct((8, FF), F32)]
    if first and not last:
        out_specs += [whole]
        out_shape += [struct((GROUPS, D, 2 * FG), BF16)]
    outs = pl.pallas_call(
        functools.partial(feed_forward_kernel, first, last, parts, len(pieces)),
        grid_spec=pltpu.PrefetchScalarGridSpec(
            num_scalar_prefetch=2,
            grid=(spans,),
            in_specs=in_specs,
            out_specs=out_specs,
            scratch_shapes=scratch,
        ),
        out_shape=out_shape,
        input_output_aliases=aliases,
        compiler_params=params(),
        cost_estimate=cost(11 * spans, rows * D * 10),
        name="feed_forward",
    )(meta, places, *args)
    return outs[0], outs[1], outs[2], outs[3:]


def gradient_outs(parts, width):
    shape = (GROUPS, 8, D // 16 // parts, width)
    return [fixed(shape)] * (2 * parts), [struct(shape, BF16)] * (2 * parts)


def attention_backward_kernel(
    first, last, parts, cuts, first_span, meta, places, *refs
):
    frames_ref, n1_ref, q_ref, k_ref, v_ref, gm_ref, norm_ref, weights_ref = refs[:8]
    refs = refs[8:]
    if not first:
        (_, before_ref, before_sums_ref), refs = refs[:3], refs[3:]
    gf_ref, chunk_refs, gctx_ref = refs[0], refs[1 : 1 + len(cuts)], refs[1 + len(cuts)]
    refs = refs[2 + len(cuts) :]
    if last:
        keeps, sends, refs = refs[:parts], refs[parts : 2 * parts], refs[2 * parts :]
    else:
        (grad_ref, left_sums_ref), refs = refs[:2], refs[2:]
    w_ref, sems, gatt_ref, dq_ref, dk_ref, dv_ref, dkb_ref, dvb_ref = refs[:8]
    n1t_ref, dn_ref, bias_ref, acc_ref, sums_ref = refs[8:13]
    refs = refs[13:]
    step = pl.program_id(0)
    span = meta[0, 0] + first_span + step

    @pl.when(step == 0)
    def _():
        load_weights(places, [weights_ref], w_ref, sems, True)
        acc_ref[...] = jnp.zeros_like(acc_ref)
        if first:
            sums_ref[...] = jnp.zeros_like(sums_ref)
        else:
            pltpu.make_async_copy(before_ref, refs[0], refs[1]).start()
            sums_ref[...] = before_sums_ref[...]
        r, c = iota((160, 256), 0), iota((160, 256), 1) % 128
        bias_ref[...] = jnp.where((r >= c + 6) & (r <= c + 18), 0.0, NEGATIVE)

    n1t_ref[...] = n1_ref[...].T

    @pl.when(step == 0)
    def _():
        load_weights(places, [weights_ref], w_ref, sems, False)

    for g in range(GROUPS):
        gatt_ref[:, g * EG : (g + 1) * EG] = dot(gm_ref[...], w_ref[g, :, 3 * EG :]).astype(BF16)

    first_key = TOP - meta[5, span]
    even = low_half()
    zero = jnp.zeros((), BF16)
    for j in range(PAIRS):
        lanes = slice(j * PAIR, (j + 1) * PAIR)
        for b in range(SPAN // 128):
            rows, window = slice(128 * b, 128 * b + 128), slice(128 * b, 128 * b + 160)
            kw, vw = k_ref[0, window, lanes], v_ref[0, window, lanes]
            qb, ob = q_ref[rows, lanes], gatt_ref[rows, lanes]
            qs = jnp.concatenate([jnp.where(even, qb, zero), jnp.where(even, zero, qb)], axis=0)
            os = jnp.concatenate([jnp.where(even, ob, zero), jnp.where(even, zero, ob)], axis=0)
            scores = dot_nt(kw, qs) + bias_ref[...]
            if b == 0:
                scores = jnp.where(iota((160, 256), 0) >= first_key, scores, NEGATIVE)
            if b == SPAN // 128 - 1:
                scores = jnp.where(iota((160, 256), 0) < 144, scores, NEGATIVE)
            expo = jnp.exp(scores - jnp.max(scores, axis=0, keepdims=True))
            probs = expo * (1.0 / jnp.sum(expo, axis=0, keepdims=True))
            grad_probs = dot_nt(vw, os)
            delta = jnp.sum(probs * grad_probs, axis=0, keepdims=True)
            ds = (probs * (grad_probs - delta)).astype(BF16)
            dv = dot(probs.astype(BF16), os)
            dk = dot(ds, qs)
            if b == 0:
                dkb_ref[window, lanes] = dk
                dvb_ref[window, lanes] = dv
            else:
                lap, rest = slice(128 * b, 128 * b + 32), slice(128 * b + 32, 128 * b + 160)
                dkb_ref[lap, lanes] += dk[:32]
                dvb_ref[lap, lanes] += dv[:32]
                dkb_ref[rest, lanes] = dk[32:]
                dvb_ref[rest, lanes] = dv[32:]
            dq = dot_tn(ds, kw)
            dq = jnp.where(even, dq[:128], dq[128:]) * HEAD_DIM**-0.5
            dq_ref[rows, lanes] = dq.astype(BF16)
    for g in range(GROUPS):
        gctx_ref[g, 0, 0] = dkb_ref[0:TOP, g * EG : (g + 1) * EG]
        gctx_ref[g, 1, 0] = dvb_ref[0:TOP, g * EG : (g + 1) * EG]
    dk_ref[...] = dkb_ref[TOP : TOP + SPAN, :].astype(BF16)
    dv_ref[...] = dvb_ref[TOP : TOP + SPAN, :].astype(BF16)

    for g in range(GROUPS):
        cols = slice(g * EG, (g + 1) * EG)
        acc_ref[g, :, 0:EG] += dot(n1t_ref[...], dq_ref[:, cols])
        acc_ref[g, :, EG : 2 * EG] += dot(n1t_ref[...], dk_ref[:, cols])
        acc_ref[g, :, 2 * EG : 3 * EG] += dot(n1t_ref[...], dv_ref[:, cols])
    total = None
    for g in range(GROUPS):
        cols = slice(g * EG, (g + 1) * EG)
        for m, ref in enumerate((dq_ref, dk_ref, dv_ref)):
            term = dot_nt(ref[:, cols], w_ref[g, :, m * EG : (m + 1) * EG])
            total = term if total is None else total + term
    dn_ref[...] = total
    for r0 in range(0, SPAN, 128):
        rows = slice(r0, r0 + 128)
        masked, keep = masked_rows(meta, span, frames_ref, r0, 128)
        xhat, scale = normalize(masked)
        grad = dn_ref[rows, :]
        sums_ref[0:8, :] += fold_rows(grad * xhat)
        sums_ref[8:16, :] += fold_rows(grad)
        t = grad * norm_ref[0:1, :]
        back = scale * (t - row_mean(t) - xhat * row_mean(t * xhat))
        result = ((gm_ref[rows, :].astype(F32) + back) * keep).astype(BF16)
        gf_ref[rows, :] = result
        column = 0
        for chunk_ref in chunk_refs:
            width = chunk_ref.shape[1]
            chunk_ref[rows, :] = result[:, column : column + width]
            column += width

    @pl.when(step == pl.num_programs(0) - 1)
    def _():
        if not first:
            pltpu.make_async_copy(before_ref, refs[0], refs[1]).wait()
            for g in range(GROUPS):
                acc_ref[g] += refs[0][g].astype(F32)
        if not last:
            for g in range(GROUPS):
                grad_ref[g] = acc_ref[g].astype(BF16)
            left_sums_ref[...] = sums_ref[...]
        else:
            split_core(meta[0, 1], acc_ref, keeps, sends, 3 * EG)
            vectors = [column_sum(sums_ref[8 * i : 8 * i + 8, :]) for i in range(2)]
            block = vector_block(vectors, None, 2 * 16).astype(F32)
            for g in range(GROUPS):
                refs[-1][g] = block
            split_extra(meta[0, 1], refs[-1], keeps, sends, 3 * EG)


def attention_backward(
    meta, places, frames, kept, gm, norm, weights, before, first_span, spans, last, parts, cuts
):
    rows = spans * SPAN
    first = not before
    whole = pl.BlockSpec(memory_space=pl.ANY)
    whole_rows = spec((SPAN, D), lambda s, m, p: (m[0, 0] + first_span + s, 0))
    keys_block = spec((1, KEYS, D), lambda s, m, p: (first_span + s, 0, 0))
    kept_rows = row_block(first_span)
    low = pltpu.VMEM((SPAN, D), BF16)
    in_specs = [
        whole_rows, kept_rows, kept_rows, keys_block, keys_block, row_block(), fixed((8, D)),
        whole,
    ]
    args = [frames, *kept, gm, norm, weights]
    aliases = {}
    scratch = [
        pltpu.VMEM((GROUPS, D, 4 * EG), BF16),
        pltpu.SemaphoreType.DMA((1,)),
        low,
        low,
        low,
        low,
        pltpu.VMEM((KEYS, D), F32),
        pltpu.VMEM((KEYS, D), F32),
        low,
        pltpu.VMEM((SPAN, D), F32),
        pltpu.VMEM((160, 256), F32),
        pltpu.VMEM((GROUPS, D, 3 * EG), F32),
        pltpu.VMEM((16, D), F32),
    ]
    if not first:
        aliases = {2 + len(args): 0}
        in_specs += [whole, whole, fixed((16, D))]
        args += before
        scratch += [pltpu.VMEM((GROUPS, D, 3 * EG), BF16), pltpu.SemaphoreType.DMA(())]
    out_specs = [
        whole_rows,
        *[spec((SPAN, cut), lambda s, m, p: (s, 0)) for cut in cuts],
        spec((GROUPS, 2, 1, TOP, EG), lambda s, m, p: (0, 0, s, 0, 0)),
    ]
    out_shape = [
        struct(frames.shape, BF16),
        *[struct((rows, cut), BF16) for cut in cuts],
        struct((GROUPS, 2, spans, TOP, EG), F32),
    ]
    if last:
        more_specs, more_shapes = gradient_outs(parts, ATTENTION_WIDTH)
        scratch += [pltpu.VMEM((GROUPS, D, EXTRA), F32)]
    else:
        more_specs = [fixed((GROUPS, D, 3 * EG)), fixed((16, D))]
        more_shapes = [struct((GROUPS, D, 3 * EG), BF16), struct((16, D), F32)]
    outs = pl.pallas_call(
        functools.partial(attention_backward_kernel, first, last, parts, cuts, first_span),
        grid_spec=pltpu.PrefetchScalarGridSpec(
            num_scalar_prefetch=2,
            grid=(spans,),
            in_specs=in_specs,
            out_specs=out_specs + more_specs,
            scratch_shapes=scratch,
        ),
        out_shape=out_shape + more_shapes,
        input_output_aliases=aliases,
        compiler_params=params(),
        cost_estimate=cost(10 * spans, rows * D * 14),
        name="attention_backward",
    )(meta, places, *args)
    count = len(cuts)
    return outs[0], outs[1 : 1 + count], outs[1 + count], outs[2 + count :]


BITS = {"core": ("dp", 1), "y": ("dp", 2), "z1": ("dp", 4), "z2": ("dp", 8), "x": ("tensor", 1)}
BIT_DIM = {"x": 0, "z2": 1, "z1": 2, "y": 3}


def swap(value, bits, flips=(1, 1)):
    bits = (bits,) if isinstance(bits, str) else bits
    axis = BITS[bits[0]][0]
    distance = sum(BITS[bit][1] * flip for bit, flip in zip(bits, flips))
    return lax.ppermute(value, axis, [(i, i ^ distance) for i in range(lax.axis_size(axis))])


def my_bit(bit):
    axis, distance = BITS[bit]
    return (lax.axis_index(axis) // distance) % 2


def tie(value, *tokens):
    return lax.optimization_barrier((value, tokens))[0]


def piece_places(order, rows, first):
    groups, firsts = [], []
    dp, tensor = lax.axis_index("dp"), lax.axis_index("tensor")
    for j in range(2 ** len(order)):
        dp_flip = sum(BITS[b][1] for i, b in enumerate(order) if j >> i & 1 and b != "x")
        x_flip = sum(1 for i, b in enumerate(order) if j >> i & 1 and b == "x")
        groups.append(tensor ^ x_flip)
        firsts.append((dp ^ dp_flip) * rows + first)
    return jnp.stack([jnp.stack(groups), jnp.stack(firsts)]).astype(jnp.int32)


class Gather:
    def __init__(self, piece, shared, orders):
        self.shared, self.orders = shared, orders
        self.rows = piece.shape[0]
        self.part = self.rows // len(orders)
        self.held = [piece[None]]
        self.got = None
        self.step = 0
        self.steps = len(shared) + len(orders[0])

    def after(self, *tokens):
        if self.got is None:
            self.held = list(tie(tuple(self.held), *tokens))
        else:
            self.got = list(tie(tuple(self.got), *tokens))

    def exchange(self):
        if self.got is not None:
            self.held = [jnp.concatenate(pair, axis=0) for pair in zip(self.held, self.got)]
        if self.step < len(self.shared):
            bits = self.shared[self.step]
            if len(bits) == 2:
                held = self.held[0]
                flips = [(1, 0), (0, 1), (1, 1)]
                self.got = [jnp.concatenate([swap(held, bits, flip) for flip in flips], axis=0)]
                self.step += 1
                return
            bits = [bits[0]]
        else:
            if self.step == len(self.shared):
                whole = self.held[0]
                self.held = [
                    whole[:, h * self.part : (h + 1) * self.part] for h in range(len(self.orders))
                ]
            bits = [order[self.step - len(self.shared)] for order in self.orders]
        self.got = [swap(held, bit) for held, bit in zip(self.held, bits)]
        self.step += 1

    def result(self):
        return [array for pair in zip(self.held, self.got) for array in pair]

    def places(self):
        return jnp.concatenate(
            [
                piece_places(sum(self.shared, ()) + order, self.rows, h * self.part)
                for h, order in enumerate(self.orders)
            ],
            axis=1,
        )


class Scatter:
    def __init__(self, keeps_sends, stages):
        parts = len(stages)
        self.stages = stages
        self.rows, self.columns = keeps_sends[0].shape[2:]
        shape = (2, 2, 2, 2, self.rows, self.columns)
        self.terms = [
            [keep.reshape(shape), swap(send, "core").reshape(shape)]
            for keep, send in zip(keeps_sends[:parts], keeps_sends[parts:])
        ]
        self.step = 0

    def after(self, *tokens):
        self.terms = tie(self.terms, *tokens)

    def kept(self):
        return [terms[0] for terms in self.terms]

    def exchange(self):
        for h, stage in enumerate(self.stages):
            bits = stage[self.step]

            def block(flips):
                total = 0.0
                for term in self.terms[h]:
                    for bit, flip in zip(bits, flips):
                        place = my_bit(bit) ^ flip
                        term = lax.dynamic_index_in_dim(term, place, BIT_DIM[bit], keepdims=True)
                    total = total + term.astype(F32)
                return total.astype(BF16)

            flips = [(1,)] if len(bits) == 1 else [(1, 0), (0, 1), (1, 1)]
            got = [swap(block(flip), bits, flip) for flip in flips]
            self.terms[h] = [block((0,) * len(bits)), *got]
        self.step += 1


def finish_sums(scatters, *others):
    mine = my_bit("x")
    keeps, sends = [], []
    for scatter in scatters:
        for place, blocks in ((mine, keeps), (1 - mine, sends)):
            parts = []
            for terms in scatter.terms:
                total = sum(
                    lax.dynamic_index_in_dim(term, place, 0, keepdims=False).astype(F32)
                    for term in terms
                )
                parts.append(total.reshape(scatter.rows, scatter.columns))
            blocks.append(jnp.concatenate(parts, axis=0))
    got = swap(jnp.concatenate(sends, axis=1).astype(BF16), "x").astype(F32)
    others = [swap(other, "x") for other in others]
    results, first = [], 0
    for keep in keeps:
        results.append(keep + got[:, first : first + keep.shape[1]])
        first += keep.shape[1]
    return (*results, *others)


ATTENTION_SHARED = (("z2", "z1"),)
FEED_SHARED = (("z2",), ("z1",))
ATTENTION_ORDERS = (("y", "x", "core"), ("x", "y", "core"))
FEED_ORDERS = (("y", "x", "core"), ("x", "y", "core"))
ATTENTION_SUMS = ((("y", "z1"), ("z2",)),)
FEED_SUMS = ((("y",), ("z1",), ("z2",)), (("z1",), ("z2",), ("y",)))


def body(
    frames,
    context_keys,
    context_values,
    time_start,
    time_width,
    freq_start,
    freq_width,
    context_count,
    gain_one,
    shift_one,
    query_w,
    key_w,
    value_w,
    out_w,
    gain_two,
    shift_two,
    inner_w,
    inner_b,
    outer_w,
    outer_b,
    cotangent,
):
    tensor, dp = lax.axis_size("tensor"), lax.axis_size("dp")
    tuned = tensor == 2 and dp == 16
    spans = time_start.shape[0] // tensor
    t_index = lax.axis_index("tensor")
    base = t_index * spans

    def pick(first, second):
        return jnp.where(t_index == 0, first, second)

    attention_piece = jnp.concatenate([query_w, key_w, value_w, out_w.T], axis=1)
    feed_piece = jnp.concatenate([inner_w, outer_w.T], axis=1)
    context = jnp.stack([context_keys, context_values])
    if tuned:
        gather = Gather(attention_piece, ATTENTION_SHARED, ATTENTION_ORDERS)
        feed_gather = Gather(feed_piece, FEED_SHARED, FEED_ORDERS)
        gather.exchange()
        context, inner_b = tie((context, inner_b), *gather.got)
        mine = lax.dynamic_slice_in_dim(context, base, spans, 1)
        theirs = swap(lax.dynamic_slice_in_dim(context, (1 - t_index) * spans, spans, 1), "x")
        context = pick(
            jnp.concatenate([mine, theirs], axis=3), jnp.concatenate([theirs, mine], axis=3)
        )
        other_b = swap(inner_b, "x")
        inner_b_full = pick(
            jnp.concatenate([inner_b, other_b]), jnp.concatenate([other_b, inner_b])
        ).reshape(1, FF)
        feed_gather.after(*gather.got)
        feed_gather.exchange()
        gather.exchange()
        gather.exchange()
        feed_gather.exchange()
        gather.after(*feed_gather.got)
        gather.exchange()
        feed_gather.exchange()
        attention_pieces, attention_places = gather.result(), gather.places()
        feed_places = feed_gather.places()
    else:
        def canonical(parts, width):
            grouped = []
            for part in parts:
                whole = lax.all_gather(part, "dp", axis=0, tiled=True)
                whole = lax.all_gather(whole, "tensor", axis=1, tiled=True)
                grouped.append(whole.reshape(D, GROUPS, width).swapaxes(0, 1))
            return [jnp.concatenate(grouped, axis=2)]

        attention_pieces = canonical((query_w, key_w, value_w, out_w.T), EG)
        feed_pieces = canonical((inner_w, outer_w.T), FG)
        attention_places = feed_places = jnp.array([[0, 1], [0, 0]], jnp.int32)
        context = lax.all_to_all(context, "tensor", split_axis=1, concat_axis=3, tiled=True)
        inner_b_full = lax.all_gather(inner_b, "tensor", axis=0, tiled=True).reshape(1, FF)
    context = jnp.pad(context, ((0, 0), (0, 0), (TOP - LEFT, 0), (0, 0)))

    core_bit = my_bit("core") if tuned else 0
    first_row = jnp.zeros_like(time_start).at[0].set(base).at[1].set(core_bit)
    meta = jnp.stack(
        [first_row, time_start, time_width, freq_start, freq_width, context_count]
    ).astype(jnp.int32)
    norm = jnp.stack(
        [gain_one, shift_one, gain_two, shift_two, outer_b] + [jnp.zeros_like(gain_one)] * 3
    )

    chunk = min(CHUNK, spans)
    firsts = range(0, spans, chunk)
    final = spans - chunk

    def exchange(value):
        return swap(value, "x") if tuned else value

    if tuned:
        meta = tie(meta, inner_b_full, attention_places, feed_places, feed_gather.got)
        feed_gather.exchange()
    n1, q, k, v, att, mid, weights = attention_forward(
        meta, attention_places, frames, context[0], context[1], norm, attention_pieces, [], 0, spans
    )
    if tuned:
        feed_gather.after(n1)
        feed_gather.exchange()
        feed_pieces = feed_gather.result()
    outs, gms, before, feed_weights = [], [], [], None
    parts = len(FEED_SUMS) if tuned else 1
    for first in firsts:
        pieces = feed_pieces if feed_weights is None else [feed_weights]
        output, part, gm, rest = feed_forward(
            meta, feed_places, mid, cotangent, att, norm, inner_b_full, pieces, before,
            first, chunk, first == final, parts,
        )
        if first == 0 and first != final:
            *rest, feed_weights = rest
        outs.append(exchange(part))
        gms.append(gm)
        before = [output, *rest]
    feed_grad = rest
    frame_parts, contexts, before = [], [], []
    parts = len(ATTENTION_SUMS) if tuned else 1
    if tuned:
        feed_grad = list(tie(tuple(feed_grad), outs[0]))
        feed_scatter = Scatter(feed_grad, FEED_SUMS)
        feed_scatter.exchange()
    for index, (first, gm) in enumerate(zip(firsts, gms)):
        own_meta = meta
        if tuned:
            own_meta = tie(meta, *feed_scatter.kept(), *(outs[-1:] if index > 0 else []))
        cuts = (3 * D // 4, D // 4) if tuned and first == final else (D,)
        grad_frames, pieces, gctx, rest = attention_backward(
            own_meta, attention_places, frames, (n1, q, k, v), gm, norm, weights, before, first, chunk,
            first == final, parts, cuts,
        )
        frame_parts.append([exchange(piece) for piece in pieces])
        contexts.append(gctx)
        before = [grad_frames, *rest]
        if tuned and index == 0:
            feed_scatter.after(grad_frames)
            feed_scatter.exchange()
    attention_grad = rest
    if tuned:
        attention_grad = list(tie(tuple(attention_grad), frame_parts[:-1], feed_scatter.terms))
        attention_scatter = Scatter(attention_grad, ATTENTION_SUMS)
        output, grad_frames = tie((output, grad_frames), attention_scatter.terms)
        feed_scatter.exchange()
        attention_scatter.after(*feed_scatter.kept())
        attention_scatter.exchange()
        feed_scatter.after(attention_scatter.terms)
        attention_scatter.after(frame_parts[-1][0])
        attention_scatter.exchange()
        (feed_sum,) = finish_sums([feed_scatter])
        attention_scatter.terms, frame_parts[-1], contexts = tie(
            (attention_scatter.terms, frame_parts[-1], contexts)
        )

    if tuned:
        def both(whole, parts):
            for first, pieces in zip(firsts, parts):
                place, column = ((1 - t_index) * spans + first) * SPAN, 0
                for piece in pieces:
                    whole = lax.dynamic_update_slice(whole, piece, (place, column))
                    column += piece.shape[1]
            return whole

        output = both(output, [[part] for part in outs])
        grad_frames = both(grad_frames, frame_parts)
        gctx = jnp.concatenate(contexts, axis=2)[:, :, :, TOP - LEFT :]
        mine, theirs = (
            lax.dynamic_index_in_dim(gctx, place, 0, keepdims=False)
            for place in (t_index, 1 - t_index)
        )
        attention_sum, theirs = finish_sums([attention_scatter], theirs)
        grad_context = pick(
            jnp.concatenate([mine, theirs], axis=1), jnp.concatenate([theirs, mine], axis=1)
        )
        extra = feed_sum[:4, FEED_WIDTH - EXTRA :]
        sum_gain_two, sum_shift_two, sum_outer_b = (extra[i, :32] for i in range(3))
        sum_inner_b = extra[3, :64]
        sum_gain_one, sum_shift_one = (
            attention_sum[i, 3 * EG : 3 * EG + 32] for i in range(2)
        )
        sum_query, sum_key, sum_value = (
            attention_sum[:, i * EG : (i + 1) * EG] for i in range(3)
        )
        sum_inner, sum_outer = feed_sum[:, :FG], feed_sum[:, FG : 2 * FG]
        sum_out = feed_sum[:, 2 * FG : 2 * FG + EG]
    else:
        def both(parts):
            return lax.all_gather(jnp.concatenate(parts, axis=0), "tensor", axis=0, tiled=True)

        output = both(outs)
        grad_frames = both([piece for (piece,) in frame_parts])
        gctx = jnp.concatenate(contexts, axis=2)[:, :, :, TOP - LEFT :]
        grad_context = jnp.moveaxis(gctx, 0, 3).reshape(2, spans, LEFT, D)
        grad_context = lax.all_to_all(
            grad_context, "tensor", split_axis=3, concat_axis=1, tiled=True
        )
        attention_grad, feed_grad = (
            jnp.stack(pair, axis=2).reshape(GROUPS, D, -1) for pair in (attention_grad, feed_grad)
        )

        def whole_grad(grad, index, width):
            return grad[:, :, index * width : (index + 1) * width].swapaxes(0, 1).reshape(D, -1)

        def scattered(grad):
            part = lax.psum_scatter(grad, "dp", scatter_dimension=0, tiled=True)
            return lax.psum_scatter(part, "tensor", scatter_dimension=1, tiled=True).astype(F32)

        def summed(item):
            item = lax.psum(item, "tensor")
            return lax.psum_scatter(item, "dp", scatter_dimension=0, tiled=True)

        def vector(grad, index):
            item = grad[0, :, -EXTRA:].reshape(16, 32, EXTRA)[:, index, :32].reshape(D)
            return summed(item.astype(F32))

        sum_query, sum_key, sum_value = (
            scattered(whole_grad(attention_grad, i, EG)) for i in range(3)
        )
        sum_inner, sum_outer = (scattered(whole_grad(feed_grad, i, FG)) for i in range(2))
        sum_out = scattered(feed_grad[:, :, 2 * FG : 2 * FG + EG].swapaxes(0, 1).reshape(D, -1))
        sum_gain_one, sum_shift_one = (vector(attention_grad, i) for i in range(2))
        sum_gain_two, sum_shift_two, sum_outer_b = (vector(feed_grad, i) for i in range(3))
        sum_inner_b = feed_grad[:, :, -EXTRA:].reshape(GROUPS, 16, 32, EXTRA)[:, :, 3, :64]
        sum_inner_b = sum_inner_b.reshape(FF).astype(F32)
        sum_inner_b = lax.psum_scatter(sum_inner_b, "tensor", scatter_dimension=0, tiled=True)
        sum_inner_b = lax.psum_scatter(sum_inner_b, "dp", scatter_dimension=0, tiled=True)

    return (
        output,
        grad_frames,
        grad_context[0],
        grad_context[1],
        sum_gain_one,
        sum_shift_one,
        sum_query,
        sum_key,
        sum_value,
        sum_out.T,
        sum_gain_two,
        sum_shift_two,
        sum_inner,
        sum_inner_b,
        sum_outer.T,
        sum_outer_b,
    )


def solution(mesh):
    in_specs = (
        P("dp", None),
        P("dp", None, "tensor"),
        P("dp", None, "tensor"),
        P("dp"),
        P("dp"),
        P("dp"),
        P("dp"),
        P("dp"),
        P(),
        P(),
        P("dp", "tensor"),
        P("dp", "tensor"),
        P("dp", "tensor"),
        P("tensor", "dp"),
        P(),
        P(),
        P("dp", "tensor"),
        P("tensor"),
        P("tensor", "dp"),
        P(),
        P("dp", None),
    )
    out_specs = (
        P("dp", None),
        P("dp", None),
        P("dp", None, "tensor"),
        P("dp", None, "tensor"),
        P("dp"),
        P("dp"),
        P("dp", "tensor"),
        P("dp", "tensor"),
        P("dp", "tensor"),
        P("tensor", "dp"),
        P("dp"),
        P("dp"),
        P("dp", "tensor"),
        P(("tensor", "dp")),
        P("tensor", "dp"),
        P("dp"),
    )
    return jax.shard_map(body, mesh=mesh, in_specs=in_specs, out_specs=out_specs, check_vma=False)
```

```python
import functools

import jax
import jax.numpy as jnp
from jax import lax
from jax.experimental import pallas as pl
from jax.experimental.pallas import tpu as pltpu
from jax.sharding import PartitionSpec as P

D = 512
HEAD_DIM = 64
SPAN = 512
LEFT = 10
RIGHT = 2
FF = 2048
PAIR = 2 * HEAD_DIM
PAIRS = D // PAIR
GROUPS = 2
EG = D // GROUPS
FG = FF // GROUPS
TOP = 16
KEYS = TOP + SPAN + 16
EXTRA = 128
CHUNK = 2
NEGATIVE = -1e30
epsilon = 1e-05
F32 = jnp.float32
BF16 = jnp.bfloat16
VMEM_LIMIT = 56 * 1024 * 1024
FORWARD_BLOCKS = tuple((96, 96 * b, 96 * b) for b in range(5)) + ((32, 480, 416),)


def dot(a, b):
    return lax.dot_general(a, b, (((1,), (0,)), ((), ())), preferred_element_type=F32)


def dot_nt(a, b):
    return lax.dot_general(a, b, (((1,), (1,)), ((), ())), preferred_element_type=F32)


def dot_tn(a, b):
    return lax.dot_general(a, b, (((0,), (0,)), ((), ())), preferred_element_type=F32)


def iota(shape, dim):
    return lax.broadcasted_iota(jnp.int32, shape, dim)


def row_mean(v):
    return jnp.sum(v, axis=-1, keepdims=True) * (1.0 / D)


def normalize(v):
    center = v - row_mean(v)
    scale = lax.rsqrt(row_mean(center * center) + epsilon)
    return center * scale, scale


def fold_rows(v):
    total = v[0:8]
    for r in range(8, v.shape[0], 8):
        total = total + v[r : r + 8]
    return total


def masked_rows(meta, span, frames_ref, row0, rows):
    places = iota((rows, 1), 0) + row0
    hide_t = (places >= meta[1, span]) & (places < meta[1, span] + meta[2, span])
    columns = iota((1, D), 1)
    hide_f = (columns >= meta[3, span]) & (columns < meta[3, span] + meta[4, span])
    keep = jnp.where(hide_t, 0.0, 1.0) * jnp.where(hide_f, 0.0, 1.0)
    return frames_ref[pl.ds(row0, rows), :].astype(F32) * keep, keep


def load_slots(places, pieces, w_ref, sems, start):
    j = 0
    for piece in pieces:
        for i in range(piece.shape[0]):
            copy = pltpu.make_async_copy(
                piece.at[i],
                w_ref.at[
                    places[0, j], pl.ds(pl.multiple_of(places[1, j], 16), piece.shape[1]), :
                ],
                sems.at[j],
            )
            if start:
                copy.start()
            else:
                copy.wait()
            j += 1


def load_weights(places, pieces, w_ref, sems, start):
    if len(pieces) > 1 or pieces[0].shape != w_ref.shape:
        load_slots(places, pieces, w_ref, sems, start)
        return
    copy = pltpu.make_async_copy(pieces[0], w_ref, sems.at[0])
    if start:
        copy.start()
    else:
        copy.wait()


def vector_block(rows_of, wide, own_rows):
    blocks = D // own_rows
    r, c = iota((D, D), 0), iota((D, D), 1)
    value = jnp.zeros((D, D), F32)
    for i, vector in enumerate(rows_of):
        value = jnp.where(r % own_rows == i, vector, value)
    value = jnp.where(r // own_rows == c // own_rows, value, 0.0).astype(BF16)
    pick = jnp.where(iota((D, EXTRA), 0) % own_rows == iota((D, EXTRA), 1), 1.0, 0.0)
    block = dot(value, pick.astype(BF16))
    if wide is not None:
        width = wide.shape[1]
        share = width // blocks
        r, c = iota((D, width), 0), iota((D, width), 1)
        here = (r // own_rows == c // share) & (r % own_rows == len(rows_of))
        value = jnp.where(here, wide, 0.0).astype(BF16)
        pick = jnp.where(iota((width, EXTRA), 0) % share == iota((width, EXTRA), 1), 1.0, 0.0)
        block = block + dot(value, pick.astype(BF16))
    return block.astype(BF16)


def column_sum(v):
    return jnp.sum(v, axis=0, keepdims=True)


def split_core(core_bit, grad_ref, keeps, sends, width):
    blocks, part = keeps[0].shape[1], keeps[0].shape[2]
    rows = D // (2 * blocks)
    for outs, bit in ((keeps, core_bit), (sends, 1 - core_bit)):
        for i in range(blocks):
            first = pl.multiple_of((2 * i + bit) * rows, 16)
            for h, out in enumerate(outs):
                for g in range(GROUPS):
                    out[g, i, :, :width] = grad_ref[g, pl.ds(first + h * part, part), :width].astype(BF16)


def split_extra(core_bit, block_ref, keeps, sends, width):
    blocks, part = keeps[0].shape[1], keeps[0].shape[2]
    rows = D // (2 * blocks)
    for outs, bit in ((keeps, core_bit), (sends, 1 - core_bit)):
        for i in range(blocks):
            first = pl.multiple_of((2 * i + bit) * rows, 16)
            for h, out in enumerate(outs):
                for g in range(GROUPS):
                    value = block_ref[g, pl.ds(first + h * part, part), :]
                    out[g, i, :, width:] = value.astype(BF16)


class GradientStore:
    def __init__(self, last, core_bit, held, outs, sems):
        self.last, self.core_bit, self.held, self.outs, self.sems = last, core_bit, held, outs, sems
        self.jobs = []

    def copies(self, number, columns):
        for g, _, target, width in columns:
            cols = pl.ds(target, width)
            if not self.last:
                yield pltpu.make_async_copy(
                    self.held[0].at[g, :, cols], self.outs[0].at[g, :, cols],
                    self.sems.at[number, 0, 0, g],
                )
                continue
            parts = len(self.held)
            for h, held in enumerate(self.held):
                for side in range(2):
                    yield pltpu.make_async_copy(
                        held.at[side, g, :, :, cols],
                        self.outs[h + side * parts].at[g, :, :, cols],
                        self.sems.at[number, h, side, g],
                    )

    def put(self, result_ref, columns):
        for g, source, target, width in columns:
            if not self.last:
                self.held[0][g, :, target : target + width] = result_ref[
                    :, source : source + width
                ].astype(BF16)
                continue
            for h, held in enumerate(self.held):
                blocks, part = held.shape[2], held.shape[3]
                rows = D // (2 * blocks)
                for side, bit in ((0, self.core_bit), (1, 1 - self.core_bit)):
                    for i in range(blocks):
                        first = pl.multiple_of((2 * i + bit) * rows + h * part, 16)
                        held[side, g, i, :, target : target + width] = result_ref[
                            pl.ds(first, part), source : source + width
                        ].astype(BF16)
        number = len(self.jobs)
        self.jobs.append(columns)
        for copy in self.copies(number, columns):
            copy.start()

    def finish(self):
        for number, columns in enumerate(self.jobs):
            for copy in self.copies(number, columns):
                copy.wait()


def gradient_buffers(last, parts, width, jobs):
    if not last:
        shapes = [struct((GROUPS, D, width), BF16)]
        held = [pltpu.VMEM((GROUPS, D, width), BF16)]
    else:
        part = D // 16 // parts
        shapes = [struct((GROUPS, 8, part, width), BF16)] * (2 * parts)
        held = [pltpu.VMEM((2, GROUPS, 8, part, width), BF16)] * parts
    sems = pltpu.SemaphoreType.DMA((jobs, parts if last else 1, 2, GROUPS))
    return held, sems, shapes


def low_half():
    return iota((1, PAIR), 1) < HEAD_DIM


def attention_forward_kernel(first_span, count, tokens, meta, places, *refs):
    frames_ref, ctx_k_ref, ctx_v_ref, norm_ref = refs[:4]
    slots_ref, refs = refs[4 : 4 + count], refs[4 + count + tokens :]
    n1_ref, q_ref, k_ref, v_ref, att_ref, mid_ref = refs[:6]
    if first_span == 0:
        weights_out, refs = refs[6], refs[7:]
    else:
        refs = refs[6:]
    w_ref, sems, ke_ref, ko_ref, ve_ref, vo_ref, bias_ref, ones_ref = refs
    step = pl.program_id(0)
    span = meta[0, 0] + first_span + step

    @pl.when(step == 0)
    def _():
        load_weights(places, slots_ref, w_ref, sems, True)
        r, c = iota((96, 256), 0), iota((96, 256), 1) % 128
        bias_ref[...] = jnp.where((c >= r + 6) & (c <= r + 18), 0.0, NEGATIVE)
        r, c = iota((256, 128), 0), iota((256, 128), 1)
        ones_ref[...] = jnp.where((r < 128) == (c < 64), 1.0, 0.0).astype(BF16)

    for r0 in range(0, SPAN, 128):
        masked, _ = masked_rows(meta, span, frames_ref, r0, 128)
        xhat, _ = normalize(masked)
        n1_ref[r0 : r0 + 128, :] = (xhat * norm_ref[0:1, :] + norm_ref[1:2, :]).astype(BF16)

    @pl.when(step == 0)
    def _():
        load_weights(places, slots_ref, w_ref, sems, False)
        if first_span == 0:
            pltpu.make_async_copy(w_ref, weights_out, sems.at[0]).start()

    k_ref[0, 0:TOP, :] = ctx_k_ref[0]
    v_ref[0, 0:TOP, :] = ctx_v_ref[0]
    k_ref[0, TOP + SPAN :, :] = jnp.zeros((16, D), BF16)
    v_ref[0, TOP + SPAN :, :] = jnp.zeros((16, D), BF16)
    n1 = n1_ref[...]
    for g in range(GROUPS):
        cols = slice(g * EG, (g + 1) * EG)
        q_ref[:, cols] = (dot(n1, w_ref[g, :, 0:EG]) * HEAD_DIM**-0.5).astype(BF16)
        k_ref[0, TOP : TOP + SPAN, cols] = dot(n1, w_ref[g, :, EG : 2 * EG]).astype(BF16)
        v_ref[0, TOP : TOP + SPAN, cols] = dot(n1, w_ref[g, :, 2 * EG : 3 * EG]).astype(BF16)

    even = iota((1, D), 1) % PAIR < HEAD_DIM
    zero = jnp.zeros((), BF16)
    for r0, rows in ((0, 144), (144, 144), (288, 128), (416, 128)):
        kb, vb = k_ref[0, r0 : r0 + rows, :], v_ref[0, r0 : r0 + rows, :]
        ke_ref[r0 : r0 + rows, :] = jnp.where(even, kb, zero)
        ko_ref[r0 : r0 + rows, :] = jnp.where(even, zero, kb)
        ve_ref[r0 : r0 + rows, :] = jnp.where(even, vb, zero)
        vo_ref[r0 : r0 + rows, :] = jnp.where(even, zero, vb)

    first_key = TOP - meta[5, span]
    for j in range(PAIRS):
        lanes = slice(j * PAIR, (j + 1) * PAIR)
        for rows, q0, w0 in FORWARD_BLOCKS:
            window = slice(w0, w0 + 128)
            keys = jnp.concatenate([ke_ref[window, lanes], ko_ref[window, lanes]], axis=0)
            scores = dot_nt(q_ref[q0 : q0 + rows, lanes], keys)
            if q0 == 480:
                r, c = iota((rows, 256), 0), iota((rows, 256), 1) % 128 - 64
                bias = jnp.where((c >= r + 6) & (c <= r + 18) & (c < 48), 0.0, NEGATIVE)
            else:
                bias = bias_ref[...]
            scores = scores + bias
            if q0 == 0:
                scores = jnp.where(iota((rows, 256), 1) % 128 >= first_key, scores, NEGATIVE)
            expo = []
            for half in (scores[:, :128], scores[:, 128:]):
                top = jnp.max(half, axis=-1, keepdims=True)
                expo.append(jnp.exp(half - top).astype(BF16))
            values = jnp.concatenate([ve_ref[window, lanes], vo_ref[window, lanes]], axis=0)
            values = jnp.concatenate([values, ones_ref[...]], axis=1)
            mixed = dot(jnp.concatenate(expo, axis=1), values)
            att_ref[q0 : q0 + rows, lanes] = (mixed[:, :PAIR] / mixed[:, PAIR:]).astype(BF16)

    att = att_ref[...]
    mid_ref[...] = dot_nt(att[:, :EG], w_ref[0, :, 3 * EG :]) + dot_nt(
        att[:, EG:], w_ref[1, :, 3 * EG :]
    )
    for r0 in range(0, SPAN, 128):
        masked, _ = masked_rows(meta, span, frames_ref, r0, 128)
        mid_ref[r0 : r0 + 128, :] = mid_ref[r0 : r0 + 128, :] + masked

    if first_span == 0:
        @pl.when(step == 0)
        def _():
            pltpu.make_async_copy(w_ref, weights_out, sems.at[0]).wait()


def spec(block, index, **kw):
    return pl.BlockSpec(block, index, **kw)


def params():
    return pltpu.CompilerParams(
        dimension_semantics=("arbitrary",), vmem_limit_bytes=VMEM_LIMIT
    )


def cost(micros, size):
    return pl.CostEstimate(flops=int(micros * 1.1e9), bytes_accessed=size, transcendentals=0)


def slot_count(pieces):
    return sum(piece.shape[0] for piece in pieces)


def row_block(first=0):
    return spec((SPAN, D), lambda s, m, p: (first + s, 0))


def fixed(shape):
    return spec(shape, lambda s, m, p: (0,) * len(shape))


def struct(shape, dtype):
    return jax.ShapeDtypeStruct(shape, dtype)


def attention_forward(
    meta, places, frames, ctx_k, ctx_v, norm, pieces, tokens, first_span, spans
):
    rows = spans * SPAN
    keys_block = spec((1, KEYS, D), lambda s, m, p: (s, 0, 0))
    top_block = spec((1, TOP, D), lambda s, m, p: (first_span + s, 0, 0))
    return pl.pallas_call(
        functools.partial(attention_forward_kernel, first_span, len(pieces), len(tokens)),
        grid_spec=pltpu.PrefetchScalarGridSpec(
            num_scalar_prefetch=2,
            grid=(spans,),
            in_specs=[
                spec((SPAN, D), lambda s, m, p: (m[0, 0] + first_span + s, 0)),
                top_block,
                top_block,
                fixed((8, D)),
            ]
            + [pl.BlockSpec(memory_space=pl.ANY)] * (len(pieces) + len(tokens)),
            out_specs=[
                row_block(), row_block(), keys_block, keys_block, row_block(), row_block()
            ]
            + [pl.BlockSpec(memory_space=pl.ANY)] * (first_span == 0),
            scratch_shapes=[
                pltpu.VMEM((GROUPS, D, 4 * EG), BF16),
                pltpu.SemaphoreType.DMA((slot_count(pieces),)),
                pltpu.VMEM((KEYS, D), BF16),
                pltpu.VMEM((KEYS, D), BF16),
                pltpu.VMEM((KEYS, D), BF16),
                pltpu.VMEM((KEYS, D), BF16),
                pltpu.VMEM((96, 256), F32),
                pltpu.VMEM((256, 128), BF16),
            ],
        ),
        out_shape=[
            struct((rows, D), BF16),
            struct((rows, D), BF16),
            struct((spans, KEYS, D), BF16),
            struct((spans, KEYS, D), BF16),
            struct((rows, D), BF16),
            struct((rows, D), F32),
        ]
        + [struct((GROUPS, D, 4 * EG), BF16)] * (first_span == 0),
        compiler_params=params(),
        cost_estimate=cost(4.5 * spans, rows * D * 14),
        name="attention_forward",
    )(meta, places, frames, ctx_k, ctx_v, norm, *pieces, *tokens)


FEED_WIDTH = 2 * FG + EG + EXTRA
ATTENTION_WIDTH = 3 * EG + EXTRA


def feed_forward_kernel(first, last, parts, count, meta, places, *refs):
    mid_ref, cot_ref, att_ref, norm_ref, inner_b_ref = refs[:5]
    slots_ref, refs = refs[5 : 5 + count], refs[5 + count :]
    if not first:
        (_, before_src, before_sums_ref, before_sums_b_ref), refs = refs[:4], refs[4:]
    (out_ref, chunk_ref, gm_ref), refs = refs[:3], refs[3:]
    if last:
        outs, refs = refs[: 2 * parts], refs[2 * parts :]
    else:
        outs, (left_sums_ref, left_sums_b_ref), refs = refs[:1], refs[1:3], refs[3:]
    if first and not last:
        weights_out, refs = refs[0], refs[1:]
    held, refs = refs[: len(outs) // 2 or 1], refs[len(outs) // 2 or 1 :]
    w_ref, sems, out_sems, n2_ref, cots_ref, gms_ref, atts_ref, hid_ref, gin_ref, dn_ref = refs[:10]
    result_ref, sums_ref, sums_b_ref = refs[10:13]
    refs = refs[13:]
    step = pl.program_id(0)
    here = pl.ds(pl.multiple_of(step * SPAN, SPAN), SPAN)

    @pl.when(step == 0)
    def _():
        load_weights(places, slots_ref, w_ref, sems, True)
        if first:
            sums_ref[...] = jnp.zeros_like(sums_ref)
            sums_b_ref[...] = jnp.zeros_like(sums_b_ref)
        else:
            pltpu.make_async_copy(before_src, refs[0], refs[1]).start()
            sums_ref[...] = before_sums_ref[...]
            sums_b_ref[...] = before_sums_b_ref[...]

    for r0 in range(0, SPAN, 128):
        xhat, _ = normalize(mid_ref[r0 : r0 + 128, :])
        place = pl.ds(pl.multiple_of(step * SPAN + r0, 128), 128)
        n2_ref[place, :] = (xhat * norm_ref[2:3, :] + norm_ref[3:4, :]).astype(BF16)
    cots_ref[here, :] = cot_ref[...]
    atts_ref[here, :] = att_ref[...]

    @pl.when(step == 0)
    def _():
        load_weights(places, slots_ref, w_ref, sems, False)
        if first and not last:
            pltpu.make_async_copy(w_ref, weights_out, sems.at[0]).start()

    chunk = 512
    for g in range(GROUPS):
        for c0 in range(0, FG, chunk):
            cols = slice(g * FG + c0, g * FG + c0 + chunk)
            act = dot(n2_ref[here, :], w_ref[g, :, c0 : c0 + chunk]) + inner_b_ref[0:1, cols]
            square = act * act
            tanh = jnp.tanh(act * (0.7978845608 + (0.7978845608 * 0.044715) * square))
            weight = 0.5 + 0.5 * tanh
            hidden = act * weight
            hid_ref[here, cols] = hidden.astype(BF16)
            slope = weight + (hidden - hidden * weight) * (
                2.0 * 0.7978845608 + (6.0 * 0.7978845608 * 0.044715) * square
            )
            grad = dot(cot_ref[...], w_ref[g, :, FG + c0 : FG + c0 + chunk]) * slope
            grad_low = grad.astype(BF16)
            gin_ref[here, cols] = grad_low
            sums_b_ref[:, cols] += fold_rows(grad)

    out = (
        mid_ref[...]
        + dot_nt(hid_ref[here, :FG], w_ref[0, :, FG:])
        + dot_nt(hid_ref[here, FG:], w_ref[1, :, FG:])
        + norm_ref[4:5, :]
    ).astype(BF16)
    out_ref[...] = out
    chunk_ref[...] = out
    dn_ref[...] = dot_nt(gin_ref[here, :FG], w_ref[0, :, :FG]) + dot_nt(
        gin_ref[here, FG:], w_ref[1, :, :FG]
    )

    for r0 in range(0, SPAN, 128):
        rows = slice(r0, r0 + 128)
        xhat, scale = normalize(mid_ref[rows, :])
        grad = dn_ref[rows, :]
        cot = cot_ref[rows, :].astype(F32)
        sums_ref[0:8, :] += fold_rows(grad * xhat)
        sums_ref[8:16, :] += fold_rows(grad)
        sums_ref[16:24, :] += fold_rows(cot)
        t = grad * norm_ref[2:3, :]
        gm = (cot + scale * (t - row_mean(t) - xhat * row_mean(t * xhat))).astype(BF16)
        gm_ref[rows, :] = gm
        gms_ref[pl.ds(pl.multiple_of(step * SPAN + r0, 128), 128), :] = gm

    @pl.when(step == pl.num_programs(0) - 1)
    def _():
        store = GradientStore(last, meta[0, 1], held, outs, out_sems)
        if first and not last:
            pltpu.make_async_copy(w_ref, weights_out, sems.at[0]).wait()
        if not first:
            pltpu.make_async_copy(before_src, refs[0], refs[1]).wait()
        if last:
            vectors = [column_sum(sums_ref[8 * i : 8 * i + 8, :]) for i in range(3)]
            for g in range(GROUPS):
                wide = column_sum(sums_b_ref[:, g * FG : (g + 1) * FG])
                result_ref[1, :, g * EXTRA : (g + 1) * EXTRA] = vector_block(
                    vectors, wide, 32
                ).astype(F32)
            store.put(
                result_ref.at[1],
                [(g, g * EXTRA, FEED_WIDTH - EXTRA, EXTRA) for g in range(GROUPS)],
            )
        else:
            left_sums_ref[...] = sums_ref[...]
            left_sums_b_ref[...] = sums_b_ref[...]
        jobs = [(n2_ref, gin_ref, 512 * c, [(c // 2, 0, 512 * (c % 2), 512)]) for c in range(4)]
        jobs += [
            (cots_ref, hid_ref, 512 * c, [(c // 2, 0, FG + 512 * (c % 2), 512)]) for c in range(4)
        ]
        jobs += [(gms_ref, atts_ref, 0, [(g, g * EG, 2 * FG, EG) for g in range(GROUPS)])]
        for number, (left, right, first_column, columns) in enumerate(jobs):
            result = dot_tn(left[...], right[:, first_column : first_column + 512])
            buffer = result_ref.at[number % 2]
            if first:
                buffer[...] = result
            else:
                for g, source, target, width in columns:
                    buffer[:, source : source + width] = result[
                        :, source : source + width
                    ] + refs[0][g, :, target : target + width].astype(F32)
            store.put(buffer, columns)
        store.finish()


def feed_forward(
    meta, places, mid, cot, att, norm, inner_b, pieces, before, first_span, spans, last, parts
):
    rows = spans * SPAN
    first = not before
    whole = pl.BlockSpec(memory_space=pl.ANY)
    whole_rows = spec((SPAN, D), lambda s, m, p: (m[0, 0] + first_span + s, 0))
    in_specs = [row_block(first_span), whole_rows, row_block(first_span), fixed((8, D)), fixed((1, FF))]
    in_specs += [whole] * len(pieces)
    args = [mid, cot, att, norm, inner_b, *pieces]
    aliases = {}
    held, out_sems, shapes = gradient_buffers(last, parts, FEED_WIDTH if last else FEED_WIDTH - EXTRA, 10)
    low = pltpu.VMEM((rows, D), BF16)
    scratch = held + [
        pltpu.VMEM((GROUPS, D, 2 * FG), BF16),
        pltpu.SemaphoreType.DMA((slot_count(pieces),)),
        out_sems,
        low,
        low,
        low,
        low,
        pltpu.VMEM((rows, FF), BF16),
        pltpu.VMEM((rows, FF), BF16),
        pltpu.VMEM((SPAN, D), F32),
        pltpu.VMEM((2, D, 512), F32),
        pltpu.VMEM((24, D), F32),
        pltpu.VMEM((8, FF), F32),
    ]
    if not first:
        aliases = {2 + len(args): 0}
        in_specs += [whole, whole, fixed((24, D)), fixed((8, FF))]
        args += before
        scratch += [
            pltpu.VMEM((GROUPS, D, FEED_WIDTH - EXTRA), BF16), pltpu.SemaphoreType.DMA(())
        ]
    out_specs = [whole_rows, row_block(), row_block()] + [whole] * len(shapes)
    out_shape = [struct(cot.shape, BF16), struct((rows, D), BF16), struct((rows, D), BF16)]
    out_shape += shapes
    if not last:
        out_specs += [fixed((24, D)), fixed((8, FF))]
        out_shape += [struct((24, D), F32), struct((8, FF), F32)]
    if first and not last:
        out_specs += [whole]
        out_shape += [struct((GROUPS, D, 2 * FG), BF16)]
    outs = pl.pallas_call(
        functools.partial(feed_forward_kernel, first, last, parts, len(pieces)),
        grid_spec=pltpu.PrefetchScalarGridSpec(
            num_scalar_prefetch=2,
            grid=(spans,),
            in_specs=in_specs,
            out_specs=out_specs,
            scratch_shapes=scratch,
        ),
        out_shape=out_shape,
        input_output_aliases=aliases,
        compiler_params=params(),
        cost_estimate=cost(11 * spans, rows * D * 10),
        name="feed_forward",
    )(meta, places, *args)
    return outs[0], outs[1], outs[2], outs[3:]


def gradient_outs(parts, width):
    shape = (GROUPS, 8, D // 16 // parts, width)
    return [fixed(shape)] * (2 * parts), [struct(shape, BF16)] * (2 * parts)


def attention_backward_kernel(
    first, last, parts, cuts, first_span, meta, places, *refs
):
    frames_ref, n1_ref, q_ref, k_ref, v_ref, gm_ref, norm_ref, weights_ref = refs[:8]
    refs = refs[8:]
    if not first:
        (_, before_ref, before_sums_ref), refs = refs[:3], refs[3:]
    gf_ref, chunk_refs, gctx_ref = refs[0], refs[1 : 1 + len(cuts)], refs[1 + len(cuts)]
    refs = refs[2 + len(cuts) :]
    if last:
        keeps, sends, refs = refs[:parts], refs[parts : 2 * parts], refs[2 * parts :]
    else:
        (grad_ref, left_sums_ref), refs = refs[:2], refs[2:]
    w_ref, sems, gatt_ref, dq_ref, dk_ref, dv_ref, dkb_ref, dvb_ref = refs[:8]
    n1t_ref, dn_ref, bias_ref, acc_ref, sums_ref = refs[8:13]
    refs = refs[13:]
    step = pl.program_id(0)
    span = meta[0, 0] + first_span + step

    @pl.when(step == 0)
    def _():
        load_weights(places, [weights_ref], w_ref, sems, True)
        acc_ref[...] = jnp.zeros_like(acc_ref)
        if first:
            sums_ref[...] = jnp.zeros_like(sums_ref)
        else:
            pltpu.make_async_copy(before_ref, refs[0], refs[1]).start()
            sums_ref[...] = before_sums_ref[...]
        r, c = iota((160, 256), 0), iota((160, 256), 1) % 128
        bias_ref[...] = jnp.where((r >= c + 6) & (r <= c + 18), 0.0, NEGATIVE)

    n1t_ref[...] = n1_ref[...].T

    @pl.when(step == 0)
    def _():
        load_weights(places, [weights_ref], w_ref, sems, False)

    for g in range(GROUPS):
        gatt_ref[:, g * EG : (g + 1) * EG] = dot(gm_ref[...], w_ref[g, :, 3 * EG :]).astype(BF16)

    first_key = TOP - meta[5, span]
    even = low_half()
    zero = jnp.zeros((), BF16)
    for j in range(PAIRS):
        lanes = slice(j * PAIR, (j + 1) * PAIR)
        for b in range(SPAN // 128):
            rows, window = slice(128 * b, 128 * b + 128), slice(128 * b, 128 * b + 160)
            kw, vw = k_ref[0, window, lanes], v_ref[0, window, lanes]
            qb, ob = q_ref[rows, lanes], gatt_ref[rows, lanes]
            qs = jnp.concatenate([jnp.where(even, qb, zero), jnp.where(even, zero, qb)], axis=0)
            os = jnp.concatenate([jnp.where(even, ob, zero), jnp.where(even, zero, ob)], axis=0)
            scores = dot_nt(kw, qs) + bias_ref[...]
            if b == 0:
                scores = jnp.where(iota((160, 256), 0) >= first_key, scores, NEGATIVE)
            if b == SPAN // 128 - 1:
                scores = jnp.where(iota((160, 256), 0) < 144, scores, NEGATIVE)
            expo = jnp.exp(scores - jnp.max(scores, axis=0, keepdims=True))
            probs = expo * (1.0 / jnp.sum(expo, axis=0, keepdims=True))
            grad_probs = dot_nt(vw, os)
            delta = jnp.sum(probs * grad_probs, axis=0, keepdims=True)
            ds = (probs * (grad_probs - delta)).astype(BF16)
            dv = dot(probs.astype(BF16), os)
            dk = dot(ds, qs)
            if b == 0:
                dkb_ref[window, lanes] = dk
                dvb_ref[window, lanes] = dv
            else:
                lap, rest = slice(128 * b, 128 * b + 32), slice(128 * b + 32, 128 * b + 160)
                dkb_ref[lap, lanes] += dk[:32]
                dvb_ref[lap, lanes] += dv[:32]
                dkb_ref[rest, lanes] = dk[32:]
                dvb_ref[rest, lanes] = dv[32:]
            dq = dot_tn(ds, kw)
            dq = jnp.where(even, dq[:128], dq[128:]) * HEAD_DIM**-0.5
            dq_ref[rows, lanes] = dq.astype(BF16)
    for g in range(GROUPS):
        gctx_ref[g, 0, 0] = dkb_ref[0:TOP, g * EG : (g + 1) * EG]
        gctx_ref[g, 1, 0] = dvb_ref[0:TOP, g * EG : (g + 1) * EG]
    dk_ref[...] = dkb_ref[TOP : TOP + SPAN, :].astype(BF16)
    dv_ref[...] = dvb_ref[TOP : TOP + SPAN, :].astype(BF16)

    for g in range(GROUPS):
        cols = slice(g * EG, (g + 1) * EG)
        acc_ref[g, :, 0:EG] += dot(n1t_ref[...], dq_ref[:, cols])
        acc_ref[g, :, EG : 2 * EG] += dot(n1t_ref[...], dk_ref[:, cols])
        acc_ref[g, :, 2 * EG : 3 * EG] += dot(n1t_ref[...], dv_ref[:, cols])
    total = None
    for g in range(GROUPS):
        cols = slice(g * EG, (g + 1) * EG)
        for m, ref in enumerate((dq_ref, dk_ref, dv_ref)):
            term = dot_nt(ref[:, cols], w_ref[g, :, m * EG : (m + 1) * EG])
            total = term if total is None else total + term
    dn_ref[...] = total
    for r0 in range(0, SPAN, 128):
        rows = slice(r0, r0 + 128)
        masked, keep = masked_rows(meta, span, frames_ref, r0, 128)
        xhat, scale = normalize(masked)
        grad = dn_ref[rows, :]
        sums_ref[0:8, :] += fold_rows(grad * xhat)
        sums_ref[8:16, :] += fold_rows(grad)
        t = grad * norm_ref[0:1, :]
        back = scale * (t - row_mean(t) - xhat * row_mean(t * xhat))
        result = ((gm_ref[rows, :].astype(F32) + back) * keep).astype(BF16)
        gf_ref[rows, :] = result
        column = 0
        for chunk_ref in chunk_refs:
            width = chunk_ref.shape[1]
            chunk_ref[rows, :] = result[:, column : column + width]
            column += width

    @pl.when(step == pl.num_programs(0) - 1)
    def _():
        if not first:
            pltpu.make_async_copy(before_ref, refs[0], refs[1]).wait()
            for g in range(GROUPS):
                acc_ref[g] += refs[0][g].astype(F32)
        if not last:
            for g in range(GROUPS):
                grad_ref[g] = acc_ref[g].astype(BF16)
            left_sums_ref[...] = sums_ref[...]
        else:
            split_core(meta[0, 1], acc_ref, keeps, sends, 3 * EG)
            vectors = [column_sum(sums_ref[8 * i : 8 * i + 8, :]) for i in range(2)]
            block = vector_block(vectors, None, 2 * 16).astype(F32)
            for g in range(GROUPS):
                refs[-1][g] = block
            split_extra(meta[0, 1], refs[-1], keeps, sends, 3 * EG)


def attention_backward(
    meta, places, frames, kept, gm, norm, weights, before, first_span, spans, last, parts, cuts
):
    rows = spans * SPAN
    first = not before
    whole = pl.BlockSpec(memory_space=pl.ANY)
    whole_rows = spec((SPAN, D), lambda s, m, p: (m[0, 0] + first_span + s, 0))
    keys_block = spec((1, KEYS, D), lambda s, m, p: (first_span + s, 0, 0))
    kept_rows = row_block(first_span)
    low = pltpu.VMEM((SPAN, D), BF16)
    in_specs = [
        whole_rows, kept_rows, kept_rows, keys_block, keys_block, row_block(), fixed((8, D)),
        whole,
    ]
    args = [frames, *kept, gm, norm, weights]
    aliases = {}
    scratch = [
        pltpu.VMEM((GROUPS, D, 4 * EG), BF16),
        pltpu.SemaphoreType.DMA((1,)),
        low,
        low,
        low,
        low,
        pltpu.VMEM((KEYS, D), F32),
        pltpu.VMEM((KEYS, D), F32),
        low,
        pltpu.VMEM((SPAN, D), F32),
        pltpu.VMEM((160, 256), F32),
        pltpu.VMEM((GROUPS, D, 3 * EG), F32),
        pltpu.VMEM((16, D), F32),
    ]
    if not first:
        aliases = {2 + len(args): 0}
        in_specs += [whole, whole, fixed((16, D))]
        args += before
        scratch += [pltpu.VMEM((GROUPS, D, 3 * EG), BF16), pltpu.SemaphoreType.DMA(())]
    out_specs = [
        whole_rows,
        *[spec((SPAN, cut), lambda s, m, p: (s, 0)) for cut in cuts],
        spec((GROUPS, 2, 1, TOP, EG), lambda s, m, p: (0, 0, s, 0, 0)),
    ]
    out_shape = [
        struct(frames.shape, BF16),
        *[struct((rows, cut), BF16) for cut in cuts],
        struct((GROUPS, 2, spans, TOP, EG), F32),
    ]
    if last:
        more_specs, more_shapes = gradient_outs(parts, ATTENTION_WIDTH)
        scratch += [pltpu.VMEM((GROUPS, D, EXTRA), F32)]
    else:
        more_specs = [fixed((GROUPS, D, 3 * EG)), fixed((16, D))]
        more_shapes = [struct((GROUPS, D, 3 * EG), BF16), struct((16, D), F32)]
    outs = pl.pallas_call(
        functools.partial(attention_backward_kernel, first, last, parts, cuts, first_span),
        grid_spec=pltpu.PrefetchScalarGridSpec(
            num_scalar_prefetch=2,
            grid=(spans,),
            in_specs=in_specs,
            out_specs=out_specs + more_specs,
            scratch_shapes=scratch,
        ),
        out_shape=out_shape + more_shapes,
        input_output_aliases=aliases,
        compiler_params=params(),
        cost_estimate=cost(10 * spans, rows * D * 14),
        name="attention_backward",
    )(meta, places, *args)
    count = len(cuts)
    return outs[0], outs[1 : 1 + count], outs[1 + count], outs[2 + count :]


BITS = {"core": ("dp", 1), "y": ("dp", 2), "z1": ("dp", 4), "z2": ("dp", 8), "x": ("tensor", 1)}
BIT_DIM = {"x": 0, "z2": 1, "z1": 2, "y": 3}


def swap(value, bits, flips=(1, 1)):
    bits = (bits,) if isinstance(bits, str) else bits
    axis = BITS[bits[0]][0]
    distance = sum(BITS[bit][1] * flip for bit, flip in zip(bits, flips))
    return lax.ppermute(value, axis, [(i, i ^ distance) for i in range(lax.axis_size(axis))])


def my_bit(bit):
    axis, distance = BITS[bit]
    return (lax.axis_index(axis) // distance) % 2


def tie(value, *tokens):
    return lax.optimization_barrier((value, tokens))[0]


def piece_places(order, rows, first):
    groups, firsts = [], []
    dp, tensor = lax.axis_index("dp"), lax.axis_index("tensor")
    for j in range(2 ** len(order)):
        dp_flip = sum(BITS[b][1] for i, b in enumerate(order) if j >> i & 1 and b != "x")
        x_flip = sum(1 for i, b in enumerate(order) if j >> i & 1 and b == "x")
        groups.append(tensor ^ x_flip)
        firsts.append((dp ^ dp_flip) * rows + first)
    return jnp.stack([jnp.stack(groups), jnp.stack(firsts)]).astype(jnp.int32)


class Gather:
    def __init__(self, piece, shared, orders):
        self.shared, self.orders = shared, orders
        self.rows = piece.shape[0]
        self.part = self.rows // len(orders)
        self.held = [piece[None]]
        self.got = None
        self.step = 0
        self.steps = len(shared) + len(orders[0])

    def after(self, *tokens):
        if self.got is None:
            self.held = list(tie(tuple(self.held), *tokens))
        else:
            self.got = list(tie(tuple(self.got), *tokens))

    def exchange(self):
        if self.got is not None:
            self.held = [jnp.concatenate(pair, axis=0) for pair in zip(self.held, self.got)]
        if self.step < len(self.shared):
            bits = self.shared[self.step]
            if len(bits) == 2:
                held = self.held[0]
                flips = [(1, 0), (0, 1), (1, 1)]
                self.got = [jnp.concatenate([swap(held, bits, flip) for flip in flips], axis=0)]
                self.step += 1
                return
            bits = [bits[0]]
        else:
            if self.step == len(self.shared):
                whole = self.held[0]
                self.held = [
                    whole[:, h * self.part : (h + 1) * self.part] for h in range(len(self.orders))
                ]
            bits = [order[self.step - len(self.shared)] for order in self.orders]
        self.got = [swap(held, bit) for held, bit in zip(self.held, bits)]
        self.step += 1

    def result(self):
        return [array for pair in zip(self.held, self.got) for array in pair]

    def places(self):
        return jnp.concatenate(
            [
                piece_places(sum(self.shared, ()) + order, self.rows, h * self.part)
                for h, order in enumerate(self.orders)
            ],
            axis=1,
        )


class Scatter:
    def __init__(self, keeps_sends, stages):
        parts = len(stages)
        self.stages = stages
        self.rows, self.columns = keeps_sends[0].shape[2:]
        shape = (2, 2, 2, 2, self.rows, self.columns)
        self.terms = [
            [keep.reshape(shape), swap(send, "core").reshape(shape)]
            for keep, send in zip(keeps_sends[:parts], keeps_sends[parts:])
        ]
        self.step = 0

    def after(self, *tokens):
        self.terms = tie(self.terms, *tokens)

    def kept(self):
        return [terms[0] for terms in self.terms]

    def exchange(self):
        for h, stage in enumerate(self.stages):
            bits = stage[self.step]

            def block(flips):
                total = 0.0
                for term in self.terms[h]:
                    for bit, flip in zip(bits, flips):
                        place = my_bit(bit) ^ flip
                        term = lax.dynamic_index_in_dim(term, place, BIT_DIM[bit], keepdims=True)
                    total = total + term.astype(F32)
                return total.astype(BF16)

            flips = [(1,)] if len(bits) == 1 else [(1, 0), (0, 1), (1, 1)]
            got = [swap(block(flip), bits, flip) for flip in flips]
            self.terms[h] = [block((0,) * len(bits)), *got]
        self.step += 1


def finish_sums(scatters, *others):
    mine = my_bit("x")
    keeps, sends = [], []
    for scatter in scatters:
        for place, blocks in ((mine, keeps), (1 - mine, sends)):
            parts = []
            for terms in scatter.terms:
                total = sum(
                    lax.dynamic_index_in_dim(term, place, 0, keepdims=False).astype(F32)
                    for term in terms
                )
                parts.append(total.reshape(scatter.rows, scatter.columns))
            blocks.append(jnp.concatenate(parts, axis=0))
    got = swap(jnp.concatenate(sends, axis=1).astype(BF16), "x").astype(F32)
    others = [swap(other, "x") for other in others]
    results, first = [], 0
    for keep in keeps:
        results.append(keep + got[:, first : first + keep.shape[1]])
        first += keep.shape[1]
    return (*results, *others)


ATTENTION_SHARED = (("z2", "z1"),)
FEED_SHARED = (("z2",), ("z1",))
ATTENTION_ORDERS = (("y", "x", "core"), ("x", "y", "core"))
FEED_ORDERS = (("y", "x", "core"), ("x", "y", "core"))
ATTENTION_SUMS = ((("y", "z1"), ("z2",)),)
FEED_SUMS = ((("y",), ("z1",), ("z2",)), (("z1",), ("z2",), ("y",)))


def body(
    frames,
    context_keys,
    context_values,
    time_start,
    time_width,
    freq_start,
    freq_width,
    context_count,
    gain_one,
    shift_one,
    query_w,
    key_w,
    value_w,
    out_w,
    gain_two,
    shift_two,
    inner_w,
    inner_b,
    outer_w,
    outer_b,
    cotangent,
):
    tensor, dp = lax.axis_size("tensor"), lax.axis_size("dp")
    tuned = tensor == 2 and dp == 16
    spans = time_start.shape[0] // tensor
    t_index = lax.axis_index("tensor")
    base = t_index * spans

    def pick(first, second):
        return jnp.where(t_index == 0, first, second)

    attention_piece = jnp.concatenate([query_w, key_w, value_w, out_w.T], axis=1)
    feed_piece = jnp.concatenate([inner_w, outer_w.T], axis=1)
    context = jnp.stack([context_keys, context_values])
    if tuned:
        gather = Gather(attention_piece, ATTENTION_SHARED, ATTENTION_ORDERS)
        feed_gather = Gather(feed_piece, FEED_SHARED, FEED_ORDERS)
        gather.exchange()
        feed_gather.held[0] = feed_gather.held[0] + 0.0 * gather.got[0][0, 0, 0]
        feed_gather.exchange()
        gather.exchange()
        gather.exchange()
        feed_gather.exchange()
        context, inner_b = tie((context, inner_b), *feed_gather.got)
        mine = lax.dynamic_slice_in_dim(context, base, spans, 1)
        theirs = swap(lax.dynamic_slice_in_dim(context, (1 - t_index) * spans, spans, 1), "x")
        context = pick(
            jnp.concatenate([mine, theirs], axis=3), jnp.concatenate([theirs, mine], axis=3)
        )
        other_b = swap(inner_b, "x")
        inner_b_full = pick(
            jnp.concatenate([inner_b, other_b]), jnp.concatenate([other_b, inner_b])
        ).reshape(1, FF)
        gather.after(*feed_gather.got)
        gather.exchange()
        feed_gather.exchange()
        attention_pieces, attention_places = gather.result(), gather.places()
        feed_places = feed_gather.places()
    else:
        def canonical(parts, width):
            grouped = []
            for part in parts:
                whole = lax.all_gather(part, "dp", axis=0, tiled=True)
                whole = lax.all_gather(whole, "tensor", axis=1, tiled=True)
                grouped.append(whole.reshape(D, GROUPS, width).swapaxes(0, 1))
            return [jnp.concatenate(grouped, axis=2)]

        attention_pieces = canonical((query_w, key_w, value_w, out_w.T), EG)
        feed_pieces = canonical((inner_w, outer_w.T), FG)
        attention_places = feed_places = jnp.array([[0, 1], [0, 0]], jnp.int32)
        context = lax.all_to_all(context, "tensor", split_axis=1, concat_axis=3, tiled=True)
        inner_b_full = lax.all_gather(inner_b, "tensor", axis=0, tiled=True).reshape(1, FF)
    context = jnp.pad(context, ((0, 0), (0, 0), (TOP - LEFT, 0), (0, 0)))

    core_bit = my_bit("core") if tuned else 0
    first_row = jnp.zeros_like(time_start).at[0].set(base).at[1].set(core_bit)
    meta = jnp.stack(
        [first_row, time_start, time_width, freq_start, freq_width, context_count]
    ).astype(jnp.int32)
    norm = jnp.stack(
        [gain_one, shift_one, gain_two, shift_two, outer_b] + [jnp.zeros_like(gain_one)] * 3
    )

    chunk = min(CHUNK, spans)
    firsts = range(0, spans, chunk)
    final = spans - chunk

    def exchange(value):
        return swap(value, "x") if tuned else value

    if tuned:
        meta = tie(meta, inner_b_full, attention_places, feed_places, feed_gather.got)
        feed_gather.exchange()
    n1, q, k, v, att, mid, weights = attention_forward(
        meta, attention_places, frames, context[0], context[1], norm, attention_pieces, [], 0, spans
    )
    if tuned:
        feed_gather.after(n1)
        feed_gather.exchange()
        feed_pieces = feed_gather.result()
    outs, gms, before, feed_weights = [], [], [], None
    parts = len(FEED_SUMS) if tuned else 1
    for first in firsts:
        pieces = feed_pieces if feed_weights is None else [feed_weights]
        output, part, gm, rest = feed_forward(
            meta, feed_places, mid, cotangent, att, norm, inner_b_full, pieces, before,
            first, chunk, first == final, parts,
        )
        if first == 0 and first != final:
            *rest, feed_weights = rest
        outs.append(exchange(part))
        gms.append(gm)
        before = [output, *rest]
    feed_grad = rest
    frame_parts, contexts, before = [], [], []
    parts = len(ATTENTION_SUMS) if tuned else 1
    if tuned:
        feed_grad = list(tie(tuple(feed_grad), outs[0]))
        feed_scatter = Scatter(feed_grad, FEED_SUMS)
        feed_scatter.exchange()
    for index, (first, gm) in enumerate(zip(firsts, gms)):
        own_meta = meta
        if tuned:
            own_meta = tie(meta, *feed_scatter.kept(), *(outs[-1:] if index > 0 else []))
        cuts = (3 * D // 4, D // 4) if tuned and first == final else (D,)
        grad_frames, pieces, gctx, rest = attention_backward(
            own_meta, attention_places, frames, (n1, q, k, v), gm, norm, weights, before, first, chunk,
            first == final, parts, cuts,
        )
        frame_parts.append([exchange(piece) for piece in pieces])
        contexts.append(gctx)
        before = [grad_frames, *rest]
        if tuned and index == 0:
            feed_scatter.after(grad_frames)
            feed_scatter.exchange()
    attention_grad = rest
    if tuned:
        attention_grad = list(tie(tuple(attention_grad), frame_parts[:-1], feed_scatter.terms))
        attention_scatter = Scatter(attention_grad, ATTENTION_SUMS)
        output, grad_frames = tie((output, grad_frames), attention_scatter.terms)
        feed_scatter.exchange()
        attention_scatter.after(*feed_scatter.kept())
        attention_scatter.exchange()
        feed_scatter.after(attention_scatter.terms)
        attention_scatter.after(frame_parts[-1][0])
        attention_scatter.exchange()
        (feed_sum,) = finish_sums([feed_scatter])
        attention_scatter.terms, frame_parts[-1], contexts = tie(
            (attention_scatter.terms, frame_parts[-1], contexts)
        )

    if tuned:
        def both(whole, parts):
            for first, pieces in zip(firsts, parts):
                place, column = ((1 - t_index) * spans + first) * SPAN, 0
                for piece in pieces:
                    whole = lax.dynamic_update_slice(whole, piece, (place, column))
                    column += piece.shape[1]
            return whole

        output = both(output, [[part] for part in outs])
        grad_frames = both(grad_frames, frame_parts)
        gctx = jnp.concatenate(contexts, axis=2)[:, :, :, TOP - LEFT :]
        mine, theirs = (
            lax.dynamic_index_in_dim(gctx, place, 0, keepdims=False)
            for place in (t_index, 1 - t_index)
        )
        attention_sum, theirs = finish_sums([attention_scatter], theirs)
        grad_context = pick(
            jnp.concatenate([mine, theirs], axis=1), jnp.concatenate([theirs, mine], axis=1)
        )
        extra = feed_sum[:4, FEED_WIDTH - EXTRA :]
        sum_gain_two, sum_shift_two, sum_outer_b = (extra[i, :32] for i in range(3))
        sum_inner_b = extra[3, :64]
        sum_gain_one, sum_shift_one = (
            attention_sum[i, 3 * EG : 3 * EG + 32] for i in range(2)
        )
        sum_query, sum_key, sum_value = (
            attention_sum[:, i * EG : (i + 1) * EG] for i in range(3)
        )
        sum_inner, sum_outer = feed_sum[:, :FG], feed_sum[:, FG : 2 * FG]
        sum_out = feed_sum[:, 2 * FG : 2 * FG + EG]
    else:
        def both(parts):
            return lax.all_gather(jnp.concatenate(parts, axis=0), "tensor", axis=0, tiled=True)

        output = both(outs)
        grad_frames = both([piece for (piece,) in frame_parts])
        gctx = jnp.concatenate(contexts, axis=2)[:, :, :, TOP - LEFT :]
        grad_context = jnp.moveaxis(gctx, 0, 3).reshape(2, spans, LEFT, D)
        grad_context = lax.all_to_all(
            grad_context, "tensor", split_axis=3, concat_axis=1, tiled=True
        )
        attention_grad, feed_grad = (
            jnp.stack(pair, axis=2).reshape(GROUPS, D, -1) for pair in (attention_grad, feed_grad)
        )

        def whole_grad(grad, index, width):
            return grad[:, :, index * width : (index + 1) * width].swapaxes(0, 1).reshape(D, -1)

        def scattered(grad):
            part = lax.psum_scatter(grad, "dp", scatter_dimension=0, tiled=True)
            return lax.psum_scatter(part, "tensor", scatter_dimension=1, tiled=True).astype(F32)

        def summed(item):
            item = lax.psum(item, "tensor")
            return lax.psum_scatter(item, "dp", scatter_dimension=0, tiled=True)

        def vector(grad, index):
            item = grad[0, :, -EXTRA:].reshape(16, 32, EXTRA)[:, index, :32].reshape(D)
            return summed(item.astype(F32))

        sum_query, sum_key, sum_value = (
            scattered(whole_grad(attention_grad, i, EG)) for i in range(3)
        )
        sum_inner, sum_outer = (scattered(whole_grad(feed_grad, i, FG)) for i in range(2))
        sum_out = scattered(feed_grad[:, :, 2 * FG : 2 * FG + EG].swapaxes(0, 1).reshape(D, -1))
        sum_gain_one, sum_shift_one = (vector(attention_grad, i) for i in range(2))
        sum_gain_two, sum_shift_two, sum_outer_b = (vector(feed_grad, i) for i in range(3))
        sum_inner_b = feed_grad[:, :, -EXTRA:].reshape(GROUPS, 16, 32, EXTRA)[:, :, 3, :64]
        sum_inner_b = sum_inner_b.reshape(FF).astype(F32)
        sum_inner_b = lax.psum_scatter(sum_inner_b, "tensor", scatter_dimension=0, tiled=True)
        sum_inner_b = lax.psum_scatter(sum_inner_b, "dp", scatter_dimension=0, tiled=True)

    return (
        output,
        grad_frames,
        grad_context[0],
        grad_context[1],
        sum_gain_one,
        sum_shift_one,
        sum_query,
        sum_key,
        sum_value,
        sum_out.T,
        sum_gain_two,
        sum_shift_two,
        sum_inner,
        sum_inner_b,
        sum_outer.T,
        sum_outer_b,
    )


def solution(mesh):
    in_specs = (
        P("dp", None),
        P("dp", None, "tensor"),
        P("dp", None, "tensor"),
        P("dp"),
        P("dp"),
        P("dp"),
        P("dp"),
        P("dp"),
        P(),
        P(),
        P("dp", "tensor"),
        P("dp", "tensor"),
        P("dp", "tensor"),
        P("tensor", "dp"),
        P(),
        P(),
        P("dp", "tensor"),
        P("tensor"),
        P("tensor", "dp"),
        P(),
        P("dp", None),
    )
    out_specs = (
        P("dp", None),
        P("dp", None),
        P("dp", None, "tensor"),
        P("dp", None, "tensor"),
        P("dp"),
        P("dp"),
        P("dp", "tensor"),
        P("dp", "tensor"),
        P("dp", "tensor"),
        P("tensor", "dp"),
        P("dp"),
        P("dp"),
        P("dp", "tensor"),
        P(("tensor", "dp")),
        P("tensor", "dp"),
        P("dp"),
    )
    return jax.shard_map(body, mesh=mesh, in_specs=in_specs, out_specs=out_specs, check_vma=False)
```

```python
import functools

import jax
import jax.numpy as jnp
from jax import lax
from jax.experimental import pallas as pl
from jax.experimental.pallas import tpu as pltpu
from jax.sharding import PartitionSpec as P

D = 512
HEAD_DIM = 64
SPAN = 512
LEFT = 10
RIGHT = 2
FF = 2048
PAIR = 2 * HEAD_DIM
PAIRS = D // PAIR
GROUPS = 2
EG = D // GROUPS
FG = FF // GROUPS
TOP = 16
KEYS = TOP + SPAN + 16
EXTRA = 128
CHUNK = 2
NEGATIVE = -1e30
epsilon = 1e-05
F32 = jnp.float32
BF16 = jnp.bfloat16
VMEM_LIMIT = 56 * 1024 * 1024
FORWARD_BLOCKS = tuple((96, 96 * b, 96 * b) for b in range(5)) + ((32, 480, 416),)


def dot(a, b):
    return lax.dot_general(a, b, (((1,), (0,)), ((), ())), preferred_element_type=F32)


def dot_nt(a, b):
    return lax.dot_general(a, b, (((1,), (1,)), ((), ())), preferred_element_type=F32)


def dot_tn(a, b):
    return lax.dot_general(a, b, (((0,), (0,)), ((), ())), preferred_element_type=F32)


def iota(shape, dim):
    return lax.broadcasted_iota(jnp.int32, shape, dim)


def row_mean(v):
    return jnp.sum(v, axis=-1, keepdims=True) * (1.0 / D)


def normalize(v):
    center = v - row_mean(v)
    scale = lax.rsqrt(row_mean(center * center) + epsilon)
    return center * scale, scale


def fold_rows(v):
    total = v[0:8]
    for r in range(8, v.shape[0], 8):
        total = total + v[r : r + 8]
    return total


def masked_rows(meta, span, frames_ref, row0, rows):
    places = iota((rows, 1), 0) + row0
    hide_t = (places >= meta[1, span]) & (places < meta[1, span] + meta[2, span])
    columns = iota((1, D), 1)
    hide_f = (columns >= meta[3, span]) & (columns < meta[3, span] + meta[4, span])
    keep = jnp.where(hide_t, 0.0, 1.0) * jnp.where(hide_f, 0.0, 1.0)
    return frames_ref[pl.ds(row0, rows), :].astype(F32) * keep, keep


def load_slots(places, pieces, w_ref, sems, start):
    j = 0
    for piece in pieces:
        for i in range(piece.shape[0]):
            copy = pltpu.make_async_copy(
                piece.at[i],
                w_ref.at[
                    places[0, j], pl.ds(pl.multiple_of(places[1, j], 16), piece.shape[1]), :
                ],
                sems.at[j],
            )
            if start:
                copy.start()
            else:
                copy.wait()
            j += 1


def load_weights(places, pieces, w_ref, sems, start):
    if len(pieces) > 1 or pieces[0].shape != w_ref.shape:
        load_slots(places, pieces, w_ref, sems, start)
        return
    copy = pltpu.make_async_copy(pieces[0], w_ref, sems.at[0])
    if start:
        copy.start()
    else:
        copy.wait()


def vector_block(rows_of, wide, own_rows):
    blocks = D // own_rows
    r, c = iota((D, D), 0), iota((D, D), 1)
    value = jnp.zeros((D, D), F32)
    for i, vector in enumerate(rows_of):
        value = jnp.where(r % own_rows == i, vector, value)
    value = jnp.where(r // own_rows == c // own_rows, value, 0.0).astype(BF16)
    pick = jnp.where(iota((D, EXTRA), 0) % own_rows == iota((D, EXTRA), 1), 1.0, 0.0)
    block = dot(value, pick.astype(BF16))
    if wide is not None:
        width = wide.shape[1]
        share = width // blocks
        r, c = iota((D, width), 0), iota((D, width), 1)
        here = (r // own_rows == c // share) & (r % own_rows == len(rows_of))
        value = jnp.where(here, wide, 0.0).astype(BF16)
        pick = jnp.where(iota((width, EXTRA), 0) % share == iota((width, EXTRA), 1), 1.0, 0.0)
        block = block + dot(value, pick.astype(BF16))
    return block.astype(BF16)


def column_sum(v):
    return jnp.sum(v, axis=0, keepdims=True)


def split_core(core_bit, grad_ref, keeps, sends, width):
    blocks, part = keeps[0].shape[1], keeps[0].shape[2]
    rows = D // (2 * blocks)
    for outs, bit in ((keeps, core_bit), (sends, 1 - core_bit)):
        for i in range(blocks):
            first = pl.multiple_of((2 * i + bit) * rows, 16)
            for h, out in enumerate(outs):
                for g in range(GROUPS):
                    out[g, i, :, :width] = grad_ref[g, pl.ds(first + h * part, part), :width].astype(BF16)


def split_extra(core_bit, block_ref, keeps, sends, width):
    blocks, part = keeps[0].shape[1], keeps[0].shape[2]
    rows = D // (2 * blocks)
    for outs, bit in ((keeps, core_bit), (sends, 1 - core_bit)):
        for i in range(blocks):
            first = pl.multiple_of((2 * i + bit) * rows, 16)
            for h, out in enumerate(outs):
                for g in range(GROUPS):
                    value = block_ref[g, pl.ds(first + h * part, part), :]
                    out[g, i, :, width:] = value.astype(BF16)


class GradientStore:
    def __init__(self, last, core_bit, held, outs, sems):
        self.last, self.core_bit, self.held, self.outs, self.sems = last, core_bit, held, outs, sems
        self.jobs = []

    def copies(self, number, columns):
        for g, _, target, width in columns:
            cols = pl.ds(target, width)
            if not self.last:
                yield pltpu.make_async_copy(
                    self.held[0].at[g, :, cols], self.outs[0].at[g, :, cols],
                    self.sems.at[number, 0, 0, g],
                )
                continue
            parts = len(self.held)
            for h, held in enumerate(self.held):
                for side in range(2):
                    yield pltpu.make_async_copy(
                        held.at[side, g, :, :, cols],
                        self.outs[h + side * parts].at[g, :, :, cols],
                        self.sems.at[number, h, side, g],
                    )

    def put(self, result_ref, columns):
        for g, source, target, width in columns:
            if not self.last:
                self.held[0][g, :, target : target + width] = result_ref[
                    :, source : source + width
                ].astype(BF16)
                continue
            for h, held in enumerate(self.held):
                blocks, part = held.shape[2], held.shape[3]
                rows = D // (2 * blocks)
                for side, bit in ((0, self.core_bit), (1, 1 - self.core_bit)):
                    for i in range(blocks):
                        first = pl.multiple_of((2 * i + bit) * rows + h * part, 16)
                        held[side, g, i, :, target : target + width] = result_ref[
                            pl.ds(first, part), source : source + width
                        ].astype(BF16)
        number = len(self.jobs)
        self.jobs.append(columns)
        for copy in self.copies(number, columns):
            copy.start()

    def finish(self):
        for number, columns in enumerate(self.jobs):
            for copy in self.copies(number, columns):
                copy.wait()


def gradient_buffers(last, parts, width, jobs):
    if not last:
        shapes = [struct((GROUPS, D, width), BF16)]
        held = [pltpu.VMEM((GROUPS, D, width), BF16)]
    else:
        part = D // 16 // parts
        shapes = [struct((GROUPS, 8, part, width), BF16)] * (2 * parts)
        held = [pltpu.VMEM((2, GROUPS, 8, part, width), BF16)] * parts
    sems = pltpu.SemaphoreType.DMA((jobs, parts if last else 1, 2, GROUPS))
    return held, sems, shapes


def low_half():
    return iota((1, PAIR), 1) < HEAD_DIM


def attention_forward_kernel(first_span, count, tokens, meta, places, *refs):
    frames_ref, ctx_k_ref, ctx_v_ref, norm_ref = refs[:4]
    slots_ref, refs = refs[4 : 4 + count], refs[4 + count + tokens :]
    n1_ref, q_ref, k_ref, v_ref, att_ref, mid_ref = refs[:6]
    if first_span == 0:
        weights_out, refs = refs[6], refs[7:]
    else:
        refs = refs[6:]
    w_ref, sems, ke_ref, ko_ref, ve_ref, vo_ref, bias_ref, ones_ref = refs
    step = pl.program_id(0)
    span = meta[0, 0] + first_span + step

    @pl.when(step == 0)
    def _():
        load_weights(places, slots_ref, w_ref, sems, True)
        r, c = iota((96, 256), 0), iota((96, 256), 1) % 128
        bias_ref[...] = jnp.where((c >= r + 6) & (c <= r + 18), 0.0, NEGATIVE)
        r, c = iota((256, 128), 0), iota((256, 128), 1)
        ones_ref[...] = jnp.where((r < 128) == (c < 64), 1.0, 0.0).astype(BF16)

    for r0 in range(0, SPAN, 128):
        masked, _ = masked_rows(meta, span, frames_ref, r0, 128)
        xhat, _ = normalize(masked)
        n1_ref[r0 : r0 + 128, :] = (xhat * norm_ref[0:1, :] + norm_ref[1:2, :]).astype(BF16)

    @pl.when(step == 0)
    def _():
        load_weights(places, slots_ref, w_ref, sems, False)
        if first_span == 0:
            pltpu.make_async_copy(w_ref, weights_out, sems.at[0]).start()

    k_ref[0, 0:TOP, :] = ctx_k_ref[0]
    v_ref[0, 0:TOP, :] = ctx_v_ref[0]
    k_ref[0, TOP + SPAN :, :] = jnp.zeros((16, D), BF16)
    v_ref[0, TOP + SPAN :, :] = jnp.zeros((16, D), BF16)
    n1 = n1_ref[...]
    for g in range(GROUPS):
        cols = slice(g * EG, (g + 1) * EG)
        q_ref[:, cols] = (dot(n1, w_ref[g, :, 0:EG]) * HEAD_DIM**-0.5).astype(BF16)
        k_ref[0, TOP : TOP + SPAN, cols] = dot(n1, w_ref[g, :, EG : 2 * EG]).astype(BF16)
        v_ref[0, TOP : TOP + SPAN, cols] = dot(n1, w_ref[g, :, 2 * EG : 3 * EG]).astype(BF16)

    even = iota((1, D), 1) % PAIR < HEAD_DIM
    zero = jnp.zeros((), BF16)
    for r0, rows in ((0, 144), (144, 144), (288, 128), (416, 128)):
        kb, vb = k_ref[0, r0 : r0 + rows, :], v_ref[0, r0 : r0 + rows, :]
        ke_ref[r0 : r0 + rows, :] = jnp.where(even, kb, zero)
        ko_ref[r0 : r0 + rows, :] = jnp.where(even, zero, kb)
        ve_ref[r0 : r0 + rows, :] = jnp.where(even, vb, zero)
        vo_ref[r0 : r0 + rows, :] = jnp.where(even, zero, vb)

    first_key = TOP - meta[5, span]
    for j in range(PAIRS):
        lanes = slice(j * PAIR, (j + 1) * PAIR)
        for rows, q0, w0 in FORWARD_BLOCKS:
            window = slice(w0, w0 + 128)
            keys = jnp.concatenate([ke_ref[window, lanes], ko_ref[window, lanes]], axis=0)
            scores = dot_nt(q_ref[q0 : q0 + rows, lanes], keys)
            if q0 == 480:
                r, c = iota((rows, 256), 0), iota((rows, 256), 1) % 128 - 64
                bias = jnp.where((c >= r + 6) & (c <= r + 18) & (c < 48), 0.0, NEGATIVE)
            else:
                bias = bias_ref[...]
            scores = scores + bias
            if q0 == 0:
                scores = jnp.where(iota((rows, 256), 1) % 128 >= first_key, scores, NEGATIVE)
            expo = []
            for half in (scores[:, :128], scores[:, 128:]):
                top = jnp.max(half, axis=-1, keepdims=True)
                expo.append(jnp.exp(half - top).astype(BF16))
            values = jnp.concatenate([ve_ref[window, lanes], vo_ref[window, lanes]], axis=0)
            values = jnp.concatenate([values, ones_ref[...]], axis=1)
            mixed = dot(jnp.concatenate(expo, axis=1), values)
            att_ref[q0 : q0 + rows, lanes] = (mixed[:, :PAIR] / mixed[:, PAIR:]).astype(BF16)

    att = att_ref[...]
    mid_ref[...] = dot_nt(att[:, :EG], w_ref[0, :, 3 * EG :]) + dot_nt(
        att[:, EG:], w_ref[1, :, 3 * EG :]
    )
    for r0 in range(0, SPAN, 128):
        masked, _ = masked_rows(meta, span, frames_ref, r0, 128)
        mid_ref[r0 : r0 + 128, :] = mid_ref[r0 : r0 + 128, :] + masked

    if first_span == 0:
        @pl.when(step == 0)
        def _():
            pltpu.make_async_copy(w_ref, weights_out, sems.at[0]).wait()


def spec(block, index, **kw):
    return pl.BlockSpec(block, index, **kw)


def params():
    return pltpu.CompilerParams(
        dimension_semantics=("arbitrary",), vmem_limit_bytes=VMEM_LIMIT
    )


def cost(micros, size):
    return pl.CostEstimate(flops=int(micros * 1.1e9), bytes_accessed=size, transcendentals=0)


def slot_count(pieces):
    return sum(piece.shape[0] for piece in pieces)


def row_block(first=0):
    return spec((SPAN, D), lambda s, m, p: (first + s, 0))


def fixed(shape):
    return spec(shape, lambda s, m, p: (0,) * len(shape))


def struct(shape, dtype):
    return jax.ShapeDtypeStruct(shape, dtype)


def attention_forward(
    meta, places, frames, ctx_k, ctx_v, norm, pieces, tokens, first_span, spans
):
    rows = spans * SPAN
    keys_block = spec((1, KEYS, D), lambda s, m, p: (s, 0, 0))
    top_block = spec((1, TOP, D), lambda s, m, p: (first_span + s, 0, 0))
    return pl.pallas_call(
        functools.partial(attention_forward_kernel, first_span, len(pieces), len(tokens)),
        grid_spec=pltpu.PrefetchScalarGridSpec(
            num_scalar_prefetch=2,
            grid=(spans,),
            in_specs=[
                spec((SPAN, D), lambda s, m, p: (m[0, 0] + first_span + s, 0)),
                top_block,
                top_block,
                fixed((8, D)),
            ]
            + [pl.BlockSpec(memory_space=pl.ANY)] * (len(pieces) + len(tokens)),
            out_specs=[
                row_block(), row_block(), keys_block, keys_block, row_block(), row_block()
            ]
            + [pl.BlockSpec(memory_space=pl.ANY)] * (first_span == 0),
            scratch_shapes=[
                pltpu.VMEM((GROUPS, D, 4 * EG), BF16),
                pltpu.SemaphoreType.DMA((slot_count(pieces),)),
                pltpu.VMEM((KEYS, D), BF16),
                pltpu.VMEM((KEYS, D), BF16),
                pltpu.VMEM((KEYS, D), BF16),
                pltpu.VMEM((KEYS, D), BF16),
                pltpu.VMEM((96, 256), F32),
                pltpu.VMEM((256, 128), BF16),
            ],
        ),
        out_shape=[
            struct((rows, D), BF16),
            struct((rows, D), BF16),
            struct((spans, KEYS, D), BF16),
            struct((spans, KEYS, D), BF16),
            struct((rows, D), BF16),
            struct((rows, D), F32),
        ]
        + [struct((GROUPS, D, 4 * EG), BF16)] * (first_span == 0),
        compiler_params=params(),
        cost_estimate=cost(4.5 * spans, rows * D * 14),
        name="attention_forward",
    )(meta, places, frames, ctx_k, ctx_v, norm, *pieces, *tokens)


FEED_WIDTH = 2 * FG + EG + EXTRA
ATTENTION_WIDTH = 3 * EG + EXTRA


def feed_forward_kernel(first, last, parts, count, meta, places, *refs):
    mid_ref, cot_ref, att_ref, norm_ref, inner_b_ref = refs[:5]
    slots_ref, refs = refs[5 : 5 + count], refs[5 + count :]
    if not first:
        (_, before_src, before_sums_ref, before_sums_b_ref), refs = refs[:4], refs[4:]
    (out_ref, chunk_ref, gm_ref), refs = refs[:3], refs[3:]
    if last:
        outs, refs = refs[: 2 * parts], refs[2 * parts :]
    else:
        outs, (left_sums_ref, left_sums_b_ref), refs = refs[:1], refs[1:3], refs[3:]
    if first and not last:
        weights_out, refs = refs[0], refs[1:]
    held, refs = refs[: len(outs) // 2 or 1], refs[len(outs) // 2 or 1 :]
    w_ref, sems, out_sems, n2_ref, cots_ref, gms_ref, atts_ref, hid_ref, gin_ref, dn_ref = refs[:10]
    result_ref, sums_ref, sums_b_ref = refs[10:13]
    refs = refs[13:]
    step = pl.program_id(0)
    here = pl.ds(pl.multiple_of(step * SPAN, SPAN), SPAN)

    @pl.when(step == 0)
    def _():
        load_weights(places, slots_ref, w_ref, sems, True)
        if first:
            sums_ref[...] = jnp.zeros_like(sums_ref)
            sums_b_ref[...] = jnp.zeros_like(sums_b_ref)
        else:
            pltpu.make_async_copy(before_src, refs[0], refs[1]).start()
            sums_ref[...] = before_sums_ref[...]
            sums_b_ref[...] = before_sums_b_ref[...]

    for r0 in range(0, SPAN, 128):
        xhat, _ = normalize(mid_ref[r0 : r0 + 128, :])
        place = pl.ds(pl.multiple_of(step * SPAN + r0, 128), 128)
        n2_ref[place, :] = (xhat * norm_ref[2:3, :] + norm_ref[3:4, :]).astype(BF16)
    cots_ref[here, :] = cot_ref[...]
    atts_ref[here, :] = att_ref[...]

    @pl.when(step == 0)
    def _():
        load_weights(places, slots_ref, w_ref, sems, False)
        if first and not last:
            pltpu.make_async_copy(w_ref, weights_out, sems.at[0]).start()

    chunk = 512
    for g in range(GROUPS):
        for c0 in range(0, FG, chunk):
            cols = slice(g * FG + c0, g * FG + c0 + chunk)
            act = dot(n2_ref[here, :], w_ref[g, :, c0 : c0 + chunk]) + inner_b_ref[0:1, cols]
            square = act * act
            tanh = jnp.tanh(act * (0.7978845608 + (0.7978845608 * 0.044715) * square))
            weight = 0.5 + 0.5 * tanh
            hidden = act * weight
            hid_ref[here, cols] = hidden.astype(BF16)
            slope = weight + (hidden - hidden * weight) * (
                2.0 * 0.7978845608 + (6.0 * 0.7978845608 * 0.044715) * square
            )
            grad = dot(cot_ref[...], w_ref[g, :, FG + c0 : FG + c0 + chunk]) * slope
            grad_low = grad.astype(BF16)
            gin_ref[here, cols] = grad_low
            sums_b_ref[:, cols] += fold_rows(grad)

    out = (
        mid_ref[...]
        + dot_nt(hid_ref[here, :FG], w_ref[0, :, FG:])
        + dot_nt(hid_ref[here, FG:], w_ref[1, :, FG:])
        + norm_ref[4:5, :]
    ).astype(BF16)
    out_ref[...] = out
    chunk_ref[...] = out
    dn_ref[...] = dot_nt(gin_ref[here, :FG], w_ref[0, :, :FG]) + dot_nt(
        gin_ref[here, FG:], w_ref[1, :, :FG]
    )

    for r0 in range(0, SPAN, 128):
        rows = slice(r0, r0 + 128)
        xhat, scale = normalize(mid_ref[rows, :])
        grad = dn_ref[rows, :]
        cot = cot_ref[rows, :].astype(F32)
        sums_ref[0:8, :] += fold_rows(grad * xhat)
        sums_ref[8:16, :] += fold_rows(grad)
        sums_ref[16:24, :] += fold_rows(cot)
        t = grad * norm_ref[2:3, :]
        gm = (cot + scale * (t - row_mean(t) - xhat * row_mean(t * xhat))).astype(BF16)
        gm_ref[rows, :] = gm
        gms_ref[pl.ds(pl.multiple_of(step * SPAN + r0, 128), 128), :] = gm

    @pl.when(step == pl.num_programs(0) - 1)
    def _():
        store = GradientStore(last, meta[0, 1], held, outs, out_sems)
        if first and not last:
            pltpu.make_async_copy(w_ref, weights_out, sems.at[0]).wait()
        if not first:
            pltpu.make_async_copy(before_src, refs[0], refs[1]).wait()
        if last:
            vectors = [column_sum(sums_ref[8 * i : 8 * i + 8, :]) for i in range(3)]
            for g in range(GROUPS):
                wide = column_sum(sums_b_ref[:, g * FG : (g + 1) * FG])
                result_ref[1, :, g * EXTRA : (g + 1) * EXTRA] = vector_block(
                    vectors, wide, 32
                ).astype(F32)
            store.put(
                result_ref.at[1],
                [(g, g * EXTRA, FEED_WIDTH - EXTRA, EXTRA) for g in range(GROUPS)],
            )
        else:
            left_sums_ref[...] = sums_ref[...]
            left_sums_b_ref[...] = sums_b_ref[...]
        jobs = [(n2_ref, gin_ref, 512 * c, [(c // 2, 0, 512 * (c % 2), 512)]) for c in range(4)]
        jobs += [
            (cots_ref, hid_ref, 512 * c, [(c // 2, 0, FG + 512 * (c % 2), 512)]) for c in range(4)
        ]
        jobs += [(gms_ref, atts_ref, 0, [(g, g * EG, 2 * FG, EG) for g in range(GROUPS)])]
        for number, (left, right, first_column, columns) in enumerate(jobs):
            result = dot_tn(left[...], right[:, first_column : first_column + 512])
            buffer = result_ref.at[number % 2]
            if first:
                buffer[...] = result
            else:
                for g, source, target, width in columns:
                    buffer[:, source : source + width] = result[
                        :, source : source + width
                    ] + refs[0][g, :, target : target + width].astype(F32)
            store.put(buffer, columns)
        store.finish()


def feed_forward(
    meta, places, mid, cot, att, norm, inner_b, pieces, before, first_span, spans, last, parts
):
    rows = spans * SPAN
    first = not before
    whole = pl.BlockSpec(memory_space=pl.ANY)
    whole_rows = spec((SPAN, D), lambda s, m, p: (m[0, 0] + first_span + s, 0))
    in_specs = [row_block(first_span), whole_rows, row_block(first_span), fixed((8, D)), fixed((1, FF))]
    in_specs += [whole] * len(pieces)
    args = [mid, cot, att, norm, inner_b, *pieces]
    aliases = {}
    held, out_sems, shapes = gradient_buffers(last, parts, FEED_WIDTH if last else FEED_WIDTH - EXTRA, 10)
    low = pltpu.VMEM((rows, D), BF16)
    scratch = held + [
        pltpu.VMEM((GROUPS, D, 2 * FG), BF16),
        pltpu.SemaphoreType.DMA((slot_count(pieces),)),
        out_sems,
        low,
        low,
        low,
        low,
        pltpu.VMEM((rows, FF), BF16),
        pltpu.VMEM((rows, FF), BF16),
        pltpu.VMEM((SPAN, D), F32),
        pltpu.VMEM((2, D, 512), F32),
        pltpu.VMEM((24, D), F32),
        pltpu.VMEM((8, FF), F32),
    ]
    if not first:
        aliases = {2 + len(args): 0}
        in_specs += [whole, whole, fixed((24, D)), fixed((8, FF))]
        args += before
        scratch += [
            pltpu.VMEM((GROUPS, D, FEED_WIDTH - EXTRA), BF16), pltpu.SemaphoreType.DMA(())
        ]
    out_specs = [whole_rows, row_block(), row_block()] + [whole] * len(shapes)
    out_shape = [struct(cot.shape, BF16), struct((rows, D), BF16), struct((rows, D), BF16)]
    out_shape += shapes
    if not last:
        out_specs += [fixed((24, D)), fixed((8, FF))]
        out_shape += [struct((24, D), F32), struct((8, FF), F32)]
    if first and not last:
        out_specs += [whole]
        out_shape += [struct((GROUPS, D, 2 * FG), BF16)]
    outs = pl.pallas_call(
        functools.partial(feed_forward_kernel, first, last, parts, len(pieces)),
        grid_spec=pltpu.PrefetchScalarGridSpec(
            num_scalar_prefetch=2,
            grid=(spans,),
            in_specs=in_specs,
            out_specs=out_specs,
            scratch_shapes=scratch,
        ),
        out_shape=out_shape,
        input_output_aliases=aliases,
        compiler_params=params(),
        cost_estimate=cost(11 * spans, rows * D * 10),
        name="feed_forward",
    )(meta, places, *args)
    return outs[0], outs[1], outs[2], outs[3:]


def gradient_outs(parts, width):
    shape = (GROUPS, 8, D // 16 // parts, width)
    return [fixed(shape)] * (2 * parts), [struct(shape, BF16)] * (2 * parts)


def attention_backward_kernel(
    first, last, parts, cuts, first_span, meta, places, *refs
):
    frames_ref, n1_ref, q_ref, k_ref, v_ref, gm_ref, norm_ref, weights_ref = refs[:8]
    refs = refs[8:]
    if not first:
        (_, before_ref, before_sums_ref), refs = refs[:3], refs[3:]
    gf_ref, chunk_refs, gctx_ref = refs[0], refs[1 : 1 + len(cuts)], refs[1 + len(cuts)]
    refs = refs[2 + len(cuts) :]
    if last:
        keeps, sends, refs = refs[:parts], refs[parts : 2 * parts], refs[2 * parts :]
    else:
        (grad_ref, left_sums_ref), refs = refs[:2], refs[2:]
    w_ref, sems, gatt_ref, dq_ref, dk_ref, dv_ref, dkb_ref, dvb_ref = refs[:8]
    n1t_ref, dn_ref, bias_ref, acc_ref, sums_ref = refs[8:13]
    refs = refs[13:]
    step = pl.program_id(0)
    span = meta[0, 0] + first_span + step

    @pl.when(step == 0)
    def _():
        load_weights(places, [weights_ref], w_ref, sems, True)
        acc_ref[...] = jnp.zeros_like(acc_ref)
        if first:
            sums_ref[...] = jnp.zeros_like(sums_ref)
        else:
            pltpu.make_async_copy(before_ref, refs[0], refs[1]).start()
            sums_ref[...] = before_sums_ref[...]
        r, c = iota((160, 256), 0), iota((160, 256), 1) % 128
        bias_ref[...] = jnp.where((r >= c + 6) & (r <= c + 18), 0.0, NEGATIVE)

    n1t_ref[...] = n1_ref[...].T

    @pl.when(step == 0)
    def _():
        load_weights(places, [weights_ref], w_ref, sems, False)

    for g in range(GROUPS):
        gatt_ref[:, g * EG : (g + 1) * EG] = dot(gm_ref[...], w_ref[g, :, 3 * EG :]).astype(BF16)

    first_key = TOP - meta[5, span]
    even = low_half()
    zero = jnp.zeros((), BF16)
    for j in range(PAIRS):
        lanes = slice(j * PAIR, (j + 1) * PAIR)
        for b in range(SPAN // 128):
            rows, window = slice(128 * b, 128 * b + 128), slice(128 * b, 128 * b + 160)
            kw, vw = k_ref[0, window, lanes], v_ref[0, window, lanes]
            qb, ob = q_ref[rows, lanes], gatt_ref[rows, lanes]
            qs = jnp.concatenate([jnp.where(even, qb, zero), jnp.where(even, zero, qb)], axis=0)
            os = jnp.concatenate([jnp.where(even, ob, zero), jnp.where(even, zero, ob)], axis=0)
            scores = dot_nt(kw, qs) + bias_ref[...]
            if b == 0:
                scores = jnp.where(iota((160, 256), 0) >= first_key, scores, NEGATIVE)
            if b == SPAN // 128 - 1:
                scores = jnp.where(iota((160, 256), 0) < 144, scores, NEGATIVE)
            expo = jnp.exp(scores - jnp.max(scores, axis=0, keepdims=True))
            probs = expo * (1.0 / jnp.sum(expo, axis=0, keepdims=True))
            grad_probs = dot_nt(vw, os)
            delta = jnp.sum(probs * grad_probs, axis=0, keepdims=True)
            ds = (probs * (grad_probs - delta)).astype(BF16)
            dv = dot(probs.astype(BF16), os)
            dk = dot(ds, qs)
            if b == 0:
                dkb_ref[window, lanes] = dk
                dvb_ref[window, lanes] = dv
            else:
                lap, rest = slice(128 * b, 128 * b + 32), slice(128 * b + 32, 128 * b + 160)
                dkb_ref[lap, lanes] += dk[:32]
                dvb_ref[lap, lanes] += dv[:32]
                dkb_ref[rest, lanes] = dk[32:]
                dvb_ref[rest, lanes] = dv[32:]
            dq = dot_tn(ds, kw)
            dq = jnp.where(even, dq[:128], dq[128:]) * HEAD_DIM**-0.5
            dq_ref[rows, lanes] = dq.astype(BF16)
    for g in range(GROUPS):
        gctx_ref[g, 0, 0] = dkb_ref[0:TOP, g * EG : (g + 1) * EG]
        gctx_ref[g, 1, 0] = dvb_ref[0:TOP, g * EG : (g + 1) * EG]
    dk_ref[...] = dkb_ref[TOP : TOP + SPAN, :].astype(BF16)
    dv_ref[...] = dvb_ref[TOP : TOP + SPAN, :].astype(BF16)

    for g in range(GROUPS):
        cols = slice(g * EG, (g + 1) * EG)
        acc_ref[g, :, 0:EG] += dot(n1t_ref[...], dq_ref[:, cols])
        acc_ref[g, :, EG : 2 * EG] += dot(n1t_ref[...], dk_ref[:, cols])
        acc_ref[g, :, 2 * EG : 3 * EG] += dot(n1t_ref[...], dv_ref[:, cols])
    total = None
    for g in range(GROUPS):
        cols = slice(g * EG, (g + 1) * EG)
        for m, ref in enumerate((dq_ref, dk_ref, dv_ref)):
            term = dot_nt(ref[:, cols], w_ref[g, :, m * EG : (m + 1) * EG])
            total = term if total is None else total + term
    dn_ref[...] = total
    for r0 in range(0, SPAN, 128):
        rows = slice(r0, r0 + 128)
        masked, keep = masked_rows(meta, span, frames_ref, r0, 128)
        xhat, scale = normalize(masked)
        grad = dn_ref[rows, :]
        sums_ref[0:8, :] += fold_rows(grad * xhat)
        sums_ref[8:16, :] += fold_rows(grad)
        t = grad * norm_ref[0:1, :]
        back = scale * (t - row_mean(t) - xhat * row_mean(t * xhat))
        result = ((gm_ref[rows, :].astype(F32) + back) * keep).astype(BF16)
        gf_ref[rows, :] = result
        column = 0
        for chunk_ref in chunk_refs:
            width = chunk_ref.shape[1]
            chunk_ref[rows, :] = result[:, column : column + width]
            column += width

    @pl.when(step == pl.num_programs(0) - 1)
    def _():
        if not first:
            pltpu.make_async_copy(before_ref, refs[0], refs[1]).wait()
            for g in range(GROUPS):
                acc_ref[g] += refs[0][g].astype(F32)
        if not last:
            for g in range(GROUPS):
                grad_ref[g] = acc_ref[g].astype(BF16)
            left_sums_ref[...] = sums_ref[...]
        else:
            split_core(meta[0, 1], acc_ref, keeps, sends, 3 * EG)
            vectors = [column_sum(sums_ref[8 * i : 8 * i + 8, :]) for i in range(2)]
            block = vector_block(vectors, None, 2 * 16).astype(F32)
            for g in range(GROUPS):
                refs[-1][g] = block
            split_extra(meta[0, 1], refs[-1], keeps, sends, 3 * EG)


def attention_backward(
    meta, places, frames, kept, gm, norm, weights, before, first_span, spans, last, parts, cuts
):
    rows = spans * SPAN
    first = not before
    whole = pl.BlockSpec(memory_space=pl.ANY)
    whole_rows = spec((SPAN, D), lambda s, m, p: (m[0, 0] + first_span + s, 0))
    keys_block = spec((1, KEYS, D), lambda s, m, p: (first_span + s, 0, 0))
    kept_rows = row_block(first_span)
    low = pltpu.VMEM((SPAN, D), BF16)
    in_specs = [
        whole_rows, kept_rows, kept_rows, keys_block, keys_block, row_block(), fixed((8, D)),
        whole,
    ]
    args = [frames, *kept, gm, norm, weights]
    aliases = {}
    scratch = [
        pltpu.VMEM((GROUPS, D, 4 * EG), BF16),
        pltpu.SemaphoreType.DMA((1,)),
        low,
        low,
        low,
        low,
        pltpu.VMEM((KEYS, D), F32),
        pltpu.VMEM((KEYS, D), F32),
        low,
        pltpu.VMEM((SPAN, D), F32),
        pltpu.VMEM((160, 256), F32),
        pltpu.VMEM((GROUPS, D, 3 * EG), F32),
        pltpu.VMEM((16, D), F32),
    ]
    if not first:
        aliases = {2 + len(args): 0}
        in_specs += [whole, whole, fixed((16, D))]
        args += before
        scratch += [pltpu.VMEM((GROUPS, D, 3 * EG), BF16), pltpu.SemaphoreType.DMA(())]
    out_specs = [
        whole_rows,
        *[spec((SPAN, cut), lambda s, m, p: (s, 0)) for cut in cuts],
        spec((GROUPS, 2, 1, TOP, EG), lambda s, m, p: (0, 0, s, 0, 0)),
    ]
    out_shape = [
        struct(frames.shape, BF16),
        *[struct((rows, cut), BF16) for cut in cuts],
        struct((GROUPS, 2, spans, TOP, EG), F32),
    ]
    if last:
        more_specs, more_shapes = gradient_outs(parts, ATTENTION_WIDTH)
        scratch += [pltpu.VMEM((GROUPS, D, EXTRA), F32)]
    else:
        more_specs = [fixed((GROUPS, D, 3 * EG)), fixed((16, D))]
        more_shapes = [struct((GROUPS, D, 3 * EG), BF16), struct((16, D), F32)]
    outs = pl.pallas_call(
        functools.partial(attention_backward_kernel, first, last, parts, cuts, first_span),
        grid_spec=pltpu.PrefetchScalarGridSpec(
            num_scalar_prefetch=2,
            grid=(spans,),
            in_specs=in_specs,
            out_specs=out_specs + more_specs,
            scratch_shapes=scratch,
        ),
        out_shape=out_shape + more_shapes,
        input_output_aliases=aliases,
        compiler_params=params(),
        cost_estimate=cost(10 * spans, rows * D * 14),
        name="attention_backward",
    )(meta, places, *args)
    count = len(cuts)
    return outs[0], outs[1 : 1 + count], outs[1 + count], outs[2 + count :]


BITS = {"core": ("dp", 1), "y": ("dp", 2), "z1": ("dp", 4), "z2": ("dp", 8), "x": ("tensor", 1)}
BIT_DIM = {"x": 0, "z2": 1, "z1": 2, "y": 3}


def swap(value, bits, flips=(1, 1)):
    bits = (bits,) if isinstance(bits, str) else bits
    axis = BITS[bits[0]][0]
    distance = sum(BITS[bit][1] * flip for bit, flip in zip(bits, flips))
    return lax.ppermute(value, axis, [(i, i ^ distance) for i in range(lax.axis_size(axis))])


def my_bit(bit):
    axis, distance = BITS[bit]
    return (lax.axis_index(axis) // distance) % 2


def tie(value, *tokens):
    return lax.optimization_barrier((value, tokens))[0]


def piece_places(order, rows, first):
    groups, firsts = [], []
    dp, tensor = lax.axis_index("dp"), lax.axis_index("tensor")
    for j in range(2 ** len(order)):
        dp_flip = sum(BITS[b][1] for i, b in enumerate(order) if j >> i & 1 and b != "x")
        x_flip = sum(1 for i, b in enumerate(order) if j >> i & 1 and b == "x")
        groups.append(tensor ^ x_flip)
        firsts.append((dp ^ dp_flip) * rows + first)
    return jnp.stack([jnp.stack(groups), jnp.stack(firsts)]).astype(jnp.int32)


class Gather:
    def __init__(self, piece, shared, orders):
        self.shared, self.orders = shared, orders
        self.rows = piece.shape[0]
        self.part = self.rows // len(orders)
        self.held = [piece[None]]
        self.got = None
        self.step = 0
        self.steps = len(shared) + len(orders[0])

    def after(self, *tokens):
        if self.got is None:
            self.held = list(tie(tuple(self.held), *tokens))
        else:
            self.got = list(tie(tuple(self.got), *tokens))

    def exchange(self):
        if self.got is not None:
            self.held = [jnp.concatenate(pair, axis=0) for pair in zip(self.held, self.got)]
        if self.step < len(self.shared):
            bits = self.shared[self.step]
            if len(bits) == 2:
                held = self.held[0]
                flips = [(1, 0), (0, 1), (1, 1)]
                self.got = [jnp.concatenate([swap(held, bits, flip) for flip in flips], axis=0)]
                self.step += 1
                return
            bits = [bits[0]]
        else:
            if self.step == len(self.shared):
                whole = self.held[0]
                self.held = [
                    whole[:, h * self.part : (h + 1) * self.part] for h in range(len(self.orders))
                ]
            bits = [order[self.step - len(self.shared)] for order in self.orders]
        self.got = [swap(held, bit) for held, bit in zip(self.held, bits)]
        self.step += 1

    def result(self):
        return [array for pair in zip(self.held, self.got) for array in pair]

    def places(self):
        return jnp.concatenate(
            [
                piece_places(sum(self.shared, ()) + order, self.rows, h * self.part)
                for h, order in enumerate(self.orders)
            ],
            axis=1,
        )


class Scatter:
    def __init__(self, keeps_sends, stages):
        parts = len(stages)
        self.stages = stages
        self.rows, self.columns = keeps_sends[0].shape[2:]
        shape = (2, 2, 2, 2, self.rows, self.columns)
        self.terms = [
            [keep.reshape(shape), swap(send, "core").reshape(shape)]
            for keep, send in zip(keeps_sends[:parts], keeps_sends[parts:])
        ]
        self.step = 0

    def after(self, *tokens):
        self.terms = tie(self.terms, *tokens)

    def kept(self):
        return [terms[0] for terms in self.terms]

    def exchange(self):
        for h, stage in enumerate(self.stages):
            bits = stage[self.step]

            def block(flips):
                total = 0.0
                for term in self.terms[h]:
                    for bit, flip in zip(bits, flips):
                        place = my_bit(bit) ^ flip
                        term = lax.dynamic_index_in_dim(term, place, BIT_DIM[bit], keepdims=True)
                    total = total + term.astype(F32)
                return total.astype(BF16)

            flips = [(1,)] if len(bits) == 1 else [(1, 0), (0, 1), (1, 1)]
            got = [swap(block(flip), bits, flip) for flip in flips]
            self.terms[h] = [block((0,) * len(bits)), *got]
        self.step += 1


def finish_sums(scatters, *others):
    mine = my_bit("x")
    keeps, sends = [], []
    for scatter in scatters:
        for place, blocks in ((mine, keeps), (1 - mine, sends)):
            parts = []
            for terms in scatter.terms:
                total = sum(
                    lax.dynamic_index_in_dim(term, place, 0, keepdims=False).astype(F32)
                    for term in terms
                )
                parts.append(total.reshape(scatter.rows, scatter.columns))
            blocks.append(jnp.concatenate(parts, axis=0))
    got = swap(jnp.concatenate(sends, axis=1).astype(BF16), "x").astype(F32)
    others = [swap(other, "x") for other in others]
    results, first = [], 0
    for keep in keeps:
        results.append(keep + got[:, first : first + keep.shape[1]])
        first += keep.shape[1]
    return (*results, *others)


ATTENTION_SHARED = (("z2", "z1"),)
FEED_SHARED = (("z2",), ("z1",))
ATTENTION_ORDERS = (("y", "x", "core"), ("x", "y", "core"))
FEED_ORDERS = (("y", "x", "core"), ("x", "y", "core"))
ATTENTION_SUMS = ((("y", "z1"), ("z2",)),)
FEED_SUMS = ((("y",), ("z1",), ("z2",)), (("z1",), ("z2",), ("y",)))


def body(
    frames,
    context_keys,
    context_values,
    time_start,
    time_width,
    freq_start,
    freq_width,
    context_count,
    gain_one,
    shift_one,
    query_w,
    key_w,
    value_w,
    out_w,
    gain_two,
    shift_two,
    inner_w,
    inner_b,
    outer_w,
    outer_b,
    cotangent,
):
    tensor, dp = lax.axis_size("tensor"), lax.axis_size("dp")
    tuned = tensor == 2 and dp == 16
    spans = time_start.shape[0] // tensor
    t_index = lax.axis_index("tensor")
    base = t_index * spans

    def pick(first, second):
        return jnp.where(t_index == 0, first, second)

    attention_piece = jnp.concatenate([query_w, key_w, value_w, out_w.T], axis=1)
    feed_piece = jnp.concatenate([inner_w, outer_w.T], axis=1)
    context = jnp.stack([context_keys, context_values])
    if tuned:
        gather = Gather(attention_piece, ATTENTION_SHARED, ATTENTION_ORDERS)
        feed_gather = Gather(feed_piece, FEED_SHARED, FEED_ORDERS)
        gather.exchange()
        feed_gather.held[0] = feed_gather.held[0] + 0.0 * gather.got[0][0, 0, 0]
        feed_gather.exchange()
        gather.exchange()
        gather.exchange()
        feed_gather.exchange()
        context, inner_b = tie((context, inner_b), *feed_gather.got)
        mine = lax.dynamic_slice_in_dim(context, base, spans, 1)
        theirs = swap(lax.dynamic_slice_in_dim(context, (1 - t_index) * spans, spans, 1), "x")
        context = pick(
            jnp.concatenate([mine, theirs], axis=3), jnp.concatenate([theirs, mine], axis=3)
        )
        other_b = swap(inner_b, "x")
        inner_b_full = pick(
            jnp.concatenate([inner_b, other_b]), jnp.concatenate([other_b, inner_b])
        ).reshape(1, FF)
        gather.after(*feed_gather.got)
        gather.exchange()
        feed_gather.exchange()
        attention_pieces, attention_places = gather.result(), gather.places()
        feed_places = feed_gather.places()
    else:
        def canonical(parts, width):
            grouped = []
            for part in parts:
                whole = lax.all_gather(part, "dp", axis=0, tiled=True)
                whole = lax.all_gather(whole, "tensor", axis=1, tiled=True)
                grouped.append(whole.reshape(D, GROUPS, width).swapaxes(0, 1))
            return [jnp.concatenate(grouped, axis=2)]

        attention_pieces = canonical((query_w, key_w, value_w, out_w.T), EG)
        feed_pieces = canonical((inner_w, outer_w.T), FG)
        attention_places = feed_places = jnp.array([[0, 1], [0, 0]], jnp.int32)
        context = lax.all_to_all(context, "tensor", split_axis=1, concat_axis=3, tiled=True)
        inner_b_full = lax.all_gather(inner_b, "tensor", axis=0, tiled=True).reshape(1, FF)
    context = jnp.pad(context, ((0, 0), (0, 0), (TOP - LEFT, 0), (0, 0)))

    core_bit = my_bit("core") if tuned else 0
    first_row = jnp.zeros_like(time_start).at[0].set(base).at[1].set(core_bit)
    meta = jnp.stack(
        [first_row, time_start, time_width, freq_start, freq_width, context_count]
    ).astype(jnp.int32)
    norm = jnp.stack(
        [gain_one, shift_one, gain_two, shift_two, outer_b] + [jnp.zeros_like(gain_one)] * 3
    )

    chunk = min(CHUNK, spans)
    firsts = range(0, spans, chunk)
    final = spans - chunk

    def exchange(value):
        return swap(value, "x") if tuned else value

    if tuned:
        meta = tie(meta, inner_b_full, attention_places, feed_places, feed_gather.got)
        feed_gather.exchange()
    n1, q, k, v, att, mid, weights = attention_forward(
        meta, attention_places, frames, context[0], context[1], norm, attention_pieces, [], 0, spans
    )
    if tuned:
        feed_gather.after(n1)
        feed_gather.exchange()
        feed_pieces = feed_gather.result()
    outs, gms, before, feed_weights = [], [], [], None
    parts = len(FEED_SUMS) if tuned else 1
    for first in firsts:
        pieces = feed_pieces if feed_weights is None else [feed_weights]
        output, part, gm, rest = feed_forward(
            meta, feed_places, mid, cotangent, att, norm, inner_b_full, pieces, before,
            first, chunk, first == final, parts,
        )
        if first == 0 and first != final:
            *rest, feed_weights = rest
        outs.append(exchange(part))
        gms.append(gm)
        before = [output, *rest]
    feed_grad = rest
    frame_parts, contexts, before = [], [], []
    parts = len(ATTENTION_SUMS) if tuned else 1
    if tuned:
        feed_grad = list(tie(tuple(feed_grad), outs[0]))
        feed_scatter = Scatter(feed_grad, FEED_SUMS)
        feed_scatter.exchange()
    for index, (first, gm) in enumerate(zip(firsts, gms)):
        own_meta = meta
        if tuned:
            own_meta = tie(meta, *feed_scatter.kept(), *(outs[-1:] if index > 0 else []))
        cuts = (3 * D // 4, D // 4) if tuned and first == final else (D,)
        grad_frames, pieces, gctx, rest = attention_backward(
            own_meta, attention_places, frames, (n1, q, k, v), gm, norm, weights, before, first, chunk,
            first == final, parts, cuts,
        )
        frame_parts.append([exchange(piece) for piece in pieces])
        contexts.append(gctx)
        before = [grad_frames, *rest]
        if tuned and index == 0:
            feed_scatter.after(grad_frames)
            feed_scatter.exchange()
    attention_grad = rest
    if tuned:
        attention_grad = list(tie(tuple(attention_grad), frame_parts[:-1], feed_scatter.terms))
        attention_scatter = Scatter(attention_grad, ATTENTION_SUMS)
        output, grad_frames = tie((output, grad_frames), attention_scatter.terms)
        feed_scatter.exchange()
        attention_scatter.after(*feed_scatter.kept())
        attention_scatter.exchange()
        feed_scatter.after(attention_scatter.terms)
        attention_scatter.after(frame_parts[-1][0])
        attention_scatter.exchange()
        (feed_sum,) = finish_sums([feed_scatter])
        contexts = tie(contexts, attention_scatter.kept())
        gctx = jnp.concatenate(contexts, axis=2)[:, :, :, TOP - LEFT :]
        mine, theirs = (
            lax.dynamic_index_in_dim(gctx, place, 0, keepdims=False)
            for place in (t_index, 1 - t_index)
        )
        theirs = swap(theirs, "x")
        attention_scatter.terms, frame_parts[-1], theirs = tie(
            (attention_scatter.terms, frame_parts[-1], theirs)
        )

    if tuned:
        def both(whole, parts):
            for first, pieces in zip(firsts, parts):
                place, column = ((1 - t_index) * spans + first) * SPAN, 0
                for piece in pieces:
                    whole = lax.dynamic_update_slice(whole, piece, (place, column))
                    column += piece.shape[1]
            return whole

        output = both(output, [[part] for part in outs])
        grad_frames = both(grad_frames, frame_parts)
        (attention_sum,) = finish_sums([attention_scatter])
        grad_context = pick(
            jnp.concatenate([mine, theirs], axis=1), jnp.concatenate([theirs, mine], axis=1)
        )
        extra = feed_sum[:4, FEED_WIDTH - EXTRA :]
        sum_gain_two, sum_shift_two, sum_outer_b = (extra[i, :32] for i in range(3))
        sum_inner_b = extra[3, :64]
        sum_gain_one, sum_shift_one = (
            attention_sum[i, 3 * EG : 3 * EG + 32] for i in range(2)
        )
        sum_query, sum_key, sum_value = (
            attention_sum[:, i * EG : (i + 1) * EG] for i in range(3)
        )
        sum_inner, sum_outer = feed_sum[:, :FG], feed_sum[:, FG : 2 * FG]
        sum_out = feed_sum[:, 2 * FG : 2 * FG + EG]
    else:
        def both(parts):
            return lax.all_gather(jnp.concatenate(parts, axis=0), "tensor", axis=0, tiled=True)

        output = both(outs)
        grad_frames = both([piece for (piece,) in frame_parts])
        gctx = jnp.concatenate(contexts, axis=2)[:, :, :, TOP - LEFT :]
        grad_context = jnp.moveaxis(gctx, 0, 3).reshape(2, spans, LEFT, D)
        grad_context = lax.all_to_all(
            grad_context, "tensor", split_axis=3, concat_axis=1, tiled=True
        )
        attention_grad, feed_grad = (
            jnp.stack(pair, axis=2).reshape(GROUPS, D, -1) for pair in (attention_grad, feed_grad)
        )

        def whole_grad(grad, index, width):
            return grad[:, :, index * width : (index + 1) * width].swapaxes(0, 1).reshape(D, -1)

        def scattered(grad):
            part = lax.psum_scatter(grad, "dp", scatter_dimension=0, tiled=True)
            return lax.psum_scatter(part, "tensor", scatter_dimension=1, tiled=True).astype(F32)

        def summed(item):
            item = lax.psum(item, "tensor")
            return lax.psum_scatter(item, "dp", scatter_dimension=0, tiled=True)

        def vector(grad, index):
            item = grad[0, :, -EXTRA:].reshape(16, 32, EXTRA)[:, index, :32].reshape(D)
            return summed(item.astype(F32))

        sum_query, sum_key, sum_value = (
            scattered(whole_grad(attention_grad, i, EG)) for i in range(3)
        )
        sum_inner, sum_outer = (scattered(whole_grad(feed_grad, i, FG)) for i in range(2))
        sum_out = scattered(feed_grad[:, :, 2 * FG : 2 * FG + EG].swapaxes(0, 1).reshape(D, -1))
        sum_gain_one, sum_shift_one = (vector(attention_grad, i) for i in range(2))
        sum_gain_two, sum_shift_two, sum_outer_b = (vector(feed_grad, i) for i in range(3))
        sum_inner_b = feed_grad[:, :, -EXTRA:].reshape(GROUPS, 16, 32, EXTRA)[:, :, 3, :64]
        sum_inner_b = sum_inner_b.reshape(FF).astype(F32)
        sum_inner_b = lax.psum_scatter(sum_inner_b, "tensor", scatter_dimension=0, tiled=True)
        sum_inner_b = lax.psum_scatter(sum_inner_b, "dp", scatter_dimension=0, tiled=True)

    return (
        output,
        grad_frames,
        grad_context[0],
        grad_context[1],
        sum_gain_one,
        sum_shift_one,
        sum_query,
        sum_key,
        sum_value,
        sum_out.T,
        sum_gain_two,
        sum_shift_two,
        sum_inner,
        sum_inner_b,
        sum_outer.T,
        sum_outer_b,
    )


def solution(mesh):
    in_specs = (
        P("dp", None),
        P("dp", None, "tensor"),
        P("dp", None, "tensor"),
        P("dp"),
        P("dp"),
        P("dp"),
        P("dp"),
        P("dp"),
        P(),
        P(),
        P("dp", "tensor"),
        P("dp", "tensor"),
        P("dp", "tensor"),
        P("tensor", "dp"),
        P(),
        P(),
        P("dp", "tensor"),
        P("tensor"),
        P("tensor", "dp"),
        P(),
        P("dp", None),
    )
    out_specs = (
        P("dp", None),
        P("dp", None),
        P("dp", None, "tensor"),
        P("dp", None, "tensor"),
        P("dp"),
        P("dp"),
        P("dp", "tensor"),
        P("dp", "tensor"),
        P("dp", "tensor"),
        P("tensor", "dp"),
        P("dp"),
        P("dp"),
        P("dp", "tensor"),
        P(("tensor", "dp")),
        P("tensor", "dp"),
        P("dp"),
    )
    return jax.shard_map(body, mesh=mesh, in_specs=in_specs, out_specs=out_specs, check_vma=False)
```
